512 devices in a mesh: slab: 8 (over y_hi, x), walker: 16 (over z), geom: 4 (over y_lo, core).
Axes of the slice: x: 4, y: 4 (y_hi: 2, y_lo: 2; y = y_hi * 2 + y_lo), z: 16, core: 2. Of those that a mesh axis runs over, the one named last changes fastest.
Arguments:
- features: bfloat16 [4, 32, 1024, 256], P('geom', 'walker', 'slab'), may hold values from -6 to 6
- w_self: bfloat16 [256, 256], replicated, may hold values from -0.375 to 0.375
- w_pair: bfloat16 [256, 256], replicated, may hold values from -0.375 to 0.375
- w_update: bfloat16 [256, 256], replicated, may hold values from -0.375 to 0.375
- geo_embed: float32 [4, 2, 256], P('geom'), may hold values from -6 to 6
- lattice: int32 [4, 32], P('geom', 'walker'), may hold values from 0 to 1
- neighbours: int32 [4, 32, 1024, 64], P('geom', 'walker', 'slab'), may hold values from 0 to 191, as said below
- counts: int32 [4, 32, 1024], P('geom', 'walker', 'slab'), may hold values from 1 to 64
- envelope: bfloat16 [4, 32, 1024, 64], P('geom', 'walker', 'slab'), may hold values from 0.099609375 to 1
- cotangent: bfloat16 [4, 32, 1024, 256], P('geom', 'walker', 'slab'), may hold values from -6 to 6
Outputs:
- new_features: bfloat16 [4, 32, 1024, 256], P('geom', 'walker', 'slab')
- d_features: float32 [4, 32, 1024, 256], P('geom', 'walker', 'slab')
- d_w_self: float32 [256, 256], P('walker')
- d_w_pair: float32 [256, 256], P('walker')
- d_w_update: float32 [256, 256], P('walker')
- d_geo: float32 [4, 2, 256], P('geom')
The draws below stay inside these ranges and needn't reach their ends.
Inputs may be any that keep to these rules, and one draw needn't show every extreme that they name: `neighbours`: for an electron at position l within its slab, every entry lies within l to l + 64 and differs from l + 32.
All inputs are finite; a program needn't handle non-finite values.
Results may differ from the reference program's by a relative error of at most 0.0055.
Values may be sent and summed in bfloat16 or wider, within the bound.
A program may use at most 64 MiB of HBM per device.

```python
import math
import jax
import jax.numpy as jnp
from jax import lax

WIDTH = 256
NBRS = 64
RIM = 32
LATS = 2
E_DEV = 128
ELECTRONS = 1024
WALK = 32
GROUPS = 4


def draw_neighbours(key, part):
    key = jax.random.fold_in(key, 11)
    offset = jax.random.randint(key, (GROUPS, WALK, ELECTRONS, NBRS), 0, 2 * RIM)
    offset = offset - RIM + (offset >= RIM).astype(jnp.int32)
    local = (jnp.arange(ELECTRONS) % E_DEV).astype(jnp.int32)
    first = offset[..., 0]
    first = jnp.where(local[None, None, :] == 0, -RIM, jnp.where(local[None, None, :] == E_DEV - 1, RIM, first))
    offset = offset.at[..., 0].set(first)
    return (RIM + local[None, None, :, None] + offset).astype(jnp.int32)


def touch_ends(entries, stream_key, least, high):
    spot = [jax.random.randint(jax.random.fold_in(stream_key, axis), (), 0, length) for axis, length in enumerate(entries.shape)]
    widest = entries.shape.index(max(entries.shape))
    beside = spot[:widest] + [(spot[widest] + 1) % entries.shape[widest]] + spot[widest + 1:]
    return entries.at[tuple(spot)].set(least).at[tuple(beside)].set(high)


def block_levels(key, shape, split, least, top_value):
    factor_of, own = 1.0, jax.random.fold_in(key, 6)
    for axis_at, shards_of in split:
        heights = jnp.exp(jax.random.uniform(jax.random.fold_in(own, axis_at), (shards_of,), jnp.float32, least / len(split), top_value / len(split)))
        factor_of = factor_of * jnp.repeat(heights, shape[axis_at] // shards_of).reshape([-1 if axis == axis_at else 1 for axis in range(len(shape))])
    return factor_of


def scatter_about(own_key, dims, spread, limit, pieces=(), kind=jnp.bfloat16):
    values = jax.random.normal(own_key, dims, jnp.float32) * spread
    if len(pieces) > 0:
        values = block_levels(own_key, dims, pieces, -0.22, 0.18) * values
    return jnp.clip(values, min=-limit, max=limit).astype(kind)


def setup_inputs(seed: int = 0) -> dict:
    key_of = jax.random.split(jax.random.key(seed), 11)
    return {
        "features": scatter_about(key_of[0], (GROUPS, WALK, ELECTRONS, WIDTH), 1.0, 6.0, ((0, 4), (1, 16), (2, 8))),
        "w_self": scatter_about(key_of[1], (WIDTH, WIDTH), WIDTH ** -0.5, 0.375),
        "w_pair": scatter_about(key_of[2], (WIDTH, WIDTH), WIDTH ** -0.5, 0.375),
        "w_update": scatter_about(key_of[3], (WIDTH, WIDTH), WIDTH ** -0.5, 0.375),
        "geo_embed": scatter_about(key_of[4], (GROUPS, LATS, WIDTH), 1.0, 6.0, ((0, 4),), jnp.float32),
        "lattice": touch_ends(jax.random.randint(key_of[5], (GROUPS, WALK), 0, LATS), jax.random.fold_in(key_of[5], 1), 0, LATS - 1).astype(jnp.int32),
        "neighbours": draw_neighbours(jax.random.fold_in(key_of[10], 71), 0),
        "counts": touch_ends(jax.random.randint(key_of[7], (GROUPS, WALK, ELECTRONS), 1, NBRS + 1), jax.random.fold_in(key_of[7], 1), 1, NBRS).astype(jnp.int32),
        "envelope": jnp.clip(jnp.exp(math.log(1.0) - 2.306499 * jax.random.uniform(key_of[8], (GROUPS, WALK, ELECTRONS, NBRS), jnp.float32) ** block_levels(key_of[8], (GROUPS, WALK, ELECTRONS, NBRS), ((0, 4), (1, 16), (2, 8)), -0.2, 0.2)), 0.099609375, 1.0).astype(jnp.bfloat16),
        "cotangent": scatter_about(key_of[9], (GROUPS, WALK, ELECTRONS, WIDTH), 1.0, 6.0, ((0, 4), (1, 16), (2, 8))),
    }


def silu_grad(value):
    sig = jax.nn.sigmoid(value)
    return sig * (1.0 + value * (1.0 - sig))

def one_walker(feats, q_all, p_rows, nbr_index, count, env, dout, w_update):
    gathered = q_all[nbr_index]
    pre = p_rows[:, None, :] + gathered.astype(jnp.float32)
    valid = (jnp.arange(NBRS)[None, :] < count[:, None]).astype(jnp.float32)
    weight = env.astype(jnp.float32) * valid
    denom = count[:, None].astype(jnp.float32)
    agg = (lax.optimization_barrier(jnp.sum(jax.nn.silu(pre) * weight[:, :, None], axis=1)) / denom).astype(jnp.bfloat16)
    upd = jnp.dot(agg, w_update, preferred_element_type=jnp.float32)
    new_rows = (feats.astype(jnp.float32) + jax.nn.silu(upd)).astype(jnp.bfloat16)
    d_upd = (dout.astype(jnp.float32) * silu_grad(upd)).astype(jnp.bfloat16)
    d_agg = jnp.dot(d_upd, w_update.T, preferred_element_type=jnp.float32)
    d_pre = (d_agg / denom)[:, None, :] * weight[:, :, None] * silu_grad(pre)
    d_self = lax.optimization_barrier(jnp.sum(d_pre, axis=1))
    return (new_rows, agg, d_upd, d_self, d_pre)

def reference(features, w_self, w_pair, w_update, geo_embed, lattice, neighbours, counts, envelope, cotangent):
    total = GROUPS * WALK
    feats_all = features.reshape(total, ELECTRONS, WIDTH)
    nbr_all = neighbours.reshape(total, ELECTRONS, NBRS)
    cnt_all = counts.reshape(total, ELECTRONS)
    env_all = envelope.reshape(total, ELECTRONS, NBRS)
    dout_all = cotangent.reshape(total, ELECTRONS, WIDTH)
    group_of = (jnp.arange(total) // WALK).astype(jnp.int32)
    table_index = (group_of * LATS + lattice.reshape(total)).astype(jnp.int32)
    geo_flat = geo_embed.reshape(GROUPS * LATS, WIDTH)
    electron = jnp.arange(ELECTRONS).astype(jnp.int32)
    start = electron // E_DEV * E_DEV

    def step(carry, inputs):
        grad_self, grad_pair, grad_update, grad_geo = carry
        feats, nbr, cnt, env, dout, tidx = inputs
        global_index = ((start[:, None] - RIM + nbr) % ELECTRONS).astype(jnp.int32)
        q_all = jnp.dot(feats, w_pair, preferred_element_type=jnp.float32).astype(jnp.bfloat16)
        p_rows = jnp.dot(feats, w_self, preferred_element_type=jnp.float32) + geo_flat[tidx][None, :]
        new_rows, agg, d_upd, d_self, d_pre = one_walker(feats, q_all, p_rows, global_index, cnt, env, dout, w_update)
        d_pair = jax.ops.segment_sum(d_pre.reshape(ELECTRONS * NBRS, WIDTH), global_index.reshape(-1), num_segments=ELECTRONS)
        dp_b = d_self.astype(jnp.bfloat16)
        dq_b = d_pair.astype(jnp.bfloat16)
        d_feats = dout.astype(jnp.float32) + jnp.dot(dp_b, w_self.T, preferred_element_type=jnp.float32) + jnp.dot(dq_b, w_pair.T, preferred_element_type=jnp.float32)
        grad_self = grad_self + jnp.dot(feats.T, dp_b, preferred_element_type=jnp.float32)
        grad_pair = grad_pair + jnp.dot(feats.T, dq_b, preferred_element_type=jnp.float32)
        grad_update = grad_update + jnp.dot(agg.T, d_upd, preferred_element_type=jnp.float32)
        select = (jnp.arange(GROUPS * LATS) == tidx).astype(jnp.float32)
        grad_geo = grad_geo + select[:, None] * lax.optimization_barrier(jnp.sum(d_self, axis=0))[None, :]
        return ((grad_self, grad_pair, grad_update, grad_geo), (new_rows, d_feats))
    zeros = jnp.zeros((WIDTH, WIDTH), jnp.float32)
    init = (zeros, zeros, zeros, jnp.zeros((GROUPS * LATS, WIDTH), jnp.float32))
    carry, outs = lax.scan(step, init, (feats_all, nbr_all, cnt_all, env_all, dout_all, table_index))
    new_rows, d_feats = outs
    return (new_rows.reshape(GROUPS, WALK, ELECTRONS, WIDTH), d_feats.reshape(GROUPS, WALK, ELECTRONS, WIDTH), carry[0], carry[1], carry[2], carry[3].reshape(GROUPS, LATS, WIDTH))
```

```python
import functools

import jax
import jax.numpy as jnp
from jax import lax
from jax.experimental import pallas as pl
from jax.experimental.pallas import tpu as pltpu
from jax.sharding import PartitionSpec as P

RIM = 32
F32 = jnp.float32
BF16 = jnp.bfloat16
MESH = pl.DeviceIdType.MESH
BASES = (0, 8, 16, 24, 33, 41, 49, 57)
STEPS = 8


def dot(a, b, dims, **more):
    return lax.dot_general(a, b, (dims, ((), ())), preferred_element_type=F32, **more)


NN = ((1,), (0,))
NT = ((1,), (1,))
TN = ((0,), (0,))


def at(**coords):
    return dict(device_id=coords, device_id_type=MESH)


def halo_kernel(slabs, feats_ref, before_ref, after_ref, send_sem, recv_sem):
    me = lax.axis_index("slab")
    nxt, prv = lax.rem(me + 1, slabs), lax.rem(me + slabs - 1, slabs)
    barrier = pltpu.get_barrier_semaphore()
    pl.semaphore_signal(barrier, inc=1, **at(slab=nxt))
    pl.semaphore_signal(barrier, inc=1, **at(slab=prv))
    pl.semaphore_wait(barrier, 2)
    rows = feats_ref.shape[1]
    up = pltpu.make_async_remote_copy(
        feats_ref.at[:, pl.ds(rows - RIM, RIM)], before_ref, send_sem.at[0], recv_sem.at[0], **at(slab=nxt)
    )
    down = pltpu.make_async_remote_copy(
        feats_ref.at[:, pl.ds(0, RIM)], after_ref, send_sem.at[1], recv_sem.at[1], **at(slab=prv)
    )
    up.start()
    down.start()
    up.wait()
    down.wait()


def compute_kernel(
    lat_ref, feats_ref, before_ref, after_ref, ws_ref, wp_ref, wu_ref, geo_ref, nbr_ref, cnt_ref, env_ref, cot_ref,
    newf_ref, dp_ref, dq_ref, low_ref, high_ref, grads_ref, dgeo_ref,
    ext_ref, p_ref, q_ref, off_ref, wt_ref, w_ref, agg_ref, s_ref, d_ref, dqt_ref, t_ref,
):
    walkers, rows, width = feats_ref.shape
    slots = nbr_ref.shape[2]
    wide = q_ref.shape[1]
    lats = geo_ref.shape[0]
    lane = lax.broadcasted_iota(jnp.int32, (8, rows), 1)
    ws_t = ws_ref[...].T
    wp_t = wp_ref[...].T
    ext_ref[pl.ds(rows + 2 * RIM, wide - rows - 2 * RIM), :] = jnp.zeros((wide - rows - 2 * RIM, width), BF16)
    dgeo = jnp.zeros((lats, width), F32)
    for w in range(walkers):
        ext_ref[pl.ds(0, RIM), :] = before_ref[w]
        ext_ref[pl.ds(RIM, rows), :] = feats_ref[w]
        ext_ref[pl.ds(RIM + rows, RIM), :] = after_ref[w]
        ext_t = ext_ref[...].T
        feats_t = feats_ref[w].T
        lat = lat_ref[0, w]
        pick = (lax.broadcasted_iota(jnp.int32, (lats, rows), 0) == lat).astype(F32)
        p_t = dot(ws_t, feats_t, NN) + dot(geo_ref[...], pick, TN, precision=lax.Precision.HIGHEST)
        p_ref[...] = 0.5 * p_t
        q_ref[...] = 0.5 * dot(wp_t, ext_t, NN).astype(BF16).astype(F32)

        own = lax.broadcasted_iota(jnp.int32, (rows, slots), 0)
        rel = nbr_ref[w] - own
        rel = rel - (rel > RIM).astype(jnp.int32)
        off_ref[...] = rel.astype(F32).T.astype(jnp.int32)
        count = cnt_ref[pl.ds(w, 1), :]
        slot = lax.broadcasted_iota(jnp.int32, (slots, rows), 0)
        wt_ref[...] = jnp.where(slot < count, env_ref[w].astype(F32).T, 0.0)

        def place(step, acc):
            for u in range(8):
                k = step * 8 + u
                acc = acc + jnp.where(off_ref[pl.ds(k, 1), :] == slot, wt_ref[pl.ds(k, 1), :], 0.0)
            return acc

        weights = lax.fori_loop(0, slots // 8, place, jnp.zeros((slots, rows), F32))
        rolled = weights
        sub = lax.rem(slot, STEPS)
        for a in range(1, STEPS):
            rolled = jnp.where(sub == a, pltpu.roll(weights, a, 1), rolled)
        w_ref[...] = rolled

        def forward(tile, carry):
            r0 = pl.multiple_of(tile * 8, 8)
            p = p_ref[pl.ds(r0, 8), :]
            q = q_ref[pl.ds(r0, 8), :]
            qs = []
            for base in BASES:
                moved = q if base == 0 else pltpu.roll(q, wide - base, 1)
                qs.append((moved[:, :rows], moved[:, rows:]))
            agg = jnp.zeros((8, rows), F32)
            tot = jnp.zeros((8, rows), F32)
            for a in range(STEPS):
                pa = p if a == 0 else pltpu.roll(p, a, 1)
                ga = sa = None
                for b in range(len(BASES)):
                    m = b * STEPS + a
                    q0, q1 = qs[b]
                    h = pa + (q0 if a == 0 else jnp.where(lane < a, q1, q0))
                    u = 1.0 + jnp.tanh(h)
                    g = h * u
                    wm = w_ref[pl.ds(m, 1), :]
                    t = wm * (u + g * (2.0 - u))
                    t_ref[m, pl.ds(r0, 8), :] = t
                    ga = wm * g if ga is None else ga + wm * g
                    sa = t if sa is None else sa + t
                if a:
                    ga = pltpu.roll(ga, rows - a, 1)
                    sa = pltpu.roll(sa, rows - a, 1)
                agg = agg + ga
                tot = tot + sa
            agg_ref[pl.ds(r0, 8), :] = agg
            s_ref[pl.ds(r0, 8), :] = tot
            return carry

        lax.fori_loop(0, width // 8, forward, 0)

        inv = 1.0 / count.astype(F32)
        agg_t = (agg_ref[...] * inv).astype(BF16)
        upd = dot(agg_t.T, wu_ref[...], NN)
        sig = 0.5 + 0.5 * jnp.tanh(0.5 * upd)
        newf_ref[w] = (feats_ref[w].astype(F32) + upd * sig).astype(BF16)
        du = (cot_ref[w].astype(F32) * (sig * (1.0 + upd * (1.0 - sig)))).astype(BF16)
        dd = 0.5 * dot(wu_ref[...], du, NT) * inv
        d_ref[...] = dd
        dp = (dd * s_ref[...]).T
        dgeo = dgeo + jnp.where(
            lax.broadcasted_iota(jnp.int32, (lats, width), 0) == lat, jnp.sum(dp, axis=0, keepdims=True), 0.0
        )
        dp = dp.astype(BF16)
        dp_ref[w] = dp

        def backward(tile, carry):
            r0 = pl.multiple_of(tile * 8, 8)
            d = d_ref[pl.ds(r0, 8), :]
            nb = len(BASES)
            alls, wraps = [None] * nb, [None] * nb
            for a in range(STEPS):
                da = d if a == 0 else pltpu.roll(d, a, 1)
                for b in range(nb):
                    v = t_ref[b * STEPS + a, pl.ds(r0, 8), :] * da
                    alls[b] = v if a == 0 else alls[b] + v
                    if a:
                        c = jnp.where(lane < a, v, 0.0)
                        wraps[b] = c if a == 1 else wraps[b] + c
            out = jnp.zeros((8, wide), F32)
            for b, base in enumerate(BASES):
                both = jnp.concatenate((alls[b] - wraps[b], wraps[b]), axis=1)
                out = out + (both if base == 0 else pltpu.roll(both, base, 1))
            dqt_ref[pl.ds(r0, 8), :] = out
            return carry

        lax.fori_loop(0, width // 8, backward, 0)
        dq = dqt_ref[...].T
        dq_ref[w] = dq[RIM : RIM + rows]
        dqb = dq.astype(BF16)
        low_ref[w] = dqb[:RIM]
        high_ref[w] = dqb[RIM + rows : 2 * RIM + rows]
        terms = (dot(feats_t, dp, NN), dot(ext_t, dqb, NN), dot(agg_t, du, NN))
        for n in range(3):
            grads_ref[n] = terms[n] if w == 0 else grads_ref[n] + terms[n]
    dgeo_ref[...] = dgeo


def reduce_kernel(
    slabs, walks, geoms,
    grads_ref, low_ref, high_ref, dgeo_ref,
    out_ref, from_next_ref, from_prev_ref, geo_out_ref,
    core_out, core_in, half, plane_out, plane_in, ring_out, ring_in, gather_out, gather_in, gslab_in, gring_out, gring_in,
    send_sem, recv_sem,
):
    slab, z, geom = lax.axis_index("slab"), lax.axis_index("walker"), lax.axis_index("geom")
    core = lax.rem(geom, 2)
    pair = geom - core
    chips = slabs * geoms // 2
    chip = slab * (geoms // 2) + pair // 2
    nmat, rows, width = grads_ref.shape
    lanes = width // 2
    nxt, prv = lax.rem(slab + 1, slabs), lax.rem(slab + slabs - 1, slabs)

    def chip_at(c, k):
        return at(slab=c // (geoms // 2), geom=lax.rem(c, geoms // 2) * 2 + k)

    barrier = pltpu.get_barrier_semaphore()
    for k in range(2):
        kk = core if k == 0 else 1 - core
        for r in range(k ^ 1, chips):
            pl.semaphore_signal(barrier, inc=1, **chip_at(lax.rem(chip + r, chips), kk))
    for r in range(1, walks):
        pl.semaphore_signal(barrier, inc=1, **at(walker=lax.rem(z + r, walks)))
    pl.semaphore_wait(barrier, 2 * chips - 1 + walks - 1)

    def send(src, dst, n, where):
        c = pltpu.make_async_remote_copy(src, dst, send_sem.at[n], recv_sem.at[n], **where)
        c.start()
        return c

    def settle(ref, n):
        c = pltpu.make_async_remote_copy(ref, ref, send_sem.at[n], recv_sem.at[n], **at(slab=nxt))
        c.wait_send()
        c.wait_recv()

    down = send(low_ref, from_next_ref, 0, at(slab=prv))
    up = send(high_ref, from_prev_ref, 1, at(slab=nxt))

    mine = pl.ds(pl.multiple_of(core * lanes, lanes), lanes)
    theirs = pl.ds(pl.multiple_of((1 - core) * lanes, lanes), lanes)
    core_out[...] = grads_ref[:, :, theirs].astype(BF16)
    cross = send(core_out, core_in, 2, at(geom=pair + 1 - core))

    gslab_in[slab] = dgeo_ref[...]
    for r in range(1, slabs):
        send(dgeo_ref, gslab_in.at[slab], 3, at(slab=lax.rem(slab + r, slabs)))

    cross.wait()
    half[...] = grads_ref[:, :, mine] + core_in[...].astype(F32)

    for c in range(chips):
        for n in range(nmat):
            plane_out[c, n] = half[n, pl.ds(c, walks, stride=chips), :].astype(BF16)
    plane_in[chip] = plane_out[chip]
    for r in range(1, chips):
        to = lax.rem(chip + r, chips)
        send(plane_out.at[to], plane_in.at[chip], 4, chip_at(to, core))

    settle(gslab_in.at[pl.ds(0, slabs - 1)], 3)
    gsum = gslab_in[0]
    for s in range(1, slabs):
        gsum = gsum + gslab_in[s]
    gring_out[...] = gsum
    gring_in[z] = gsum
    for r in range(1, walks):
        send(gring_out, gring_in.at[z], 5, at(walker=lax.rem(z + r, walks)))

    settle(plane_in.at[pl.ds(0, chips - 1)], 4)
    part = plane_in[0].astype(F32)
    for c in range(1, chips):
        part = part + plane_in[c].astype(F32)

    ring_out[...] = jnp.zeros(ring_out.shape, F32)
    for n in range(nmat):
        for v in range(walks):
            ring_out[v, pl.ds(n, 1), :] = part[n, v : v + 1, :]
    ring_in[z] = ring_out[z]
    for r in range(1, walks):
        to = lax.rem(z + r, walks)
        send(ring_out.at[to], ring_in.at[z], 6, at(walker=to))
    settle(ring_in.at[pl.ds(0, walks - 1)], 6)
    row = ring_in[0]
    for v in range(1, walks):
        row = row + ring_in[v]

    slot = core * chips + chip
    gather_out[...] = row
    gather_in[slot] = row
    for k in range(2):
        kk = core if k == 0 else 1 - core
        for r in range(k ^ 1, chips):
            send(gather_out, gather_in.at[slot], 7, chip_at(lax.rem(chip + r, chips), kk))

    settle(gring_in.at[pl.ds(0, walks - 1)], 5)
    gsum = gring_in[0]
    for v in range(1, walks):
        gsum = gsum + gring_in[v]
    geo_out_ref[...] = gsum

    settle(gather_in.at[pl.ds(0, 2 * chips - 1)], 7)
    for n in range(nmat):
        for k in range(2):
            for c in range(chips):
                out_ref[n, pl.ds(c, 1), pl.ds(k * lanes, lanes)] = gather_in[k * chips + c, pl.ds(n, 1), :]
    down.wait()
    up.wait()


def finish_kernel(cot_ref, dp_ref, dq_ref, from_next_ref, from_prev_ref, ws_ref, wp_ref, grads_ref, geo_ref,
                  df_ref, gs_ref, gp_ref, gu_ref, geo_out_ref):
    walkers, rows, width = dq_ref.shape
    for w in range(walkers):
        dq = jnp.concatenate(
            (
                dq_ref[w, pl.ds(0, RIM), :] + from_prev_ref[w].astype(F32),
                dq_ref[w, pl.ds(RIM, rows - 2 * RIM), :],
                dq_ref[w, pl.ds(rows - RIM, RIM), :] + from_next_ref[w].astype(F32),
            ),
            axis=0,
        ).astype(BF16)
        df_ref[w] = cot_ref[w].astype(F32) + dot(dp_ref[w], ws_ref[...], NT) + dot(dq, wp_ref[...], NT)
    gs_ref[...] = grads_ref[0]
    gp_ref[...] = grads_ref[1]
    gu_ref[...] = grads_ref[2]
    geo_out_ref[...] = geo_ref[...]


def vmem(n):
    return [pl.BlockSpec(memory_space=pltpu.VMEM)] * n


def body(sizes, features, w_self, w_pair, w_update, geo_embed, lattice, neighbours, counts, envelope, cotangent):
    slabs, walks, geoms = sizes
    feats, cot = features[0], cotangent[0]
    walkers, rows, width = feats.shape
    slots = neighbours.shape[3]
    lats = geo_embed.shape[1]
    wide = 2 * rows
    sds = jax.ShapeDtypeStruct
    rim = sds((walkers, RIM, width), BF16)
    before, after = pl.pallas_call(
        functools.partial(halo_kernel, slabs),
        out_shape=(rim, rim),
        in_specs=vmem(1),
        out_specs=vmem(2),
        scratch_shapes=[pltpu.SemaphoreType.DMA((2,)), pltpu.SemaphoreType.DMA((2,))],
        compiler_params=pltpu.CompilerParams(collective_id=0, has_side_effects=True),
        name="halo",
    )(feats)

    newf, dp, dq, low, high, grads, dgeo = pl.pallas_call(
        compute_kernel,
        out_shape=(
            sds((walkers, rows, width), BF16),
            sds((walkers, rows, width), BF16),
            sds((walkers, rows, width), F32),
            rim,
            rim,
            sds((3, width, width), F32),
            sds((lats, width), F32),
        ),
        in_specs=[pl.BlockSpec(memory_space=pltpu.SMEM)] + vmem(11),
        out_specs=vmem(7),
        scratch_shapes=[
            pltpu.VMEM((wide, width), BF16),
            pltpu.VMEM((width, rows), F32),
            pltpu.VMEM((width, wide), F32),
            pltpu.VMEM((slots, rows), jnp.int32),
            pltpu.VMEM((slots, rows), F32),
            pltpu.VMEM((slots, rows), F32),
            pltpu.VMEM((width, rows), F32),
            pltpu.VMEM((width, rows), F32),
            pltpu.VMEM((width, rows), F32),
            pltpu.VMEM((width, wide), F32),
            pltpu.VMEM((slots, width, rows), F32),
        ],
        compiler_params=pltpu.CompilerParams(vmem_limit_bytes=40 * 1024 * 1024),
        name="compute",
    )(lattice, feats, before, after, w_self, w_pair, w_update, geo_embed[0], neighbours[0], counts[0], envelope[0], cot)

    chips = slabs * geoms // 2
    lanes = width // 2
    gsum, from_next, from_prev, geo = pl.pallas_call(
        functools.partial(reduce_kernel, slabs, walks, geoms),
        out_shape=(sds((3, width // walks, width), F32), rim, rim, sds((lats, width), F32)),
        in_specs=vmem(4),
        out_specs=vmem(4),
        scratch_shapes=[
            pltpu.VMEM((3, width, lanes), BF16),
            pltpu.VMEM((3, width, lanes), BF16),
            pltpu.VMEM((3, width, lanes), F32),
            pltpu.VMEM((chips, 3, walks, lanes), BF16),
            pltpu.VMEM((chips, 3, walks, lanes), BF16),
            pltpu.VMEM((walks, 8, lanes), F32),
            pltpu.VMEM((walks, 8, lanes), F32),
            pltpu.VMEM((8, lanes), F32),
            pltpu.VMEM((2 * chips, 8, lanes), F32),
            pltpu.VMEM((slabs, lats, width), F32),
            pltpu.VMEM((lats, width), F32),
            pltpu.VMEM((walks, lats, width), F32),
            pltpu.SemaphoreType.DMA((8,)),
            pltpu.SemaphoreType.DMA((8,)),
        ],
        compiler_params=pltpu.CompilerParams(
            collective_id=1, has_side_effects=True, vmem_limit_bytes=16 * 1024 * 1024
        ),
        name="reduce",
    )(grads, low, high, dgeo)

    share = sds((width // walks, width), F32)
    dfeats, gs, gp, gu, dgeo_all = pl.pallas_call(
        finish_kernel,
        out_shape=(sds((walkers, rows, width), F32), share, share, share, sds((lats, width), F32)),
        in_specs=vmem(9),
        out_specs=vmem(5),
        name="finish",
    )(cot, dp, dq, from_next, from_prev, w_self, w_pair, gsum, geo)
    return newf[None], dfeats[None], gs, gp, gu, dgeo_all[None]


def solution(mesh):
    sizes = (mesh.shape["slab"], mesh.shape["walker"], mesh.shape["geom"])
    return jax.shard_map(
        functools.partial(body, sizes),
        mesh=mesh,
        in_specs=(
            P("geom", "walker", "slab", None),
            P(),
            P(),
            P(),
            P("geom", None, None),
            P("geom", "walker"),
            P("geom", "walker", "slab", None),
            P("geom", "walker", "slab"),
            P("geom", "walker", "slab", None),
            P("geom", "walker", "slab", None),
        ),
        out_specs=(
            P("geom", "walker", "slab", None),
            P("geom", "walker", "slab", None),
            P("walker", None),
            P("walker", None),
            P("walker", None),
            P("geom", None, None),
        ),
        check_vma=False,
    )
```

```python
import functools

import jax
import jax.numpy as jnp
from jax import lax
from jax.experimental import pallas as pl
from jax.experimental.pallas import tpu as pltpu
from jax.sharding import PartitionSpec as P

RIM = 32
F32 = jnp.float32
BF16 = jnp.bfloat16
MESH = pl.DeviceIdType.MESH
BASES = (0, 8, 16, 24, 33, 41, 49, 57)
STEPS = 8
TILE = 16
MIB = 1024 * 1024
NN = ((1,), (0,))
NT = ((1,), (1,))


def dot(a, b, dims):
    return lax.dot_general(a, b, (dims, ((), ())), preferred_element_type=F32)


def split_dot(a, b, dims):
    high = a.astype(BF16)
    return dot(high, b, dims) + dot((a - high.astype(F32)).astype(BF16), b, dims)


def at(**coords):
    return dict(device_id=coords, device_id_type=MESH)


def iota(shape, dim):
    return lax.broadcasted_iota(jnp.int32, shape, dim)


def shift_matrices(turn_ref, slide_ref):
    rows = turn_ref.shape[0]
    wide = slide_ref.shape[0]
    for a in range(STEPS):
        moved = lax.rem(iota((rows, rows), 0) + a, rows)
        turn_ref[:, a * rows : (a + 1) * rows] = (moved == iota((rows, rows), 1)).astype(F32).astype(BF16)
    for b, base in enumerate(BASES):
        moved = iota((wide, wide), 1) + base
        slide_ref[:, b * wide : (b + 1) * wide] = (moved == iota((wide, wide), 0)).astype(F32).astype(BF16)


def slot_weights(nbr, env, count, off_ref, wt_ref):
    slots, rows = nbr.shape
    rel = nbr - iota((slots, rows), 1)
    off_ref[...] = rel - (rel > RIM).astype(jnp.int32)
    slot = iota((slots, rows), 0)
    wt_ref[...] = jnp.where(slot < count, env.astype(F32), 0.0)

    def place(step, acc):
        for u in range(8):
            k = step * 8 + u
            acc = acc + jnp.where(off_ref[pl.ds(k, 1), :] == slot, wt_ref[pl.ds(k, 1), :], 0.0)
        return acc

    weights = lax.fori_loop(0, slots // 8, place, jnp.zeros((slots, rows), F32))
    turned = weights
    sub = lax.rem(slot, STEPS)
    for a in range(1, STEPS):
        turned = jnp.where(sub == a, pltpu.roll(weights, a, 1), turned)
    return turned


def forward_pass(walkers, p_ref, q_ref, w_ref, t_ref, agg_ref, tot_ref):
    rows = w_ref.shape[2]
    tiles = p_ref.shape[0] // TILE
    lane = iota((TILE, rows), 1)

    def tile_work(tile, carry):
        r0 = pl.multiple_of(tile * TILE, TILE)
        w = tile // (tiles // walkers)
        here = pl.ds(r0, TILE)
        for a in range(STEPS):
            pa = p_ref[here, a * rows : (a + 1) * rows]
            ga, sa = [], []
            for b in range(len(BASES)):
                m = b * STEPS + a
                h = q_ref[here, 2 * b * rows : (2 * b + 1) * rows]
                if a:
                    h = jnp.where(lane < a, q_ref[here, (2 * b + 1) * rows : (2 * b + 2) * rows], h)
                h = h + pa
                u = 1.0 + jnp.tanh(h)
                g = h * u
                wm = w_ref[w, pl.ds(m, 1), :]
                t = wm * (u + g * (2.0 - u))
                t_ref[m, here, :] = t
                ga.append(wm * g)
                sa.append(t)
            while len(ga) > 1:
                ga = [ga[n] + ga[n + 1] for n in range(0, len(ga), 2)]
                sa = [sa[n] + sa[n + 1] for n in range(0, len(sa), 2)]
            agg_ref[here, a * rows : (a + 1) * rows] = ga[0].astype(BF16)
            tot_ref[here, a * rows : (a + 1) * rows] = sa[0].astype(BF16)
        return carry

    lax.fori_loop(0, tiles, tile_work, 0)


def backward_pass(first, count, d_ref, t_ref, v_ref):
    rows = t_ref.shape[2]
    nb = len(BASES)
    lane = iota((TILE, rows), 1)

    def tile_work(tile, carry):
        here = pl.ds(pl.multiple_of(tile * TILE, TILE), TILE)
        ds = [d_ref[here, a * rows : (a + 1) * rows] for a in range(STEPS)]
        for b in range(nb):
            total = wrap = None
            for a in range(STEPS):
                v = t_ref[b * STEPS + a, here, :] * ds[a]
                total = v if a == 0 else total + v
                if a:
                    c = jnp.where(lane < a, v, 0.0)
                    wrap = c if a == 1 else wrap + c
            v_ref[here, 2 * b * rows : (2 * b + 1) * rows] = (total - wrap).astype(BF16)
            v_ref[here, (2 * b + 1) * rows : (2 * b + 2) * rows] = wrap.astype(BF16)
        return carry

    lax.fori_loop(first, first + count, tile_work, 0)


def first_kernel(
    slabs, lat_ref, feats_hbm, nbr_hbm, env_hbm, cnt_hbm, ws_hbm, geo_hbm,
    before_ref, after_ref, w_ref, p_ref, turn_ref, slide_ref, feats_ref,
    nbr_ref, env_ref, cnt_ref, ws_ref, geo_ref, off_ref, wt_ref, load_sem, send_sem, recv_sem,
):
    me = lax.axis_index("slab")
    nxt, prv = lax.rem(me + 1, slabs), lax.rem(me + slabs - 1, slabs)
    barrier = pltpu.get_barrier_semaphore()
    pl.semaphore_signal(barrier, inc=1, **at(slab=nxt))
    pl.semaphore_signal(barrier, inc=1, **at(slab=prv))
    loads = []
    for n, (src, dst) in enumerate((
        (feats_hbm, feats_ref), (nbr_hbm, nbr_ref), (env_hbm, env_ref), (cnt_hbm, cnt_ref), (ws_hbm, ws_ref), (geo_hbm, geo_ref),
    )):
        loads.append(pltpu.make_async_copy(src, dst, load_sem.at[n]))
        loads[-1].start()
    walkers, rows, width = feats_ref.shape
    shift_matrices(turn_ref, slide_ref)
    for c in loads:
        c.wait()
    pl.semaphore_wait(barrier, 2)
    up = pltpu.make_async_remote_copy(
        feats_ref.at[:, pl.ds(rows - RIM, RIM)], before_ref, send_sem.at[0], recv_sem.at[0], **at(slab=nxt)
    )
    down = pltpu.make_async_remote_copy(
        feats_ref.at[:, pl.ds(0, RIM)], after_ref, send_sem.at[1], recv_sem.at[1], **at(slab=prv)
    )
    up.start()
    down.start()
    ws_t = ws_ref[...].T
    geo = geo_ref[...]
    for w in range(walkers):
        w_ref[w] = slot_weights(nbr_ref[w], env_ref[w], cnt_ref[pl.ds(w, 1), :], off_ref, wt_ref)
        lats = geo.shape[0]
        row = jnp.sum(jnp.where(iota((lats, width), 0) == lat_ref[0, w], geo, 0.0), axis=0, keepdims=True)
        p = (dot(feats_ref[w], ws_ref[...], NN) + row).T
        p_ref[w * width : (w + 1) * width, :] = split_dot(0.5 * p, turn_ref[...], NN)
    up.wait()
    down.wait()


def main_kernel(
    slabs, walks, geoms,
    lat_ref, cnt_ref, before_ref, after_ref, w_ref, p_ref, turn_ref, slide_ref, feats_ref, ws_hbm, wp_hbm, wu_hbm, cot_hbm,
    newf_ref, df_ref, share_ref, geo_out_ref,
    ws_ref, wp_ref, wu_ref, cot_ref, ext_ref, ext_t_ref, q_ref, t_ref, agg_ref, tot_ref, d_ref, v_ref, own_ref,
    rim_out, rim_in, grads_ref, half_us, half_p,
    core_out_us, core_in_us, core_out_p, core_in_p, plane_out, plane_in, ring_out_us, ring_in_us, ring_out_p, ring_in_p,
    row_us, gather_us, row_p, gather_p, gslab_out, gslab_in, gring_out, gring_in,
    load_sem, send_sem, recv_sem,
):
    slab, z, geom = lax.axis_index("slab"), lax.axis_index("walker"), lax.axis_index("geom")
    core = lax.rem(geom, 2)
    pair = geom - core
    half_geoms = geoms // 2
    chips = slabs * half_geoms
    chip = slab * half_geoms + pair // 2
    nxt, prv = lax.rem(slab + 1, slabs), lax.rem(slab + slabs - 1, slabs)
    walkers, rows, width = feats_ref.shape
    lanes = width // 2
    lats = gslab_out.shape[0]
    tiles = walkers * width // TILE

    def chip_at(c, k):
        return at(slab=c // half_geoms, geom=lax.rem(c, half_geoms) * 2 + k)

    barrier = pltpu.get_barrier_semaphore()
    for k in range(2):
        kk = core if k == 0 else 1 - core
        for r in range(k ^ 1, chips):
            pl.semaphore_signal(barrier, inc=1, **chip_at(lax.rem(chip + r, chips), kk))
    for r in range(1, walks):
        pl.semaphore_signal(barrier, inc=1, **at(walker=lax.rem(z + r, walks)))

    def send(src, dst, n, where):
        c = pltpu.make_async_remote_copy(src, dst, send_sem.at[n], recv_sem.at[n], **where)
        c.start()
        return c

    def settle(ref, n):
        c = pltpu.make_async_remote_copy(ref, ref, send_sem.at[n], recv_sem.at[n], **at(slab=nxt))
        c.wait_send()
        c.wait_recv()

    loads = []
    for n, (src, dst) in enumerate(((wp_hbm, wp_ref), (wu_hbm, wu_ref), (cot_hbm, cot_ref), (ws_hbm, ws_ref))):
        loads.append(pltpu.make_async_copy(src, dst, load_sem.at[n]))
        loads[-1].start()

    wide = ext_ref.shape[1]
    for w in range(walkers):
        ext_ref[w, pl.ds(0, RIM), :] = before_ref[w]
        ext_ref[w, pl.ds(RIM, rows), :] = feats_ref[w]
        ext_ref[w, pl.ds(RIM + rows, RIM), :] = after_ref[w]
        ext_ref[w, pl.ds(2 * RIM + rows, wide - rows - 2 * RIM), :] = jnp.zeros((wide - rows - 2 * RIM, width), BF16)
    for c in loads:
        c.wait()
    for w in range(walkers):
        q = (0.5 * dot(ext_ref[w], wp_ref[...], NN)).astype(BF16)
        ext_t_ref[w] = ext_ref[w].T
        q_ref[w * width : (w + 1) * width, :] = dot(q.T, slide_ref[...], NN)

    forward_pass(walkers, p_ref, q_ref, w_ref, t_ref, agg_ref, tot_ref)

    dgeo = jnp.zeros((lats, width), F32)
    dps = []
    for w in range(walkers):
        part = slice(w * width, (w + 1) * width)
        inv = 1.0 / cnt_ref[pl.ds(w, 1), :].astype(F32)
        agg_t = (dot(agg_ref[part, :], turn_ref[...], NT) * inv).astype(BF16)
        upd = dot(agg_t.T, wu_ref[...], NN)
        sig = 0.5 + 0.5 * jnp.tanh(0.5 * upd)
        newf_ref[w] = (feats_ref[w].astype(F32) + upd * sig).astype(BF16)
        du = (cot_ref[w].astype(F32) * (sig * (1.0 + upd * (1.0 - sig)))).astype(BF16)
        dd = 0.5 * dot(wu_ref[...], du, NT) * inv
        d_ref[part, :] = split_dot(dd, turn_ref[...], NN)
        dp = (dd * dot(tot_ref[part, :], turn_ref[...], NT)).T
        mine = iota((lats, width), 0) == lat_ref[0, w]
        dgeo = dgeo + jnp.where(mine, jnp.sum(dp, axis=0, keepdims=True), 0.0)
        dp = dp.astype(BF16)
        dps.append(dp)
        feats_t = feats_ref[w].T
        for n, term in enumerate((dot(feats_t, dp, NN), dot(agg_t, du, NN))):
            grads_ref[n] = term if w == 0 else grads_ref[n] + term
    gslab_out[...] = dgeo
    for w in range(walkers):
        df_ref[w] = cot_ref[w].astype(F32) + dot(dps[w], ws_ref[...], NT)

    mine = pl.ds(pl.multiple_of(core * lanes, lanes), lanes)
    theirs = pl.ds(pl.multiple_of((1 - core) * lanes, lanes), lanes)
    core_out_us[...] = grads_ref[pl.ds(0, 2), :, theirs].astype(BF16)
    pl.semaphore_wait(barrier, 2 * chips - 1 + walks - 1)
    cross = send(core_out_us, core_in_us, 0, at(geom=pair + 1 - core))
    gslab_in[slab] = gslab_out[...]
    for r in range(1, slabs):
        send(gslab_out, gslab_in.at[slab], 1, at(slab=lax.rem(slab + r, slabs)))

    backward_pass(0, tiles // 2, d_ref, t_ref, v_ref)

    cross.wait()
    half_us[...] = grads_ref[pl.ds(0, 2), :, mine] + core_in_us[...].astype(F32)
    for c in range(chips):
        for n in range(2):
            plane_out[c, n] = half_us[n, pl.ds(c, walks, stride=chips), :].astype(BF16)
    plane_in[chip] = plane_out[chip]
    for r in range(1, chips):
        to = lax.rem(chip + r, chips)
        send(plane_out.at[to], plane_in.at[chip], 2, chip_at(to, core))

    backward_pass(tiles // 2, tiles // 2, d_ref, t_ref, v_ref)

    for w in range(walkers):
        dq = dot(v_ref[w * width : (w + 1) * width, :], slide_ref[...], NT).T
        own_ref[w] = dq[RIM : RIM + rows]
        dqb = dq.astype(BF16)
        rim_out[0, w] = dqb[:RIM]
        rim_out[1, w] = dqb[RIM + rows : 2 * RIM + rows]
        term = dot(ext_t_ref[w], dqb, NN)
        grads_ref[2] = term if w == 0 else grads_ref[2] + term
    core_out_p[...] = grads_ref[2, :, theirs].astype(BF16)
    cross = send(core_out_p, core_in_p, 3, at(geom=pair + 1 - core))
    down = send(rim_out.at[0], rim_in.at[0], 4, at(slab=prv))
    up = send(rim_out.at[1], rim_in.at[1], 5, at(slab=nxt))
    cross.wait()
    half_p[...] = (grads_ref[2, :, mine] + core_in_p[...].astype(F32)).astype(BF16)
    for v in range(walks):
        ring_out_p[v] = half_p[pl.ds(v * (width // walks), width // walks), :]
    ring_in_p[z] = ring_out_p[z]
    for r in range(1, walks):
        to = lax.rem(z + r, walks)
        send(ring_out_p.at[to], ring_in_p.at[z], 6, at(walker=to))

    settle(gslab_in.at[pl.ds(0, slabs - 1)], 1)
    gsum = gslab_in[0]
    for s in range(1, slabs):
        gsum = gsum + gslab_in[s]
    gring_out[...] = gsum
    gring_in[z] = gsum
    for r in range(1, walks):
        send(gring_out, gring_in.at[z], 7, at(walker=lax.rem(z + r, walks)))

    settle(plane_in.at[pl.ds(0, chips - 1)], 2)
    part = plane_in[0].astype(F32)
    for c in range(1, chips):
        part = part + plane_in[c].astype(F32)
    for v in range(walks):
        for n in range(2):
            ring_out_us[v, pl.ds(n, 1), :] = part[n, v : v + 1, :]
    ring_in_us[z] = ring_out_us[z]
    for r in range(1, walks):
        to = lax.rem(z + r, walks)
        send(ring_out_us.at[to], ring_in_us.at[z], 8, at(walker=to))

    down.wait()
    up.wait()
    for w in range(walkers):
        dq = jnp.concatenate(
            (
                own_ref[w, pl.ds(0, RIM), :] + rim_in[1, w].astype(F32),
                own_ref[w, pl.ds(RIM, rows - 2 * RIM), :],
                own_ref[w, pl.ds(rows - RIM, RIM), :] + rim_in[0, w].astype(F32),
            ),
            axis=0,
        ).astype(BF16)
        df_ref[w] = df_ref[w] + dot(dq, wp_ref[...], NT)

    slot = core * chips + chip
    settle(ring_in_p.at[pl.ds(0, walks - 1)], 6)
    part = ring_in_p[0].astype(F32)
    for v in range(1, walks):
        part = part + ring_in_p[v].astype(F32)
    row_p[...] = part.astype(BF16)
    gather_p[slot] = row_p[...]
    for k in range(2):
        kk = core if k == 0 else 1 - core
        for r in range(k ^ 1, chips):
            send(row_p, gather_p.at[slot], 9, chip_at(lax.rem(chip + r, chips), kk))

    settle(ring_in_us.at[pl.ds(0, walks - 1)], 8)
    row = ring_in_us[0]
    for v in range(1, walks):
        row = row + ring_in_us[v]
    row_us[...] = row
    gather_us[slot] = row
    for k in range(2):
        kk = core if k == 0 else 1 - core
        for r in range(k ^ 1, chips):
            send(row_us, gather_us.at[slot], 10, chip_at(lax.rem(chip + r, chips), kk))

    settle(gring_in.at[pl.ds(0, walks - 1)], 7)
    gsum = gring_in[0]
    for v in range(1, walks):
        gsum = gsum + gring_in[v]
    geo_out_ref[...] = gsum

    settle(gather_p.at[pl.ds(0, 2 * chips - 1)], 9)
    for k in range(2):
        part = gather_p[k * chips].astype(F32)
        for c in range(1, chips):
            part = part + gather_p[k * chips + c].astype(F32)
        share_ref[1, :, pl.ds(k * lanes, lanes)] = part
    settle(gather_us.at[pl.ds(0, 2 * chips - 1)], 10)
    for n in range(2):
        for k in range(2):
            for c in range(chips):
                share_ref[2 * n, pl.ds(c, 1), pl.ds(k * lanes, lanes)] = gather_us[k * chips + c, pl.ds(n, 1), :]


def last_kernel(newf, df, share, geo, newf_out, df_out, gs_out, gp_out, gu_out, geo_out, sem):
    copies = [
        pltpu.make_async_copy(src, dst, sem.at[n])
        for n, (src, dst) in enumerate((
            (df, df_out), (newf, newf_out), (share.at[0], gs_out), (share.at[1], gp_out), (share.at[2], gu_out), (geo, geo_out),
        ))
    ]
    for c in copies:
        c.start()
    for c in copies:
        c.wait()


def vmem(n):
    return [pl.BlockSpec(memory_space=pltpu.VMEM)] * n


def hbm(n):
    return [pl.BlockSpec(memory_space=pltpu.HBM)] * n


def body(sizes, features, w_self, w_pair, w_update, geo_embed, lattice, neighbours, counts, envelope, cotangent):
    slabs, walks, geoms = sizes
    feats, cot = features[0], cotangent[0]
    walkers, rows, width = feats.shape
    slots = neighbours.shape[3]
    lats = geo_embed.shape[1]
    wide = 2 * rows
    nbr = jnp.swapaxes(neighbours[0], 1, 2)
    env = jnp.swapaxes(envelope[0], 1, 2)
    sds = jax.ShapeDtypeStruct
    scr = pltpu.VMEM
    dma = pltpu.SemaphoreType.DMA
    smem = [pl.BlockSpec(memory_space=pltpu.SMEM)]
    rim = sds((walkers, RIM, width), BF16)
    before, after, weights, p, turn, slide, feats_v = pl.pallas_call(
        functools.partial(first_kernel, slabs),
        out_shape=(
            rim,
            rim,
            sds((walkers, slots, rows), F32),
            sds((walkers * width, STEPS * rows), F32),
            sds((rows, STEPS * rows), BF16),
            sds((wide, len(BASES) * wide), BF16),
            sds((walkers, rows, width), BF16),
        ),
        in_specs=smem + hbm(6),
        out_specs=vmem(7),
        scratch_shapes=[
            scr((walkers, slots, rows), jnp.int32),
            scr((walkers, slots, rows), BF16),
            scr((walkers, rows), jnp.int32),
            scr((width, width), BF16),
            scr((lats, width), F32),
            scr((slots, rows), jnp.int32),
            scr((slots, rows), F32),
            dma((6,)),
            dma((2,)),
            dma((2,)),
        ],
        compiler_params=pltpu.CompilerParams(collective_id=0, has_side_effects=True, vmem_limit_bytes=12 * MIB),
        name="first",
    )(lattice, feats, nbr, env, counts[0], w_self, geo_embed[0])

    chips = slabs * geoms // 2
    lanes = width // 2
    share_rows = width // walks
    newf, df, share, geo = pl.pallas_call(
        functools.partial(main_kernel, slabs, walks, geoms),
        out_shape=(
            sds((walkers, rows, width), BF16),
            sds((walkers, rows, width), F32),
            sds((3, share_rows, width), F32),
            sds((lats, width), F32),
        ),
        in_specs=smem + vmem(8) + hbm(4),
        out_specs=vmem(4),
        scratch_shapes=[
            scr((width, width), BF16),
            scr((width, width), BF16),
            scr((width, width), BF16),
            scr((walkers, rows, width), BF16),
            scr((walkers, wide, width), BF16),
            scr((walkers, width, wide), BF16),
            scr((walkers * width, len(BASES) * wide), F32),
            scr((slots, walkers * width, rows), F32),
            scr((walkers * width, STEPS * rows), BF16),
            scr((walkers * width, STEPS * rows), BF16),
            scr((walkers * width, STEPS * rows), F32),
            scr((walkers * width, len(BASES) * wide), BF16),
            scr((walkers, rows, width), F32),
            scr((2, walkers, RIM, width), BF16),
            scr((2, walkers, RIM, width), BF16),
            scr((3, width, width), F32),
            scr((2, width, lanes), F32),
            scr((width, lanes), BF16),
            scr((2, width, lanes), BF16),
            scr((2, width, lanes), BF16),
            scr((width, lanes), BF16),
            scr((width, lanes), BF16),
            scr((chips, 2, walks, lanes), BF16),
            scr((chips, 2, walks, lanes), BF16),
            scr((walks, 2, lanes), F32),
            scr((walks, 2, lanes), F32),
            scr((walks, share_rows, lanes), BF16),
            scr((walks, share_rows, lanes), BF16),
            scr((2, lanes), F32),
            scr((2 * chips, 2, lanes), F32),
            scr((share_rows, lanes), BF16),
            scr((2 * chips, share_rows, lanes), BF16),
            scr((lats, width), F32),
            scr((slabs, lats, width), F32),
            scr((lats, width), F32),
            scr((walks, lats, width), F32),
            dma((4,)),
            dma((11,)),
            dma((11,)),
        ],
        compiler_params=pltpu.CompilerParams(collective_id=1, has_side_effects=True, vmem_limit_bytes=44 * MIB),
        name="main",
    )(lattice, counts[0], before, after, weights, p, turn, slide, feats_v, w_self, w_pair, w_update, cot)

    block = sds((share_rows, width), F32)
    newf, df, gs, gp, gu, geo = pl.pallas_call(
        last_kernel,
        out_shape=(
            sds((walkers, rows, width), BF16),
            sds((walkers, rows, width), F32),
            block,
            block,
            block,
            sds((lats, width), F32),
        ),
        in_specs=vmem(4),
        out_specs=hbm(6),
        scratch_shapes=[dma((6,))],
        compiler_params=pltpu.CompilerParams(vmem_limit_bytes=4 * MIB),
        name="last",
    )(newf, df, share, geo)
    return newf[None], df[None], gs, gp, gu, geo[None]


def solution(mesh):
    sizes = (mesh.shape["slab"], mesh.shape["walker"], mesh.shape["geom"])
    return jax.shard_map(
        functools.partial(body, sizes),
        mesh=mesh,
        in_specs=(
            P("geom", "walker", "slab", None),
            P(),
            P(),
            P(),
            P("geom", None, None),
            P("geom", "walker"),
            P("geom", "walker", "slab", None),
            P("geom", "walker", "slab"),
            P("geom", "walker", "slab", None),
            P("geom", "walker", "slab", None),
        ),
        out_specs=(
            P("geom", "walker", "slab", None),
            P("geom", "walker", "slab", None),
            P("walker", None),
            P("walker", None),
            P("walker", None),
            P("geom", None, None),
        ),
        check_vma=False,
    )
```

```python
import functools

import jax
import jax.numpy as jnp
from jax import lax
from jax.experimental import pallas as pl
from jax.experimental.pallas import tpu as pltpu
from jax.sharding import PartitionSpec as P

RIM = 32
F32 = jnp.float32
BF16 = jnp.bfloat16
MESH = pl.DeviceIdType.MESH
BASES = (0, 8, 16, 24, 33, 41, 49, 57)
STEPS = 8
TILE = 16
MIB = 1024 * 1024
NN = ((1,), (0,))
NT = ((1,), (1,))


def dot(a, b, dims):
    return lax.dot_general(a, b, (dims, ((), ())), preferred_element_type=F32)


def split_dot(a, b, dims):
    high = a.astype(BF16)
    return dot(high, b, dims) + dot((a - high.astype(F32)).astype(BF16), b, dims)


def at(**coords):
    return dict(device_id=coords, device_id_type=MESH)


def iota(shape, dim):
    return lax.broadcasted_iota(jnp.int32, shape, dim)


def shift_matrices(turn_ref, slide_ref):
    rows = turn_ref.shape[0]
    wide = slide_ref.shape[0]
    for a in range(STEPS):
        moved = lax.rem(iota((rows, rows), 0) + a, rows)
        turn_ref[:, a * rows : (a + 1) * rows] = (moved == iota((rows, rows), 1)).astype(F32).astype(BF16)
    for b, base in enumerate(BASES):
        moved = iota((wide, wide), 1) + base
        slide_ref[:, b * wide : (b + 1) * wide] = (moved == iota((wide, wide), 0)).astype(F32).astype(BF16)


def slot_weights(nbr, env, count, off_ref, wt_ref):
    slots, rows = nbr.shape
    rel = nbr - iota((slots, rows), 1)
    off_ref[...] = rel - (rel > RIM).astype(jnp.int32)
    slot = iota((slots, rows), 0)
    wt_ref[...] = jnp.where(slot < count, env.astype(F32), 0.0)

    def place(step, acc):
        for u in range(8):
            k = step * 8 + u
            acc = acc + jnp.where(off_ref[pl.ds(k, 1), :] == slot, wt_ref[pl.ds(k, 1), :], 0.0)
        return acc

    weights = lax.fori_loop(0, slots // 8, place, jnp.zeros((slots, rows), F32))
    turned = weights
    sub = lax.rem(slot, STEPS)
    for a in range(1, STEPS):
        turned = jnp.where(sub == a, pltpu.roll(weights, a, 1), turned)
    return turned


def forward_pass(walkers, p_ref, q_ref, w_ref, t_ref, agg_ref, tot_ref):
    rows = w_ref.shape[2]
    tiles = p_ref.shape[0] // TILE
    lane = iota((TILE, rows), 1)

    def tile_work(tile, carry):
        r0 = pl.multiple_of(tile * TILE, TILE)
        w = tile // (tiles // walkers)
        here = pl.ds(r0, TILE)
        for a in range(STEPS):
            pa = p_ref[here, a * rows : (a + 1) * rows]
            ga, sa = [], []
            for b in range(len(BASES)):
                m = b * STEPS + a
                h = q_ref[here, 2 * b * rows : (2 * b + 1) * rows]
                if a:
                    h = jnp.where(lane < a, q_ref[here, (2 * b + 1) * rows : (2 * b + 2) * rows], h)
                h = h + pa
                u = 1.0 + jnp.tanh(h)
                wu = u * w_ref[w, pl.ds(m, 1), :]
                wg = h * wu
                t = wu + wg * (2.0 - u)
                t_ref[m, here, :] = t
                ga.append(wg)
                sa.append(t)
            while len(ga) > 1:
                ga = [ga[n] + ga[n + 1] for n in range(0, len(ga), 2)]
                sa = [sa[n] + sa[n + 1] for n in range(0, len(sa), 2)]
            agg_ref[here, a * rows : (a + 1) * rows] = ga[0].astype(BF16)
            tot_ref[here, a * rows : (a + 1) * rows] = sa[0].astype(BF16)
        return carry

    lax.fori_loop(0, tiles, tile_work, 0)


def backward_pass(first, count, d_ref, t_ref, v_ref):
    rows = t_ref.shape[2]
    nb = len(BASES)
    lane = iota((TILE, rows), 1)

    def tile_work(tile, carry):
        here = pl.ds(pl.multiple_of(tile * TILE, TILE), TILE)
        ds = [d_ref[here, a * rows : (a + 1) * rows] for a in range(STEPS)]
        for b in range(nb):
            total = wrap = None
            for a in range(STEPS):
                v = t_ref[b * STEPS + a, here, :] * ds[a]
                total = v if a == 0 else total + v
                if a:
                    c = jnp.where(lane < a, v, 0.0)
                    wrap = c if a == 1 else wrap + c
            v_ref[here, 2 * b * rows : (2 * b + 1) * rows] = (total - wrap).astype(BF16)
            v_ref[here, (2 * b + 1) * rows : (2 * b + 2) * rows] = wrap.astype(BF16)
        return carry

    lax.fori_loop(first, first + count, tile_work, 0)


def first_kernel(
    slabs, lat_hbm, feats_hbm, nbr_hbm, env_hbm, cnt_hbm, ws_hbm, geo_hbm,
    before_ref, after_ref, w_ref, p_ref, turn_ref, slide_ref, feats_ref, inv_ref, member_ref,
    lat_ref, nbr_ref, env_ref, cnt_ref, ws_ref, geo_ref, off_ref, wt_ref, load_sem, send_sem, recv_sem,
):
    me = lax.axis_index("slab")
    nxt, prv = lax.rem(me + 1, slabs), lax.rem(me + slabs - 1, slabs)
    barrier = pltpu.get_barrier_semaphore()
    pl.semaphore_signal(barrier, inc=1, **at(slab=nxt))
    pl.semaphore_signal(barrier, inc=1, **at(slab=prv))
    loads = []
    for n, (src, dst) in enumerate((
        (feats_hbm, feats_ref), (nbr_hbm, nbr_ref), (env_hbm, env_ref), (cnt_hbm, cnt_ref), (ws_hbm, ws_ref), (geo_hbm, geo_ref), (lat_hbm, lat_ref),
    )):
        loads.append(pltpu.make_async_copy(src, dst, load_sem.at[n]))
        loads[-1].start()
    walkers, rows, width = feats_ref.shape
    shift_matrices(turn_ref, slide_ref)
    for c in loads:
        c.wait()
    pl.semaphore_wait(barrier, 2)
    up = pltpu.make_async_remote_copy(
        feats_ref.at[:, pl.ds(rows - RIM, RIM)], before_ref, send_sem.at[0], recv_sem.at[0], **at(slab=nxt)
    )
    down = pltpu.make_async_remote_copy(
        feats_ref.at[:, pl.ds(0, RIM)], after_ref, send_sem.at[1], recv_sem.at[1], **at(slab=prv)
    )
    up.start()
    down.start()
    ws_t = ws_ref[...].T
    geo = geo_ref[...]
    inv_ref[...] = 1.0 / cnt_ref[...].astype(F32)
    for w in range(walkers):
        w_ref[w] = slot_weights(nbr_ref[w], env_ref[w], cnt_ref[pl.ds(w, 1), :], off_ref, wt_ref)
        lats = geo.shape[0]
        member = (iota((lats, width), 0) == lat_ref[0, w]).astype(F32)
        member_ref[w] = member
        row = jnp.sum(jnp.where(member > 0.0, geo, 0.0), axis=0, keepdims=True)
        p = (dot(feats_ref[w], ws_ref[...], NN) + row).T
        p_ref[w * width : (w + 1) * width, :] = split_dot(0.5 * p, turn_ref[...], NN)
    up.wait()
    down.wait()


def main_kernel(
    slabs, walks, geoms,
    before_ref, after_ref, w_ref, p_ref, turn_ref, slide_ref, feats_ref, inv_ref, member_ref, ws_hbm, wp_hbm, wu_hbm, cot_hbm,
    newf_ref, df_ref, share_ref, geo_out_ref,
    ws_ref, wp_ref, wu_ref, cot_ref, ext_ref, ext_t_ref, q_ref, t_ref, agg_ref, tot_ref, d_ref, v_ref, own_ref,
    rim_out, rim_in, grads_ref, half_us, half_p,
    core_in_us, core_in_p, plane_out, plane_in, ring_out_us, ring_in_us, ring_out_p, ring_in_p,
    row_us, gather_us, row_p, gather_p, gslab_out, gslab_in, gring_out, gring_in,
    load_sem, send_sem, recv_sem,
):
    slab, z, geom = lax.axis_index("slab"), lax.axis_index("walker"), lax.axis_index("geom")
    core = lax.rem(geom, 2)
    pair = geom - core
    half_geoms = geoms // 2
    chips = slabs * half_geoms
    chip = slab * half_geoms + pair // 2
    nxt, prv = lax.rem(slab + 1, slabs), lax.rem(slab + slabs - 1, slabs)
    walkers, rows, width = feats_ref.shape
    lanes = width // 2
    lats = gslab_out.shape[0]
    tiles = walkers * width // TILE

    def chip_at(c, k):
        return at(slab=c // half_geoms, geom=lax.rem(c, half_geoms) * 2 + k)

    barrier = pltpu.get_barrier_semaphore()
    for k in range(2):
        kk = core if k == 0 else 1 - core
        for r in range(k ^ 1, chips):
            pl.semaphore_signal(barrier, inc=1, **chip_at(lax.rem(chip + r, chips), kk))
    for r in range(1, walks):
        pl.semaphore_signal(barrier, inc=1, **at(walker=lax.rem(z + r, walks)))

    def send(src, dst, n, where):
        c = pltpu.make_async_remote_copy(src, dst, send_sem.at[n], recv_sem.at[n], **where)
        c.start()
        return c

    def settle(ref, n):
        c = pltpu.make_async_remote_copy(ref, ref, send_sem.at[n], recv_sem.at[n], **at(slab=nxt))
        c.wait_send()
        c.wait_recv()

    loads = []
    for n, (src, dst) in enumerate(((wp_hbm, wp_ref), (wu_hbm, wu_ref), (cot_hbm, cot_ref), (ws_hbm, ws_ref))):
        loads.append(pltpu.make_async_copy(src, dst, load_sem.at[n]))
        loads[-1].start()

    wide = ext_ref.shape[1]
    for w in range(walkers):
        ext_ref[w, pl.ds(0, RIM), :] = before_ref[w]
        ext_ref[w, pl.ds(RIM, rows), :] = feats_ref[w]
        ext_ref[w, pl.ds(RIM + rows, RIM), :] = after_ref[w]
        ext_ref[w, pl.ds(2 * RIM + rows, wide - rows - 2 * RIM), :] = jnp.zeros((wide - rows - 2 * RIM, width), BF16)
    for c in loads:
        c.wait()
    for w in range(walkers):
        q = (0.5 * dot(ext_ref[w], wp_ref[...], NN)).astype(BF16)
        ext_t_ref[w] = ext_ref[w].T
        q_ref[w * width : (w + 1) * width, :] = dot(q.T, slide_ref[...], NN)

    forward_pass(walkers, p_ref, q_ref, w_ref, t_ref, agg_ref, tot_ref)

    dgeo = jnp.zeros((lats, width), F32)
    dps = []
    for w in range(walkers):
        part = slice(w * width, (w + 1) * width)
        inv = inv_ref[pl.ds(w, 1), :]
        agg_t = (dot(agg_ref[part, :], turn_ref[...], NT) * inv).astype(BF16)
        upd = dot(agg_t.T, wu_ref[...], NN)
        sig = 0.5 + 0.5 * jnp.tanh(0.5 * upd)
        newf_ref[w] = (feats_ref[w].astype(F32) + upd * sig).astype(BF16)
        du = (cot_ref[w].astype(F32) * (sig * (1.0 + upd * (1.0 - sig)))).astype(BF16)
        dd = 0.5 * dot(wu_ref[...], du, NT) * inv
        d_ref[part, :] = split_dot(dd, turn_ref[...], NN)
        dp = (dd * dot(tot_ref[part, :], turn_ref[...], NT)).T
        dgeo = dgeo + jnp.where(member_ref[w] > 0.0, jnp.sum(dp, axis=0, keepdims=True), 0.0)
        dp = dp.astype(BF16)
        dps.append(dp)
        feats_t = feats_ref[w].T
        for n, term in enumerate((dot(feats_t, dp, NN), dot(agg_t, du, NN))):
            grads_ref[n] = term if w == 0 else grads_ref[n] + term
    gslab_out[...] = dgeo
    for w in range(walkers):
        df_ref[w] = cot_ref[w].astype(F32) + dot(dps[w], ws_ref[...], NT)

    mine = pl.ds(pl.multiple_of(core * lanes, lanes), lanes)
    theirs = pl.ds(pl.multiple_of((1 - core) * lanes, lanes), lanes)
    pl.semaphore_wait(barrier, 2 * chips - 1 + walks - 1)
    cross = send(grads_ref.at[pl.ds(0, 2), :, theirs], core_in_us, 0, at(geom=pair + 1 - core))
    gslab_in[slab] = gslab_out[...]
    for r in range(1, slabs):
        send(gslab_out, gslab_in.at[slab], 1, at(slab=lax.rem(slab + r, slabs)))

    backward_pass(0, tiles // 2, d_ref, t_ref, v_ref)

    cross.wait()
    half_us[...] = grads_ref[pl.ds(0, 2), :, mine] + core_in_us[...]
    for c in range(chips):
        for n in range(2):
            plane_out[c, n] = half_us[n, pl.ds(c, walks, stride=chips), :].astype(BF16)
    plane_in[chip] = plane_out[chip]
    for r in range(1, chips):
        to = lax.rem(chip + r, chips)
        send(plane_out.at[to], plane_in.at[chip], 2, chip_at(to, core))

    backward_pass(tiles // 2, tiles // 2, d_ref, t_ref, v_ref)

    settle(gslab_in.at[pl.ds(0, slabs - 1)], 1)
    gsum = gslab_in[0]
    for s in range(1, slabs):
        gsum = gsum + gslab_in[s]
    gring_out[...] = gsum
    gring_in[z] = gsum
    for r in range(1, walks):
        send(gring_out, gring_in.at[z], 7, at(walker=lax.rem(z + r, walks)))

    for w in range(walkers):
        dq = dot(v_ref[w * width : (w + 1) * width, :], slide_ref[...], NT).T
        own_ref[w] = dq[RIM : RIM + rows]
        dqb = dq.astype(BF16)
        rim_out[0, w] = dqb[:RIM]
        rim_out[1, w] = dqb[RIM + rows : 2 * RIM + rows]
        term = dot(ext_t_ref[w], dqb, NN)
        grads_ref[2] = term if w == 0 else grads_ref[2] + term
    cross = send(grads_ref.at[2, :, theirs], core_in_p, 3, at(geom=pair + 1 - core))
    down = send(rim_out.at[0], rim_in.at[0], 4, at(slab=prv))
    up = send(rim_out.at[1], rim_in.at[1], 5, at(slab=nxt))
    cross.wait()
    half_p[...] = (grads_ref[2, :, mine] + core_in_p[...]).astype(BF16)
    for v in range(walks):
        ring_out_p[v] = half_p[pl.ds(v * (width // walks), width // walks), :]
    ring_in_p[z] = ring_out_p[z]
    for r in range(1, walks):
        to = lax.rem(z + r, walks)
        send(ring_out_p.at[to], ring_in_p.at[z], 6, at(walker=to))

    settle(plane_in.at[pl.ds(0, chips - 1)], 2)
    part = plane_in[0].astype(F32)
    for c in range(1, chips):
        part = part + plane_in[c].astype(F32)
    for v in range(walks):
        for n in range(2):
            ring_out_us[v, pl.ds(n, 1), :] = part[n, v : v + 1, :]
    ring_in_us[z] = ring_out_us[z]
    for r in range(1, walks):
        to = lax.rem(z + r, walks)
        send(ring_out_us.at[to], ring_in_us.at[z], 8, at(walker=to))

    down.wait()
    up.wait()
    for w in range(walkers):
        dq = jnp.concatenate(
            (
                own_ref[w, pl.ds(0, RIM), :] + rim_in[1, w].astype(F32),
                own_ref[w, pl.ds(RIM, rows - 2 * RIM), :],
                own_ref[w, pl.ds(rows - RIM, RIM), :] + rim_in[0, w].astype(F32),
            ),
            axis=0,
        ).astype(BF16)
        df_ref[w] = df_ref[w] + dot(dq, wp_ref[...], NT)

    slot = core * chips + chip
    settle(ring_in_p.at[pl.ds(0, walks - 1)], 6)
    part = ring_in_p[0].astype(F32)
    for v in range(1, walks):
        part = part + ring_in_p[v].astype(F32)
    row_p[...] = part.astype(BF16)
    gather_p[slot] = row_p[...]
    for k in range(2):
        kk = core if k == 0 else 1 - core
        for r in range(k ^ 1, chips):
            send(row_p, gather_p.at[slot], 9, chip_at(lax.rem(chip + r, chips), kk))

    settle(ring_in_us.at[pl.ds(0, walks - 1)], 8)
    row = ring_in_us[0]
    for v in range(1, walks):
        row = row + ring_in_us[v]
    row_us[...] = row
    gather_us[slot] = row
    for k in range(2):
        kk = core if k == 0 else 1 - core
        for r in range(k ^ 1, chips):
            send(row_us, gather_us.at[slot], 10, chip_at(lax.rem(chip + r, chips), kk))

    settle(gring_in.at[pl.ds(0, walks - 1)], 7)
    gsum = gring_in[0]
    for v in range(1, walks):
        gsum = gsum + gring_in[v]
    geo_out_ref[...] = gsum

    settle(gather_p.at[pl.ds(0, 2 * chips - 1)], 9)
    for k in range(2):
        part = gather_p[k * chips].astype(F32)
        for c in range(1, chips):
            part = part + gather_p[k * chips + c].astype(F32)
        share_ref[1, :, pl.ds(k * lanes, lanes)] = part
    settle(gather_us.at[pl.ds(0, 2 * chips - 1)], 10)
    for n in range(2):
        for k in range(2):
            for c in range(chips):
                share_ref[2 * n, pl.ds(c, 1), pl.ds(k * lanes, lanes)] = gather_us[k * chips + c, pl.ds(n, 1), :]


def last_kernel(newf, df, share, geo, newf_out, df_out, gs_out, gp_out, gu_out, geo_out, sem):
    copies = [
        pltpu.make_async_copy(src, dst, sem.at[n])
        for n, (src, dst) in enumerate((
            (df, df_out), (newf, newf_out), (share.at[0], gs_out), (share.at[1], gp_out), (share.at[2], gu_out), (geo, geo_out),
        ))
    ]
    for c in copies:
        c.start()
    for c in copies:
        c.wait()


def vmem(n):
    return [pl.BlockSpec(memory_space=pltpu.VMEM)] * n


def hbm(n):
    return [pl.BlockSpec(memory_space=pltpu.HBM)] * n


def far(*arrays):
    return [pltpu.with_memory_space_constraint(x, pltpu.HBM) for x in arrays]


def body(sizes, features, w_self, w_pair, w_update, geo_embed, lattice, neighbours, counts, envelope, cotangent):
    slabs, walks, geoms = sizes
    feats, cot = features[0], cotangent[0]
    walkers, rows, width = feats.shape
    slots = neighbours.shape[3]
    lats = geo_embed.shape[1]
    wide = 2 * rows
    nbr = jnp.swapaxes(neighbours[0], 1, 2)
    env = jnp.swapaxes(envelope[0], 1, 2)
    sds = jax.ShapeDtypeStruct
    scr = pltpu.VMEM
    dma = pltpu.SemaphoreType.DMA
    rim = sds((walkers, RIM, width), BF16)
    before, after, weights, p, turn, slide, feats_v, inv, member = pl.pallas_call(
        functools.partial(first_kernel, slabs),
        out_shape=(
            rim,
            rim,
            sds((walkers, slots, rows), F32),
            sds((walkers * width, STEPS * rows), F32),
            sds((rows, STEPS * rows), BF16),
            sds((wide, len(BASES) * wide), BF16),
            sds((walkers, rows, width), BF16),
            sds((walkers, rows), F32),
            sds((walkers, lats, width), F32),
        ),
        in_specs=hbm(7),
        out_specs=vmem(9),
        scratch_shapes=[
            pltpu.SMEM((1, walkers), jnp.int32),
            scr((walkers, slots, rows), jnp.int32),
            scr((walkers, slots, rows), BF16),
            scr((walkers, rows), jnp.int32),
            scr((width, width), BF16),
            scr((lats, width), F32),
            scr((slots, rows), jnp.int32),
            scr((slots, rows), F32),
            dma((7,)),
            dma((2,)),
            dma((2,)),
        ],
        compiler_params=pltpu.CompilerParams(collective_id=0, has_side_effects=True, vmem_limit_bytes=12 * MIB),
        name="first",
    )(*far(lattice, feats, nbr, env, counts[0], w_self, geo_embed[0]))

    chips = slabs * geoms // 2
    lanes = width // 2
    share_rows = width // walks
    newf, df, share, geo = pl.pallas_call(
        functools.partial(main_kernel, slabs, walks, geoms),
        out_shape=(
            sds((walkers, rows, width), BF16),
            sds((walkers, rows, width), F32),
            sds((3, share_rows, width), F32),
            sds((lats, width), F32),
        ),
        in_specs=vmem(9) + hbm(4),
        out_specs=vmem(4),
        scratch_shapes=[
            scr((width, width), BF16),
            scr((width, width), BF16),
            scr((width, width), BF16),
            scr((walkers, rows, width), BF16),
            scr((walkers, wide, width), BF16),
            scr((walkers, width, wide), BF16),
            scr((walkers * width, len(BASES) * wide), F32),
            scr((slots, walkers * width, rows), F32),
            scr((walkers * width, STEPS * rows), BF16),
            scr((walkers * width, STEPS * rows), BF16),
            scr((walkers * width, STEPS * rows), F32),
            scr((walkers * width, len(BASES) * wide), BF16),
            scr((walkers, rows, width), F32),
            scr((2, walkers, RIM, width), BF16),
            scr((2, walkers, RIM, width), BF16),
            scr((3, width, width), F32),
            scr((2, width, lanes), F32),
            scr((width, lanes), BF16),
            scr((2, width, lanes), F32),
            scr((width, lanes), F32),
            scr((chips, 2, walks, lanes), BF16),
            scr((chips, 2, walks, lanes), BF16),
            scr((walks, 2, lanes), F32),
            scr((walks, 2, lanes), F32),
            scr((walks, share_rows, lanes), BF16),
            scr((walks, share_rows, lanes), BF16),
            scr((2, lanes), F32),
            scr((2 * chips, 2, lanes), F32),
            scr((share_rows, lanes), BF16),
            scr((2 * chips, share_rows, lanes), BF16),
            scr((lats, width), F32),
            scr((slabs, lats, width), F32),
            scr((lats, width), F32),
            scr((walks, lats, width), F32),
            dma((4,)),
            dma((11,)),
            dma((11,)),
        ],
        compiler_params=pltpu.CompilerParams(collective_id=1, has_side_effects=True, vmem_limit_bytes=44 * MIB),
        name="main",
    )(before, after, weights, p, turn, slide, feats_v, inv, member, *far(w_self, w_pair, w_update, cot))

    block = sds((share_rows, width), F32)
    newf, df, gs, gp, gu, geo = pl.pallas_call(
        last_kernel,
        out_shape=(
            sds((walkers, rows, width), BF16),
            sds((walkers, rows, width), F32),
            block,
            block,
            block,
            sds((lats, width), F32),
        ),
        in_specs=vmem(4),
        out_specs=hbm(6),
        scratch_shapes=[dma((6,))],
        compiler_params=pltpu.CompilerParams(vmem_limit_bytes=4 * MIB),
        name="last",
    )(newf, df, share, geo)
    return newf[None], df[None], gs, gp, gu, geo[None]


def solution(mesh):
    sizes = (mesh.shape["slab"], mesh.shape["walker"], mesh.shape["geom"])
    return jax.shard_map(
        functools.partial(body, sizes),
        mesh=mesh,
        in_specs=(
            P("geom", "walker", "slab", None),
            P(),
            P(),
            P(),
            P("geom", None, None),
            P("geom", "walker"),
            P("geom", "walker", "slab", None),
            P("geom", "walker", "slab"),
            P("geom", "walker", "slab", None),
            P("geom", "walker", "slab", None),
        ),
        out_specs=(
            P("geom", "walker", "slab", None),
            P("geom", "walker", "slab", None),
            P("walker", None),
            P("walker", None),
            P("walker", None),
            P("geom", None, None),
        ),
        check_vma=False,
    )
```

```python
import functools

import jax
import jax.numpy as jnp
from jax import lax
from jax.experimental import pallas as pl
from jax.experimental.pallas import tpu as pltpu
from jax.sharding import PartitionSpec as P

RIM = 32
F32 = jnp.float32
BF16 = jnp.bfloat16
MESH = pl.DeviceIdType.MESH
SLOTS = 2 * RIM
FGROUP = 4
BGROUP = 8
TILE = 32
MIB = 1024 * 1024
NN = ((1,), (0,))
NT = ((1,), (1,))


def dot(a, b, dims):
    return lax.dot_general(a, b, (dims, ((), ())), preferred_element_type=F32)


def at(**coords):
    return dict(device_id=coords, device_id_type=MESH)


def iota(shape, dim):
    return lax.broadcasted_iota(jnp.int32, shape, dim)


def window_matrix(slide_ref):
    wide, rows = slide_ref.shape[0], slide_ref.shape[1] // SLOTS
    gap = iota((wide, rows), 0) - iota((wide, rows), 1)

    def block(m, carry):
        off = m + jnp.where(m >= RIM, 1, 0)
        slide_ref[:, pl.ds(pl.multiple_of(m * rows, rows), rows)] = jnp.where(gap == off, 1.0, 0.0).astype(BF16)
        return carry

    lax.fori_loop(0, SLOTS, block, 0)


def slot_weights(nbr, env, count, off_ref, wt_ref):
    slots, rows = nbr.shape
    rel = nbr - iota((slots, rows), 1)
    off_ref[...] = rel - (rel > RIM).astype(jnp.int32)
    slot = iota((slots, rows), 0)
    wt_ref[...] = jnp.where(slot < count, env.astype(F32), 0.0)

    def place(step, acc):
        for u in range(8):
            k = step * 8 + u
            acc = acc + jnp.where(off_ref[pl.ds(k, 1), :] == slot, wt_ref[pl.ds(k, 1), :], 0.0)
        return acc

    return lax.fori_loop(0, slots // 8, place, jnp.zeros((slots, rows), F32))


def forward_pass(q_ref, p_ref, w_ref, slide_ref, h_ref, t_ref, agg_ref, tot_ref):
    total, rows = p_ref.shape
    width = total // w_ref.shape[0]
    groups = SLOTS // FGROUP
    agg_ref[...] = jnp.zeros(agg_ref.shape, F32)
    tot_ref[...] = jnp.zeros(tot_ref.shape, F32)

    def windows(g, at_slot):
        cols = pl.ds(pl.multiple_of(g * FGROUP * rows, FGROUP * rows), FGROUP * rows)
        h_ref[at_slot] = dot(q_ref[...], slide_ref[:, cols], NN)

    def work(g, at_slot):
        for r in range(0, total, TILE):
            here = slice(r, r + TILE)
            p = p_ref[here, :]
            ga = sa = None
            for x in range(FGROUP):
                h = h_ref[at_slot, here, x * rows : (x + 1) * rows] + p
                u = 1.0 + jnp.tanh(h)
                wu = u * w_ref[r // width, pl.ds(g * FGROUP + x, 1), :]
                wg = h * wu
                t = wu + wg * (2.0 - u)
                t_ref[g * FGROUP + x, here, :] = t
                ga = wg if x == 0 else ga + wg
                sa = t if x == 0 else sa + t
            agg_ref[here, :] += ga
            tot_ref[here, :] += sa

    windows(0, 0)

    def step(i, carry):
        windows(2 * i + 1, 1)
        work(2 * i, 0)
        windows(jnp.minimum(2 * i + 2, groups - 1), 0)
        work(2 * i + 1, 1)
        return carry

    lax.fori_loop(0, groups // 2, step, 0)


def backward_pass(first, count, d_ref, t_ref, slide_ref, v_ref, dqt_ref):
    total, rows = d_ref.shape

    def work(g, at_slot):
        for r in range(0, total, TILE):
            here = slice(r, r + TILE)
            d = d_ref[here, :]
            for x in range(BGROUP):
                v_ref[at_slot, here, x * rows : (x + 1) * rows] = (t_ref[g * BGROUP + x, here, :] * d).astype(BF16)

    def gather(g, at_slot):
        cols = pl.ds(pl.multiple_of(g * BGROUP * rows, BGROUP * rows), BGROUP * rows)
        dqt_ref[...] += dot(v_ref[at_slot], slide_ref[:, cols], NT)

    work(first, 0)

    def step(i, carry):
        g = first + 2 * i
        work(g + 1, 1)
        gather(g, 0)
        work(jnp.minimum(g + 2, first + count - 1), 0)
        gather(g + 1, 1)
        return carry

    lax.fori_loop(0, count // 2, step, 0)


def first_kernel(
    slabs, lat_hbm, feats_hbm, nbr_hbm, env_hbm, cnt_hbm, ws_hbm, geo_hbm,
    before_ref, after_ref, w_ref, p_ref, slide_ref, feats_ref, inv_ref, member_ref,
    lat_ref, nbr_ref, env_ref, cnt_ref, ws_ref, geo_ref, off_ref, wt_ref, load_sem, send_sem, recv_sem,
):
    me = lax.axis_index("slab")
    nxt, prv = lax.rem(me + 1, slabs), lax.rem(me + slabs - 1, slabs)
    barrier = pltpu.get_barrier_semaphore()
    pl.semaphore_signal(barrier, inc=1, **at(slab=nxt))
    pl.semaphore_signal(barrier, inc=1, **at(slab=prv))
    loads = []
    for n, (src, dst) in enumerate((
        (feats_hbm, feats_ref), (nbr_hbm, nbr_ref), (env_hbm, env_ref), (cnt_hbm, cnt_ref), (ws_hbm, ws_ref), (geo_hbm, geo_ref), (lat_hbm, lat_ref),
    )):
        loads.append(pltpu.make_async_copy(src, dst, load_sem.at[n]))
        loads[-1].start()
    walkers, rows, width = feats_ref.shape
    for c in loads:
        c.wait()
    pl.semaphore_wait(barrier, 2)
    up = pltpu.make_async_remote_copy(
        feats_ref.at[:, pl.ds(rows - RIM, RIM)], before_ref, send_sem.at[0], recv_sem.at[0], **at(slab=nxt)
    )
    down = pltpu.make_async_remote_copy(
        feats_ref.at[:, pl.ds(0, RIM)], after_ref, send_sem.at[1], recv_sem.at[1], **at(slab=prv)
    )
    up.start()
    down.start()
    window_matrix(slide_ref)
    geo = geo_ref[...]
    inv_ref[...] = 1.0 / cnt_ref[...].astype(F32)
    for w in range(walkers):
        w_ref[w] = slot_weights(nbr_ref[w], env_ref[w], cnt_ref[pl.ds(w, 1), :], off_ref, wt_ref)
        lats = geo.shape[0]
        member = (iota((lats, width), 0) == lat_ref[0, w]).astype(F32)
        member_ref[w] = member
        row = jnp.sum(jnp.where(member > 0.0, geo, 0.0), axis=0, keepdims=True)
        p = 0.5 * (dot(feats_ref[w], ws_ref[...], NN) + row)
        p_ref[w * width : (w + 1) * width, :] = p.T
    up.wait()
    down.wait()


def main_kernel(
    slabs, walks, geoms,
    before_ref, after_ref, w_ref, p_ref, slide_ref, feats_ref, inv_ref, member_ref, ws_hbm, wp_hbm, wu_hbm, cot_hbm,
    newf_ref, df_ref, share_ref, geo_out_ref,
    ws_ref, wp_ref, wu_ref, cot_ref, ext_ref, ext_t_ref, q_ref, h_ref, t_ref, agg_ref, tot_ref, d_ref, v_ref, dqt_ref, upd_ref, dp_ref, own_ref,
    rim_out, rim_in, grads_ref, half_us, half_p,
    core_in_us, core_in_p, plane_out, plane_in, ring_out_us, ring_in_us, ring_out_p, ring_in_p,
    row_us, gather_us, row_p, gather_p, gslab_out, gslab_in, gring_out, gring_in,
    load_sem, send_sem, recv_sem,
):
    slab, z, geom = lax.axis_index("slab"), lax.axis_index("walker"), lax.axis_index("geom")
    core = lax.rem(geom, 2)
    pair = geom - core
    half_geoms = geoms // 2
    chips = slabs * half_geoms
    chip = slab * half_geoms + pair // 2
    nxt, prv = lax.rem(slab + 1, slabs), lax.rem(slab + slabs - 1, slabs)
    walkers, rows, width = feats_ref.shape
    lanes = width // 2
    lats = gslab_out.shape[0]
    groups = SLOTS // BGROUP

    def chip_at(c, k):
        return at(slab=c // half_geoms, geom=lax.rem(c, half_geoms) * 2 + k)

    barrier = pltpu.get_barrier_semaphore()
    for k in range(2):
        kk = core if k == 0 else 1 - core
        for r in range(k ^ 1, chips):
            pl.semaphore_signal(barrier, inc=1, **chip_at(lax.rem(chip + r, chips), kk))
    for r in range(1, walks):
        pl.semaphore_signal(barrier, inc=1, **at(walker=lax.rem(z + r, walks)))

    def send(src, dst, n, where):
        c = pltpu.make_async_remote_copy(src, dst, send_sem.at[n], recv_sem.at[n], **where)
        c.start()
        return c

    def settle(ref, n):
        c = pltpu.make_async_remote_copy(ref, ref, send_sem.at[n], recv_sem.at[n], **at(slab=nxt))
        c.wait_send()
        c.wait_recv()

    loads = []
    for n, (src, dst) in enumerate(((wp_hbm, wp_ref), (wu_hbm, wu_ref), (cot_hbm, cot_ref), (ws_hbm, ws_ref))):
        loads.append(pltpu.make_async_copy(src, dst, load_sem.at[n]))
        loads[-1].start()

    wide = ext_ref.shape[1]
    for w in range(walkers):
        ext_ref[w, pl.ds(0, RIM), :] = before_ref[w]
        ext_ref[w, pl.ds(RIM, rows), :] = feats_ref[w]
        ext_ref[w, pl.ds(RIM + rows, RIM), :] = after_ref[w]
        ext_ref[w, pl.ds(2 * RIM + rows, wide - rows - 2 * RIM), :] = jnp.zeros((wide - rows - 2 * RIM, width), BF16)
    for c in loads:
        c.wait()
    for w in range(walkers):
        q = (0.5 * dot(ext_ref[w], wp_ref[...], NN)).astype(BF16)
        ext_t_ref[w] = ext_ref[w].T
        q_ref[w * width : (w + 1) * width, :] = q.T

    forward_pass(q_ref, p_ref, w_ref, slide_ref, h_ref, t_ref, agg_ref, tot_ref)

    dgeo = jnp.zeros((lats, width), F32)
    for w in range(walkers):
        part = slice(w * width, (w + 1) * width)
        inv = inv_ref[pl.ds(w, 1), :]
        agg_t = (agg_ref[part, :] * inv).astype(BF16)
        upd = dot(agg_t.T, wu_ref[...], NN)
        sig = 0.5 + 0.5 * jnp.tanh(0.5 * upd)
        upd_ref[w] = upd * sig
        du = (cot_ref[w].astype(F32) * (sig * (1.0 + upd * (1.0 - sig)))).astype(BF16)
        dd = 0.5 * dot(wu_ref[...], du, NT) * inv
        d_ref[part, :] = dd
        dp = (dd * tot_ref[part, :]).T
        dgeo = dgeo + jnp.where(member_ref[w] > 0.0, jnp.sum(dp, axis=0, keepdims=True), 0.0)
        dp = dp.astype(BF16)
        dp_ref[w] = dp
        feats_t = feats_ref[w].T
        for n, term in enumerate((dot(feats_t, dp, NN), dot(agg_t, du, NN))):
            grads_ref[n] = term if w == 0 else grads_ref[n] + term
    gslab_out[...] = dgeo
    dqt_ref[...] = jnp.zeros(dqt_ref.shape, F32)

    mine = pl.ds(pl.multiple_of(core * lanes, lanes), lanes)
    theirs = pl.ds(pl.multiple_of((1 - core) * lanes, lanes), lanes)
    pl.semaphore_wait(barrier, 2 * chips - 1 + walks - 1)
    cross = send(grads_ref.at[pl.ds(0, 2), :, theirs], core_in_us, 0, at(geom=pair + 1 - core))
    gslab_in[slab] = gslab_out[...]
    for r in range(1, slabs):
        send(gslab_out, gslab_in.at[slab], 1, at(slab=lax.rem(slab + r, slabs)))

    backward_pass(0, groups // 2, d_ref, t_ref, slide_ref, v_ref, dqt_ref)

    cross.wait()
    half_us[...] = grads_ref[pl.ds(0, 2), :, mine] + core_in_us[...]
    for c in range(chips):
        for n in range(2):
            plane_out[c, n] = half_us[n, pl.ds(c, walks, stride=chips), :].astype(BF16)
    plane_in[chip] = plane_out[chip]
    for r in range(1, chips):
        to = lax.rem(chip + r, chips)
        send(plane_out.at[to], plane_in.at[chip], 2, chip_at(to, core))

    backward_pass(groups // 2, groups // 2, d_ref, t_ref, slide_ref, v_ref, dqt_ref)

    settle(gslab_in.at[pl.ds(0, slabs - 1)], 1)
    gsum = gslab_in[0]
    for s in range(1, slabs):
        gsum = gsum + gslab_in[s]
    gring_out[...] = gsum
    gring_in[z] = gsum
    for r in range(1, walks):
        send(gring_out, gring_in.at[z], 7, at(walker=lax.rem(z + r, walks)))

    for w in range(walkers):
        dq = dqt_ref[w * width : (w + 1) * width, :].T
        own_ref[w] = dq[RIM : RIM + rows]
        dqb = dq.astype(BF16)
        rim_out[0, w] = dqb[:RIM]
        rim_out[1, w] = dqb[RIM + rows : 2 * RIM + rows]
        term = dot(ext_t_ref[w], dqb, NN)
        grads_ref[2] = term if w == 0 else grads_ref[2] + term
    cross = send(grads_ref.at[2, :, theirs], core_in_p, 3, at(geom=pair + 1 - core))
    down = send(rim_out.at[0], rim_in.at[0], 4, at(slab=prv))
    up = send(rim_out.at[1], rim_in.at[1], 5, at(slab=nxt))
    cross.wait()
    half_p[...] = (grads_ref[2, :, mine] + core_in_p[...]).astype(BF16)
    for v in range(walks):
        ring_out_p[v] = half_p[pl.ds(v * (width // walks), width // walks), :]
    ring_in_p[z] = ring_out_p[z]
    for r in range(1, walks):
        to = lax.rem(z + r, walks)
        send(ring_out_p.at[to], ring_in_p.at[z], 6, at(walker=to))

    for w in range(walkers):
        newf_ref[w] = (feats_ref[w].astype(F32) + upd_ref[w]).astype(BF16)
        df_ref[w] = cot_ref[w].astype(F32) + dot(dp_ref[w], ws_ref[...], NT)

    settle(plane_in.at[pl.ds(0, chips - 1)], 2)
    part = plane_in[0].astype(F32)
    for c in range(1, chips):
        part = part + plane_in[c].astype(F32)
    for v in range(walks):
        for n in range(2):
            ring_out_us[v, pl.ds(n, 1), :] = part[n, v : v + 1, :]
    ring_in_us[z] = ring_out_us[z]
    for r in range(1, walks):
        to = lax.rem(z + r, walks)
        send(ring_out_us.at[to], ring_in_us.at[z], 8, at(walker=to))

    down.wait()
    up.wait()
    for w in range(walkers):
        dq = jnp.concatenate(
            (
                own_ref[w, pl.ds(0, RIM), :] + rim_in[1, w].astype(F32),
                own_ref[w, pl.ds(RIM, rows - 2 * RIM), :],
                own_ref[w, pl.ds(rows - RIM, RIM), :] + rim_in[0, w].astype(F32),
            ),
            axis=0,
        ).astype(BF16)
        df_ref[w] = df_ref[w] + dot(dq, wp_ref[...], NT)

    slot = core * chips + chip
    settle(ring_in_p.at[pl.ds(0, walks - 1)], 6)
    part = ring_in_p[0].astype(F32)
    for v in range(1, walks):
        part = part + ring_in_p[v].astype(F32)
    row_p[...] = part.astype(BF16)
    gather_p[slot] = row_p[...]
    for k in range(2):
        kk = core if k == 0 else 1 - core
        for r in range(k ^ 1, chips):
            send(row_p, gather_p.at[slot], 9, chip_at(lax.rem(chip + r, chips), kk))

    settle(ring_in_us.at[pl.ds(0, walks - 1)], 8)
    row = ring_in_us[0]
    for v in range(1, walks):
        row = row + ring_in_us[v]
    row_us[...] = row
    gather_us[slot] = row
    for k in range(2):
        kk = core if k == 0 else 1 - core
        for r in range(k ^ 1, chips):
            send(row_us, gather_us.at[slot], 10, chip_at(lax.rem(chip + r, chips), kk))

    settle(gring_in.at[pl.ds(0, walks - 1)], 7)
    gsum = gring_in[0]
    for v in range(1, walks):
        gsum = gsum + gring_in[v]
    geo_out_ref[...] = gsum

    settle(gather_p.at[pl.ds(0, 2 * chips - 1)], 9)
    for k in range(2):
        part = gather_p[k * chips].astype(F32)
        for c in range(1, chips):
            part = part + gather_p[k * chips + c].astype(F32)
        share_ref[1, :, pl.ds(k * lanes, lanes)] = part
    settle(gather_us.at[pl.ds(0, 2 * chips - 1)], 10)
    for n in range(2):
        for k in range(2):
            for c in range(chips):
                share_ref[2 * n, pl.ds(c, 1), pl.ds(k * lanes, lanes)] = gather_us[k * chips + c, pl.ds(n, 1), :]


def last_kernel(newf, df, share, geo, newf_out, df_out, gs_out, gp_out, gu_out, geo_out, sem):
    copies = [
        pltpu.make_async_copy(src, dst, sem.at[n])
        for n, (src, dst) in enumerate((
            (df, df_out), (newf, newf_out), (share.at[0], gs_out), (share.at[1], gp_out), (share.at[2], gu_out), (geo, geo_out),
        ))
    ]
    for c in copies:
        c.start()
    for c in copies:
        c.wait()


def vmem(n):
    return [pl.BlockSpec(memory_space=pltpu.VMEM)] * n


def hbm(n):
    return [pl.BlockSpec(memory_space=pltpu.HBM)] * n


def far(*arrays):
    return [pltpu.with_memory_space_constraint(x, pltpu.HBM) for x in arrays]


def body(sizes, features, w_self, w_pair, w_update, geo_embed, lattice, neighbours, counts, envelope, cotangent):
    slabs, walks, geoms = sizes
    feats, cot = features[0], cotangent[0]
    walkers, rows, width = feats.shape
    slots = neighbours.shape[3]
    lats = geo_embed.shape[1]
    wide = 2 * rows
    nbr = jnp.swapaxes(neighbours[0], 1, 2)
    env = jnp.swapaxes(envelope[0], 1, 2)
    sds = jax.ShapeDtypeStruct
    scr = pltpu.VMEM
    dma = pltpu.SemaphoreType.DMA
    rim = sds((walkers, RIM, width), BF16)
    before, after, weights, p, slide, feats_v, inv, member = pl.pallas_call(
        functools.partial(first_kernel, slabs),
        out_shape=(
            rim,
            rim,
            sds((walkers, slots, rows), F32),
            sds((walkers * width, rows), F32),
            sds((wide, SLOTS * rows), BF16),
            sds((walkers, rows, width), BF16),
            sds((walkers, rows), F32),
            sds((walkers, lats, width), F32),
        ),
        in_specs=hbm(7),
        out_specs=vmem(8),
        scratch_shapes=[
            pltpu.SMEM((1, walkers), jnp.int32),
            scr((walkers, slots, rows), jnp.int32),
            scr((walkers, slots, rows), BF16),
            scr((walkers, rows), jnp.int32),
            scr((width, width), BF16),
            scr((lats, width), F32),
            scr((slots, rows), jnp.int32),
            scr((slots, rows), F32),
            dma((7,)),
            dma((2,)),
            dma((2,)),
        ],
        compiler_params=pltpu.CompilerParams(collective_id=0, has_side_effects=True, vmem_limit_bytes=12 * MIB),
        name="first",
    )(*far(lattice, feats, nbr, env, counts[0], w_self, geo_embed[0]))

    chips = slabs * geoms // 2
    lanes = width // 2
    share_rows = width // walks
    newf, df, share, geo = pl.pallas_call(
        functools.partial(main_kernel, slabs, walks, geoms),
        out_shape=(
            sds((walkers, rows, width), BF16),
            sds((walkers, rows, width), F32),
            sds((3, share_rows, width), F32),
            sds((lats, width), F32),
        ),
        in_specs=vmem(8) + hbm(4),
        out_specs=vmem(4),
        scratch_shapes=[
            scr((width, width), BF16),
            scr((width, width), BF16),
            scr((width, width), BF16),
            scr((walkers, rows, width), BF16),
            scr((walkers, wide, width), BF16),
            scr((walkers, width, wide), BF16),
            scr((walkers * width, wide), BF16),
            scr((2, walkers * width, FGROUP * rows), F32),
            scr((slots, walkers * width, rows), F32),
            scr((walkers * width, rows), F32),
            scr((walkers * width, rows), F32),
            scr((walkers * width, rows), F32),
            scr((2, walkers * width, BGROUP * rows), BF16),
            scr((walkers * width, wide), F32),
            scr((walkers, rows, width), F32),
            scr((walkers, rows, width), BF16),
            scr((walkers, rows, width), F32),
            scr((2, walkers, RIM, width), BF16),
            scr((2, walkers, RIM, width), BF16),
            scr((3, width, width), F32),
            scr((2, width, lanes), F32),
            scr((width, lanes), BF16),
            scr((2, width, lanes), F32),
            scr((width, lanes), F32),
            scr((chips, 2, walks, lanes), BF16),
            scr((chips, 2, walks, lanes), BF16),
            scr((walks, 2, lanes), F32),
            scr((walks, 2, lanes), F32),
            scr((walks, share_rows, lanes), BF16),
            scr((walks, share_rows, lanes), BF16),
            scr((2, lanes), F32),
            scr((2 * chips, 2, lanes), F32),
            scr((share_rows, lanes), BF16),
            scr((2 * chips, share_rows, lanes), BF16),
            scr((lats, width), F32),
            scr((slabs, lats, width), F32),
            scr((lats, width), F32),
            scr((walks, lats, width), F32),
            dma((4,)),
            dma((11,)),
            dma((11,)),
        ],
        compiler_params=pltpu.CompilerParams(collective_id=1, has_side_effects=True, vmem_limit_bytes=44 * MIB),
        name="main",
    )(before, after, weights, p, slide, feats_v, inv, member, *far(w_self, w_pair, w_update, cot))

    block = sds((share_rows, width), F32)
    newf, df, gs, gp, gu, geo = pl.pallas_call(
        last_kernel,
        out_shape=(
            sds((walkers, rows, width), BF16),
            sds((walkers, rows, width), F32),
            block,
            block,
            block,
            sds((lats, width), F32),
        ),
        in_specs=vmem(4),
        out_specs=hbm(6),
        scratch_shapes=[dma((6,))],
        compiler_params=pltpu.CompilerParams(vmem_limit_bytes=4 * MIB),
        name="last",
    )(newf, df, share, geo)
    return newf[None], df[None], gs, gp, gu, geo[None]


def solution(mesh):
    sizes = (mesh.shape["slab"], mesh.shape["walker"], mesh.shape["geom"])
    return jax.shard_map(
        functools.partial(body, sizes),
        mesh=mesh,
        in_specs=(
            P("geom", "walker", "slab", None),
            P(),
            P(),
            P(),
            P("geom", None, None),
            P("geom", "walker"),
            P("geom", "walker", "slab", None),
            P("geom", "walker", "slab"),
            P("geom", "walker", "slab", None),
            P("geom", "walker", "slab", None),
        ),
        out_specs=(
            P("geom", "walker", "slab", None),
            P("geom", "walker", "slab", None),
            P("walker", None),
            P("walker", None),
            P("walker", None),
            P("geom", None, None),
        ),
        check_vma=False,
    )
```

```python
import functools

import jax
import jax.numpy as jnp
from jax import lax
from jax.experimental import pallas as pl
from jax.experimental.pallas import tpu as pltpu
from jax.sharding import PartitionSpec as P

RIM = 32
F32 = jnp.float32
BF16 = jnp.bfloat16
MESH = pl.DeviceIdType.MESH
SLOTS = 2 * RIM
FGROUP = 4
BGROUP = 8
TILE = 32
MIB = 1024 * 1024
NN = ((1,), (0,))
NT = ((1,), (1,))


def dot(a, b, dims):
    return lax.dot_general(a, b, (dims, ((), ())), preferred_element_type=F32)


def at(**coords):
    return dict(device_id=coords, device_id_type=MESH)


def iota(shape, dim):
    return lax.broadcasted_iota(jnp.int32, shape, dim)


def window_matrix(slide_ref):
    wide, rows = slide_ref.shape[0], slide_ref.shape[1] // SLOTS
    gap = iota((wide, rows), 0) - iota((wide, rows), 1)

    def block(m, carry):
        off = m + jnp.where(m >= RIM, 1, 0)
        slide_ref[:, pl.ds(pl.multiple_of(m * rows, rows), rows)] = jnp.where(gap == off, 1.0, 0.0).astype(BF16)
        return carry

    lax.fori_loop(0, SLOTS, block, 0)


def slot_weights(nbr, env, count, off_ref, wt_ref):
    slots, rows = nbr.shape
    rel = nbr - iota((slots, rows), 1)
    off_ref[...] = rel - (rel > RIM).astype(jnp.int32)
    slot = iota((slots, rows), 0)
    wt_ref[...] = jnp.where(slot < count, env.astype(F32), 0.0)

    def place(step, acc):
        for u in range(8):
            k = step * 8 + u
            acc = acc + jnp.where(off_ref[pl.ds(k, 1), :] == slot, wt_ref[pl.ds(k, 1), :], 0.0)
        return acc

    return lax.fori_loop(0, slots // 8, place, jnp.zeros((slots, rows), F32))


def forward_pass(q_ref, p_ref, w_ref, slide_ref, h_ref, t_ref, agg_ref, tot_ref):
    total, rows = p_ref.shape
    width = total // w_ref.shape[0]
    groups = SLOTS // FGROUP
    agg_ref[...] = jnp.zeros(agg_ref.shape, F32)
    tot_ref[...] = jnp.zeros(tot_ref.shape, F32)

    def windows(g, at_slot):
        cols = pl.ds(pl.multiple_of(g * FGROUP * rows, FGROUP * rows), FGROUP * rows)
        h_ref[at_slot] = dot(q_ref[...], slide_ref[:, cols], NN)

    def work(g, at_slot):
        for r in range(0, total, TILE):
            here = slice(r, r + TILE)
            p = p_ref[here, :]
            ga = sa = None
            for x in range(FGROUP):
                h = h_ref[at_slot, here, x * rows : (x + 1) * rows] + p
                u = 1.0 + jnp.tanh(h)
                wu = u * w_ref[r // width, pl.ds(g * FGROUP + x, 1), :]
                wg = h * wu
                t = wu + wg * (2.0 - u)
                t_ref[g * FGROUP + x, here, :] = t
                ga = wg if x == 0 else ga + wg
                sa = t if x == 0 else sa + t
            agg_ref[here, :] += ga
            tot_ref[here, :] += sa

    windows(0, 0)

    def step(i, carry):
        windows(2 * i + 1, 1)
        work(2 * i, 0)
        windows(jnp.minimum(2 * i + 2, groups - 1), 0)
        work(2 * i + 1, 1)
        return carry

    lax.fori_loop(0, groups // 2, step, 0)


def backward_pass(part, first, count, d_ref, t_ref, slide_ref, v_ref, dqt_ref):
    rows = d_ref.shape[1]
    lanes = dqt_ref.shape[1] // 2
    width = 2 * lanes

    def work(g, at_slot):
        for w in range(2):
            for r in range(0, lanes, TILE):
                here = slice(w * width + part * lanes + r, w * width + part * lanes + r + TILE)
                there = slice(w * lanes + r, w * lanes + r + TILE)
                d = d_ref[here, :]
                for x in range(BGROUP):
                    v_ref[at_slot, there, x * rows : (x + 1) * rows] = (t_ref[g * BGROUP + x, here, :] * d).astype(BF16)

    def gather(g, at_slot):
        cols = pl.ds(pl.multiple_of(g * BGROUP * rows, BGROUP * rows), BGROUP * rows)
        dqt_ref[part] += dot(v_ref[at_slot], slide_ref[:, cols], NT)

    work(first, 0)

    def step(i, carry):
        g = first + 2 * i
        work(g + 1, 1)
        gather(g, 0)
        work(jnp.minimum(g + 2, first + count - 1), 0)
        gather(g + 1, 1)
        return carry

    lax.fori_loop(0, count // 2, step, 0)


def first_kernel(
    slabs, lat_hbm, feats_hbm, nbr_hbm, env_hbm, cnt_hbm, ws_hbm, geo_hbm,
    before_ref, after_ref, w_ref, p_ref, slide_ref, feats_ref, inv_ref, member_ref,
    lat_ref, nbr_ref, env_ref, cnt_ref, ws_ref, geo_ref, off_ref, wt_ref, load_sem, send_sem, recv_sem,
):
    me = lax.axis_index("slab")
    nxt, prv = lax.rem(me + 1, slabs), lax.rem(me + slabs - 1, slabs)
    barrier = pltpu.get_barrier_semaphore()
    pl.semaphore_signal(barrier, inc=1, **at(slab=nxt))
    pl.semaphore_signal(barrier, inc=1, **at(slab=prv))
    loads = []
    for n, (src, dst) in enumerate((
        (feats_hbm, feats_ref), (nbr_hbm, nbr_ref), (env_hbm, env_ref), (cnt_hbm, cnt_ref), (ws_hbm, ws_ref), (geo_hbm, geo_ref), (lat_hbm, lat_ref),
    )):
        loads.append(pltpu.make_async_copy(src, dst, load_sem.at[n]))
        loads[-1].start()
    walkers, rows, width = feats_ref.shape
    for c in loads:
        c.wait()
    pl.semaphore_wait(barrier, 2)
    up = pltpu.make_async_remote_copy(
        feats_ref.at[:, pl.ds(rows - RIM, RIM)], before_ref, send_sem.at[0], recv_sem.at[0], **at(slab=nxt)
    )
    down = pltpu.make_async_remote_copy(
        feats_ref.at[:, pl.ds(0, RIM)], after_ref, send_sem.at[1], recv_sem.at[1], **at(slab=prv)
    )
    up.start()
    down.start()
    window_matrix(slide_ref)
    geo = geo_ref[...]
    inv_ref[...] = 1.0 / cnt_ref[...].astype(F32)
    for w in range(walkers):
        w_ref[w] = slot_weights(nbr_ref[w], env_ref[w], cnt_ref[pl.ds(w, 1), :], off_ref, wt_ref)
        lats = geo.shape[0]
        member = (iota((lats, width), 0) == lat_ref[0, w]).astype(F32)
        member_ref[w] = member
        row = jnp.sum(jnp.where(member > 0.0, geo, 0.0), axis=0, keepdims=True)
        p = 0.5 * (dot(feats_ref[w], ws_ref[...], NN) + row)
        p_ref[w * width : (w + 1) * width, :] = p.T
    up.wait()
    down.wait()


def main_kernel(
    slabs, walks, geoms,
    before_ref, after_ref, w_ref, p_ref, slide_ref, feats_ref, inv_ref, member_ref, ws_hbm, wp_hbm, wu_hbm, cot_hbm,
    newf_ref, df_ref, share_ref, geo_out_ref,
    ws_ref, wp_ref, wu_ref, cot_ref, ext_ref, ext_t_ref, q_ref, h_ref, t_ref, agg_ref, tot_ref, d_ref, v_ref, dqt_ref, upd_ref, dp_ref, own_ref,
    rim_out, rim_in, grads_ref, half_us, pair_ref,
    core_in_us, core_in_p, plane_out, plane_in, ring_out_us, ring_in_us, ring_out_p, ring_in_p,
    row_us, gather_us, row_p, gather_p, gslab_out, gslab_in, gring_out, gring_in,
    load_sem, send_sem, recv_sem,
):
    slab, z, geom = lax.axis_index("slab"), lax.axis_index("walker"), lax.axis_index("geom")
    core = lax.rem(geom, 2)
    pair = geom - core
    half_geoms = geoms // 2
    chips = slabs * half_geoms
    chip = slab * half_geoms + pair // 2
    nxt, prv = lax.rem(slab + 1, slabs), lax.rem(slab + slabs - 1, slabs)
    walkers, rows, width = feats_ref.shape
    lanes = width // 2
    lats = gslab_out.shape[0]
    groups = SLOTS // BGROUP

    def chip_at(c, k):
        return at(slab=c // half_geoms, geom=lax.rem(c, half_geoms) * 2 + k)

    barrier = pltpu.get_barrier_semaphore()
    for k in range(2):
        kk = core if k == 0 else 1 - core
        for r in range(k ^ 1, chips):
            pl.semaphore_signal(barrier, inc=1, **chip_at(lax.rem(chip + r, chips), kk))
    for r in range(1, walks):
        pl.semaphore_signal(barrier, inc=1, **at(walker=lax.rem(z + r, walks)))

    def send(src, dst, n, where):
        c = pltpu.make_async_remote_copy(src, dst, send_sem.at[n], recv_sem.at[n], **where)
        c.start()
        return c

    def settle_send(ref, n):
        pltpu.make_async_remote_copy(ref, ref, send_sem.at[n], recv_sem.at[n], **at(slab=nxt)).wait_send()

    def settle_recv(ref, n):
        pltpu.make_async_remote_copy(ref, ref, send_sem.at[n], recv_sem.at[n], **at(slab=nxt)).wait_recv()

    def settle(ref, n):
        settle_send(ref, n)
        settle_recv(ref, n)

    loads = []
    for n, (src, dst) in enumerate(((wp_hbm, wp_ref), (wu_hbm, wu_ref), (cot_hbm, cot_ref), (ws_hbm, ws_ref))):
        loads.append(pltpu.make_async_copy(src, dst, load_sem.at[n]))
        loads[-1].start()

    wide = ext_ref.shape[1]
    for w in range(walkers):
        ext_ref[w, pl.ds(0, RIM), :] = before_ref[w]
        ext_ref[w, pl.ds(RIM, rows), :] = feats_ref[w]
        ext_ref[w, pl.ds(RIM + rows, RIM), :] = after_ref[w]
        ext_ref[w, pl.ds(2 * RIM + rows, wide - rows - 2 * RIM), :] = jnp.zeros((wide - rows - 2 * RIM, width), BF16)
    for c in loads:
        c.wait()
    for w in range(walkers):
        q = (0.5 * dot(ext_ref[w], wp_ref[...], NN)).astype(BF16)
        ext_t_ref[w] = ext_ref[w].T
        q_ref[w * width : (w + 1) * width, :] = q.T

    forward_pass(q_ref, p_ref, w_ref, slide_ref, h_ref, t_ref, agg_ref, tot_ref)

    dgeo = jnp.zeros((lats, width), F32)
    for w in range(walkers):
        part = slice(w * width, (w + 1) * width)
        inv = inv_ref[pl.ds(w, 1), :]
        agg_t = (agg_ref[part, :] * inv).astype(BF16)
        upd = dot(agg_t.T, wu_ref[...], NN)
        sig = 0.5 + 0.5 * jnp.tanh(0.5 * upd)
        upd_ref[w] = upd * sig
        du = (cot_ref[w].astype(F32) * (sig * (1.0 + upd * (1.0 - sig)))).astype(BF16)
        dd = 0.5 * dot(wu_ref[...], du, NT) * inv
        d_ref[part, :] = dd
        dp = (dd * tot_ref[part, :]).T
        dgeo = dgeo + jnp.where(member_ref[w] > 0.0, jnp.sum(dp, axis=0, keepdims=True), 0.0)
        dp = dp.astype(BF16)
        dp_ref[w] = dp
        feats_t = feats_ref[w].T
        for n, term in enumerate((dot(feats_t, dp, NN), dot(agg_t, du, NN))):
            grads_ref[n] = term if w == 0 else grads_ref[n] + term
    gslab_out[...] = dgeo
    dqt_ref[...] = jnp.zeros(dqt_ref.shape, F32)

    mine = pl.ds(pl.multiple_of(core * lanes, lanes), lanes)
    theirs = pl.ds(pl.multiple_of((1 - core) * lanes, lanes), lanes)
    pl.semaphore_wait(barrier, 2 * chips - 1 + walks - 1)
    cross = send(grads_ref.at[pl.ds(0, 2), :, theirs], core_in_us, 0, at(geom=pair + 1 - core))
    gslab_in[slab] = gslab_out[...]
    for r in range(1, slabs):
        send(gslab_out, gslab_in.at[slab], 1, at(slab=lax.rem(slab + r, slabs)))

    def pair_half(part):
        term = None
        for w in range(walkers):
            dq = dqt_ref[part, w * lanes : (w + 1) * lanes, :].T
            cols = slice(part * lanes, (part + 1) * lanes)
            own_ref[w, :, cols] = dq[RIM : RIM + rows]
            dqb = dq.astype(BF16)
            rim_out[0, w, :, cols] = dqb[:RIM]
            rim_out[1, w, :, cols] = dqb[RIM + rows : 2 * RIM + rows]
            more = dot(ext_t_ref[w], dqb, NN)
            term = more if w == 0 else term + more
        pair_ref[part] = term.reshape(pair_ref.shape[1:])
        return send(pair_ref.at[part, :, 1 - core], core_in_p.at[part], 3 + part, at(geom=pair + 1 - core))

    owner = lax.rem(z + core, 2) == 0
    zz = z // 2

    def ring_half(part, cross):
        cross.wait()
        ring_out_p[part] = (pair_ref[part, :, core] + core_in_p[part]).astype(BF16)

        @pl.when(owner)
        def _():
            ring_in_p[part, z] = ring_out_p[part, zz]

        @pl.when(jnp.logical_not(owner))
        def _():
            send(ring_out_p.at[part, zz], ring_in_p.at[part, z], 11 + part, at(walker=2 * zz + core))

        for r in range(1, walks // 2):
            to = lax.rem(zz + r, walks // 2)
            send(ring_out_p.at[part, to], ring_in_p.at[part, z], 11 + part, at(walker=2 * to + core))

    backward_pass(0, 0, groups, d_ref, t_ref, slide_ref, v_ref, dqt_ref)
    cross_p = pair_half(0)

    cross.wait()
    half_us[...] = grads_ref[pl.ds(0, 2), :, mine] + core_in_us[...]
    for c in range(chips):
        for n in range(2):
            plane_out[c, n] = half_us[n, pl.ds(c, walks, stride=chips), :].astype(BF16)
    plane_in[chip] = plane_out[chip]
    for r in range(1, chips):
        to = lax.rem(chip + r, chips)
        send(plane_out.at[to], plane_in.at[chip], 2, chip_at(to, core))

    backward_pass(1, 0, 2, d_ref, t_ref, slide_ref, v_ref, dqt_ref)
    ring_half(0, cross_p)
    settle(gslab_in.at[pl.ds(0, slabs - 1)], 1)
    gsum = gslab_in[0]
    for s in range(1, slabs):
        gsum = gsum + gslab_in[s]
    gring_out[...] = gsum
    gring_in[z] = gsum
    for r in range(1, walks):
        send(gring_out, gring_in.at[z], 7, at(walker=lax.rem(z + r, walks)))

    backward_pass(1, 2, groups - 2, d_ref, t_ref, slide_ref, v_ref, dqt_ref)
    cross_p = pair_half(1)
    down = send(rim_out.at[0], rim_in.at[0], 5, at(slab=prv))
    up = send(rim_out.at[1], rim_in.at[1], 6, at(slab=nxt))
    ring_half(1, cross_p)

    for w in range(walkers):
        newf_ref[w] = (feats_ref[w].astype(F32) + upd_ref[w]).astype(BF16)
        df_ref[w] = cot_ref[w].astype(F32) + dot(dp_ref[w], ws_ref[...], NT)

    settle(plane_in.at[pl.ds(0, chips - 1)], 2)
    part = plane_in[0].astype(F32)
    for c in range(1, chips):
        part = part + plane_in[c].astype(F32)
    for v in range(walks):
        for n in range(2):
            ring_out_us[v, pl.ds(n, 1), :] = part[n, v : v + 1, :]
    ring_in_us[z] = ring_out_us[z]
    for r in range(1, walks):
        to = lax.rem(z + r, walks)
        send(ring_out_us.at[to], ring_in_us.at[z], 8, at(walker=to))

    down.wait()
    up.wait()
    for w in range(walkers):
        dq = jnp.concatenate(
            (
                own_ref[w, pl.ds(0, RIM), :] + rim_in[1, w].astype(F32),
                own_ref[w, pl.ds(RIM, rows - 2 * RIM), :],
                own_ref[w, pl.ds(rows - RIM, RIM), :] + rim_in[0, w].astype(F32),
            ),
            axis=0,
        ).astype(BF16)
        df_ref[w] = df_ref[w] + dot(dq, wp_ref[...], NT)

    slot = core * chips + chip

    for part in range(2):

        @pl.when(jnp.logical_not(owner))
        def _():
            settle_send(ring_out_p.at[part], 11 + part)

        @pl.when(owner)
        def _():
            settle_send(ring_out_p.at[part, pl.ds(0, walks // 2 - 1)], 11 + part)
            settle_recv(ring_in_p.at[part, pl.ds(0, walks - 1)], 11 + part)
            total = ring_in_p[part, 0].astype(F32)
            for v in range(1, walks):
                total = total + ring_in_p[part, v].astype(F32)
            row_p[part] = total.astype(BF16)
            gather_p[part * chips + chip] = row_p[part]
            for k in range(2):
                kk = core if k == 0 else 1 - core
                for r in range(k ^ 1, chips):
                    send(row_p.at[part], gather_p.at[part * chips + chip], 13 + part, chip_at(lax.rem(chip + r, chips), kk))

    settle(ring_in_us.at[pl.ds(0, walks - 1)], 8)
    row = ring_in_us[0]
    for v in range(1, walks):
        row = row + ring_in_us[v]
    row_us[...] = row
    gather_us[slot] = row
    for k in range(2):
        kk = core if k == 0 else 1 - core
        for r in range(k ^ 1, chips):
            send(row_us, gather_us.at[slot], 10, chip_at(lax.rem(chip + r, chips), kk))

    settle(gring_in.at[pl.ds(0, walks - 1)], 7)
    gsum = gring_in[0]
    for v in range(1, walks):
        gsum = gsum + gring_in[v]
    geo_out_ref[...] = gsum

    for part in range(2):

        @pl.when(owner)
        def _():
            settle_recv(gather_p.at[pl.ds(0, chips - 1)], 13 + part)
            settle_send(gather_p.at[pl.ds(0, 2 * chips - 1)], 13 + part)

        @pl.when(jnp.logical_not(owner))
        def _():
            settle_recv(gather_p.at[pl.ds(0, chips)], 13 + part)

        total = gather_p[part * chips].astype(F32)
        for c in range(1, chips):
            total = total + gather_p[part * chips + c].astype(F32)
        share_ref[1, :, part * lanes : (part + 1) * lanes] = total
    settle(gather_us.at[pl.ds(0, 2 * chips - 1)], 10)
    for n in range(2):
        for k in range(2):
            for c in range(chips):
                share_ref[2 * n, pl.ds(c, 1), pl.ds(k * lanes, lanes)] = gather_us[k * chips + c, pl.ds(n, 1), :]


def last_kernel(newf, df, share, geo, newf_out, df_out, gs_out, gp_out, gu_out, geo_out, sem):
    copies = [
        pltpu.make_async_copy(src, dst, sem.at[n])
        for n, (src, dst) in enumerate((
            (df, df_out), (newf, newf_out), (share.at[0], gs_out), (share.at[1], gp_out), (share.at[2], gu_out), (geo, geo_out),
        ))
    ]
    for c in copies:
        c.start()
    for c in copies:
        c.wait()


def vmem(n):
    return [pl.BlockSpec(memory_space=pltpu.VMEM)] * n


def hbm(n):
    return [pl.BlockSpec(memory_space=pltpu.HBM)] * n


def far(*arrays):
    return [pltpu.with_memory_space_constraint(x, pltpu.HBM) for x in arrays]


def body(sizes, features, w_self, w_pair, w_update, geo_embed, lattice, neighbours, counts, envelope, cotangent):
    slabs, walks, geoms = sizes
    feats, cot = features[0], cotangent[0]
    walkers, rows, width = feats.shape
    slots = neighbours.shape[3]
    lats = geo_embed.shape[1]
    wide = 2 * rows
    nbr = jnp.swapaxes(neighbours[0], 1, 2)
    env = jnp.swapaxes(envelope[0], 1, 2)
    sds = jax.ShapeDtypeStruct
    scr = pltpu.VMEM
    dma = pltpu.SemaphoreType.DMA
    rim = sds((walkers, RIM, width), BF16)
    before, after, weights, p, slide, feats_v, inv, member = pl.pallas_call(
        functools.partial(first_kernel, slabs),
        out_shape=(
            rim,
            rim,
            sds((walkers, slots, rows), F32),
            sds((walkers * width, rows), F32),
            sds((wide, SLOTS * rows), BF16),
            sds((walkers, rows, width), BF16),
            sds((walkers, rows), F32),
            sds((walkers, lats, width), F32),
        ),
        in_specs=hbm(7),
        out_specs=vmem(8),
        scratch_shapes=[
            pltpu.SMEM((1, walkers), jnp.int32),
            scr((walkers, slots, rows), jnp.int32),
            scr((walkers, slots, rows), BF16),
            scr((walkers, rows), jnp.int32),
            scr((width, width), BF16),
            scr((lats, width), F32),
            scr((slots, rows), jnp.int32),
            scr((slots, rows), F32),
            dma((7,)),
            dma((2,)),
            dma((2,)),
        ],
        compiler_params=pltpu.CompilerParams(collective_id=0, has_side_effects=True, vmem_limit_bytes=12 * MIB),
        name="first",
    )(*far(lattice, feats, nbr, env, counts[0], w_self, geo_embed[0]))

    chips = slabs * geoms // 2
    lanes = width // 2
    share_rows = width // walks
    newf, df, share, geo = pl.pallas_call(
        functools.partial(main_kernel, slabs, walks, geoms),
        out_shape=(
            sds((walkers, rows, width), BF16),
            sds((walkers, rows, width), F32),
            sds((3, share_rows, width), F32),
            sds((lats, width), F32),
        ),
        in_specs=vmem(8) + hbm(4),
        out_specs=vmem(4),
        scratch_shapes=[
            scr((width, width), BF16),
            scr((width, width), BF16),
            scr((width, width), BF16),
            scr((walkers, rows, width), BF16),
            scr((walkers, wide, width), BF16),
            scr((walkers, width, wide), BF16),
            scr((walkers * width, wide), BF16),
            scr((2, walkers * width, FGROUP * rows), F32),
            scr((slots, walkers * width, rows), F32),
            scr((walkers * width, rows), F32),
            scr((walkers * width, rows), F32),
            scr((walkers * width, rows), F32),
            scr((2, width, BGROUP * rows), BF16),
            scr((2, width, wide), F32),
            scr((walkers, rows, width), F32),
            scr((walkers, rows, width), BF16),
            scr((walkers, rows, width), F32),
            scr((2, walkers, RIM, width), BF16),
            scr((2, walkers, RIM, width), BF16),
            scr((2, width, width), F32),
            scr((2, width, lanes), F32),
            scr((2, walks // 2, 2, share_rows, lanes), F32),
            scr((2, width, lanes), F32),
            scr((2, walks // 2, share_rows, lanes), F32),
            scr((chips, 2, walks, lanes), BF16),
            scr((chips, 2, walks, lanes), BF16),
            scr((walks, 2, lanes), F32),
            scr((walks, 2, lanes), F32),
            scr((2, walks // 2, share_rows, lanes), BF16),
            scr((2, walks, share_rows, lanes), BF16),
            scr((2, lanes), F32),
            scr((2 * chips, 2, lanes), F32),
            scr((2, share_rows, lanes), BF16),
            scr((2 * chips, share_rows, lanes), BF16),
            scr((lats, width), F32),
            scr((slabs, lats, width), F32),
            scr((lats, width), F32),
            scr((walks, lats, width), F32),
            dma((4,)),
            dma((15,)),
            dma((15,)),
        ],
        compiler_params=pltpu.CompilerParams(collective_id=1, has_side_effects=True, vmem_limit_bytes=44 * MIB),
        name="main",
    )(before, after, weights, p, slide, feats_v, inv, member, *far(w_self, w_pair, w_update, cot))

    block = sds((share_rows, width), F32)
    newf, df, gs, gp, gu, geo = pl.pallas_call(
        last_kernel,
        out_shape=(
            sds((walkers, rows, width), BF16),
            sds((walkers, rows, width), F32),
            block,
            block,
            block,
            sds((lats, width), F32),
        ),
        in_specs=vmem(4),
        out_specs=hbm(6),
        scratch_shapes=[dma((6,))],
        compiler_params=pltpu.CompilerParams(vmem_limit_bytes=4 * MIB),
        name="last",
    )(newf, df, share, geo)
    return newf[None], df[None], gs, gp, gu, geo[None]


def solution(mesh):
    sizes = (mesh.shape["slab"], mesh.shape["walker"], mesh.shape["geom"])
    return jax.shard_map(
        functools.partial(body, sizes),
        mesh=mesh,
        in_specs=(
            P("geom", "walker", "slab", None),
            P(),
            P(),
            P(),
            P("geom", None, None),
            P("geom", "walker"),
            P("geom", "walker", "slab", None),
            P("geom", "walker", "slab"),
            P("geom", "walker", "slab", None),
            P("geom", "walker", "slab", None),
        ),
        out_specs=(
            P("geom", "walker", "slab", None),
            P("geom", "walker", "slab", None),
            P("walker", None),
            P("walker", None),
            P("walker", None),
            P("geom", None, None),
        ),
        check_vma=False,
    )
```

```python
import functools

import jax
import jax.numpy as jnp
from jax import lax
from jax.experimental import pallas as pl
from jax.experimental.pallas import tpu as pltpu
from jax.sharding import PartitionSpec as P

RIM = 32
F32 = jnp.float32
BF16 = jnp.bfloat16
MESH = pl.DeviceIdType.MESH
SLOTS = 2 * RIM
FGROUP = 4
BGROUP = 8
TILE = 32
MIB = 1024 * 1024
NN = ((1,), (0,))
NT = ((1,), (1,))


def dot(a, b, dims):
    return lax.dot_general(a, b, (dims, ((), ())), preferred_element_type=F32)


def at(**coords):
    return dict(device_id=coords, device_id_type=MESH)


def iota(shape, dim):
    return lax.broadcasted_iota(jnp.int32, shape, dim)


def window_matrix(slide_ref):
    wide, rows = slide_ref.shape[0], slide_ref.shape[1] // SLOTS
    gap = iota((wide, rows), 0) - iota((wide, rows), 1)

    def block(m, carry):
        off = m + jnp.where(m >= RIM, 1, 0)
        slide_ref[:, pl.ds(pl.multiple_of(m * rows, rows), rows)] = jnp.where(gap == off, 1.0, 0.0).astype(BF16)
        return carry

    lax.fori_loop(0, SLOTS, block, 0)


def slot_weights(nbr, env, count, off_ref, wt_ref):
    slots, rows = nbr.shape
    rel = nbr - iota((slots, rows), 1)
    off_ref[...] = rel - (rel > RIM).astype(jnp.int32)
    slot = iota((slots, rows), 0)
    wt_ref[...] = jnp.where(slot < count, env.astype(F32), 0.0)

    def place(step, acc):
        for u in range(8):
            k = step * 8 + u
            acc = acc + jnp.where(off_ref[pl.ds(k, 1), :] == slot, wt_ref[pl.ds(k, 1), :], 0.0)
        return acc

    return lax.fori_loop(0, slots // 8, place, jnp.zeros((slots, rows), F32))


def forward_pass(q_ref, p_ref, w_ref, slide_ref, h_ref, t_ref, agg_ref, tot_ref):
    total, rows = p_ref.shape
    width = total // w_ref.shape[0]
    groups = SLOTS // FGROUP
    agg_ref[...] = jnp.zeros(agg_ref.shape, F32)
    tot_ref[...] = jnp.zeros(tot_ref.shape, F32)

    def windows(g, at_slot):
        cols = pl.ds(pl.multiple_of(g * FGROUP * rows, FGROUP * rows), FGROUP * rows)
        h_ref[at_slot] = dot(q_ref[...], slide_ref[:, cols], NN)

    def work(g, at_slot):
        for r in range(0, total, TILE):
            here = slice(r, r + TILE)
            p = p_ref[here, :]
            ga = sa = None
            for x in range(FGROUP):
                h = h_ref[at_slot, here, x * rows : (x + 1) * rows] + p
                u = 1.0 + jnp.tanh(h)
                wu = u * w_ref[r // width, pl.ds(g * FGROUP + x, 1), :]
                wg = h * wu
                t = wu + wg * (2.0 - u)
                t_ref[g * FGROUP + x, here, :] = t
                ga = wg if x == 0 else ga + wg
                sa = t if x == 0 else sa + t
            agg_ref[here, :] += ga
            tot_ref[here, :] += sa

    windows(0, 0)

    def step(i, carry):
        windows(2 * i + 1, 1)
        work(2 * i, 0)
        windows(jnp.minimum(2 * i + 2, groups - 1), 0)
        work(2 * i + 1, 1)
        return carry

    lax.fori_loop(0, groups // 2, step, 0)


def backward_pass(part, first, count, d_ref, t_ref, slide_ref, v_ref, dqt_ref):
    rows = d_ref.shape[1]
    lanes = dqt_ref.shape[1] // 2
    width = 2 * lanes

    def work(g, at_slot):
        for w in range(2):
            for r in range(0, lanes, TILE):
                here = slice(w * width + part * lanes + r, w * width + part * lanes + r + TILE)
                there = slice(w * lanes + r, w * lanes + r + TILE)
                d = d_ref[here, :]
                for x in range(BGROUP):
                    v_ref[at_slot, there, x * rows : (x + 1) * rows] = (t_ref[g * BGROUP + x, here, :] * d).astype(BF16)

    def gather(g, at_slot):
        cols = pl.ds(pl.multiple_of(g * BGROUP * rows, BGROUP * rows), BGROUP * rows)
        dqt_ref[part] += dot(v_ref[at_slot], slide_ref[:, cols], NT)

    work(first, 0)

    def step(i, carry):
        g = first + 2 * i
        work(g + 1, 1)
        gather(g, 0)
        work(jnp.minimum(g + 2, first + count - 1), 0)
        gather(g + 1, 1)
        return carry

    lax.fori_loop(0, count // 2, step, 0)


def first_kernel(
    slabs, lat_hbm, feats_hbm, nbr_hbm, env_hbm, cnt_hbm, ws_hbm, geo_hbm, wp_hbm,
    ext_ref, w_ref, p_ref, slide_ref, feats_ref, feats_t_ref, inv_ref, member_ref, wp_ref,
    lat_ref, nbr_ref, env_ref, cnt_ref, ws_ref, geo_ref, off_ref, wt_ref, load_sem, send_sem, recv_sem,
):
    me = lax.axis_index("slab")
    nxt, prv = lax.rem(me + 1, slabs), lax.rem(me + slabs - 1, slabs)
    barrier = pltpu.get_barrier_semaphore()
    pl.semaphore_signal(barrier, inc=1, **at(slab=nxt))
    pl.semaphore_signal(barrier, inc=1, **at(slab=prv))
    loads = []
    for n, (src, dst) in enumerate((
        (feats_hbm, feats_ref), (nbr_hbm, nbr_ref), (env_hbm, env_ref), (cnt_hbm, cnt_ref), (ws_hbm, ws_ref), (geo_hbm, geo_ref), (lat_hbm, lat_ref), (wp_hbm, wp_ref),
    )):
        loads.append(pltpu.make_async_copy(src, dst, load_sem.at[n]))
        loads[-1].start()
    walkers, rows, width = feats_ref.shape
    for c in loads:
        c.wait()
    pl.semaphore_wait(barrier, 2)
    up = pltpu.make_async_remote_copy(
        feats_ref.at[:, pl.ds(rows - RIM, RIM)], ext_ref.at[:, pl.ds(0, RIM)], send_sem.at[0], recv_sem.at[0], **at(slab=nxt)
    )
    down = pltpu.make_async_remote_copy(
        feats_ref.at[:, pl.ds(0, RIM)], ext_ref.at[:, pl.ds(rows + RIM, RIM)], send_sem.at[1], recv_sem.at[1], **at(slab=prv)
    )
    up.start()
    down.start()
    window_matrix(slide_ref)
    geo = geo_ref[...]
    inv_ref[...] = 1.0 / cnt_ref[...].astype(F32)
    for w in range(walkers):
        w_ref[w] = slot_weights(nbr_ref[w], env_ref[w], cnt_ref[pl.ds(w, 1), :], off_ref, wt_ref)
        lats = geo.shape[0]
        member = (iota((lats, width), 0) == lat_ref[0, w]).astype(F32)
        member_ref[w] = member
        row = jnp.sum(jnp.where(member > 0.0, geo, 0.0), axis=0, keepdims=True)
        p = 0.5 * (dot(feats_ref[w], ws_ref[...], NN) + row)
        p_ref[w * width : (w + 1) * width, :] = p.T
        feats_t_ref[w] = feats_ref[w].T
        ext_ref[w, pl.ds(RIM, rows), :] = feats_ref[w]
        pad = ext_ref.shape[1] - rows - 2 * RIM
        ext_ref[w, pl.ds(rows + 2 * RIM, pad), :] = jnp.zeros((pad, width), BF16)
    up.wait()
    down.wait()


def main_kernel(
    slabs, walks, geoms,
    ext_ref, w_ref, p_ref, slide_ref, feats_ref, feats_t_ref, inv_ref, member_ref, wp_ref, ws_hbm, wu_hbm, cot_hbm,
    newf_ref, df_ref, share_ref, geo_out_ref,
    ws_ref, wu_ref, cot_ref, q_ref, h_ref, t_ref, agg_ref, tot_ref, d_ref, v_ref, dqt_ref, upd_ref, dp_ref, own_ref,
    rim_out, rim_in, grads_ref, half_us, pair_ref,
    core_in_us, core_in_p, plane_out, plane_in, ring_out_us, ring_in_us, ring_out_p, ring_in_p,
    row_us, gather_us, row_p, gather_p, gslab_out, gslab_in, gring_out, gring_in,
    load_sem, send_sem, recv_sem,
):
    slab, z, geom = lax.axis_index("slab"), lax.axis_index("walker"), lax.axis_index("geom")
    core = lax.rem(geom, 2)
    pair = geom - core
    half_geoms = geoms // 2
    chips = slabs * half_geoms
    chip = slab * half_geoms + pair // 2
    nxt, prv = lax.rem(slab + 1, slabs), lax.rem(slab + slabs - 1, slabs)
    walkers, rows, width = feats_ref.shape
    lanes = width // 2
    lats = gslab_out.shape[0]
    groups = SLOTS // BGROUP

    def chip_at(c, k):
        return at(slab=c // half_geoms, geom=lax.rem(c, half_geoms) * 2 + k)

    barrier = pltpu.get_barrier_semaphore()
    for k in range(2):
        kk = core if k == 0 else 1 - core
        for r in range(k ^ 1, chips):
            pl.semaphore_signal(barrier, inc=1, **chip_at(lax.rem(chip + r, chips), kk))
    for r in range(1, walks):
        pl.semaphore_signal(barrier, inc=1, **at(walker=lax.rem(z + r, walks)))

    def send(src, dst, n, where):
        c = pltpu.make_async_remote_copy(src, dst, send_sem.at[n], recv_sem.at[n], **where)
        c.start()
        return c

    def settle_send(ref, n):
        pltpu.make_async_remote_copy(ref, ref, send_sem.at[n], recv_sem.at[n], **at(slab=nxt)).wait_send()

    def settle_recv(ref, n):
        pltpu.make_async_remote_copy(ref, ref, send_sem.at[n], recv_sem.at[n], **at(slab=nxt)).wait_recv()

    def settle(ref, n):
        settle_send(ref, n)
        settle_recv(ref, n)

    loads = []
    for n, (src, dst) in enumerate(((wu_hbm, wu_ref), (cot_hbm, cot_ref), (ws_hbm, ws_ref))):
        loads.append(pltpu.make_async_copy(src, dst, load_sem.at[n]))
        loads[-1].start()

    for w in range(walkers):
        q = (0.5 * dot(ext_ref[w], wp_ref[...], NN)).astype(BF16)
        q_ref[w * width : (w + 1) * width, :] = q.T

    forward_pass(q_ref, p_ref, w_ref, slide_ref, h_ref, t_ref, agg_ref, tot_ref)

    for c in loads:
        c.wait()
    dgeo = jnp.zeros((lats, width), F32)
    for w in range(walkers):
        part = slice(w * width, (w + 1) * width)
        inv = inv_ref[pl.ds(w, 1), :]
        agg_t = (agg_ref[part, :] * inv).astype(BF16)
        upd = dot(agg_t.T, wu_ref[...], NN)
        sig = 0.5 + 0.5 * jnp.tanh(0.5 * upd)
        upd_ref[w] = upd * sig
        du = (cot_ref[w].astype(F32) * (sig * (1.0 + upd * (1.0 - sig)))).astype(BF16)
        dd = 0.5 * dot(wu_ref[...], du, NT) * inv
        d_ref[part, :] = dd
        dp = (dd * tot_ref[part, :]).T
        dgeo = dgeo + jnp.where(member_ref[w] > 0.0, jnp.sum(dp, axis=0, keepdims=True), 0.0)
        dp = dp.astype(BF16)
        dp_ref[w] = dp
        for n, term in enumerate((dot(feats_t_ref[w], dp, NN), dot(agg_t, du, NN))):
            grads_ref[n] = term if w == 0 else grads_ref[n] + term
    gslab_out[...] = dgeo
    dqt_ref[...] = jnp.zeros(dqt_ref.shape, F32)

    mine = pl.ds(pl.multiple_of(core * lanes, lanes), lanes)
    theirs = pl.ds(pl.multiple_of((1 - core) * lanes, lanes), lanes)
    pl.semaphore_wait(barrier, 2 * chips - 1 + walks - 1)
    cross = send(grads_ref.at[pl.ds(0, 2), :, theirs], core_in_us, 0, at(geom=pair + 1 - core))
    gslab_in[slab] = gslab_out[...]
    for r in range(1, slabs):
        send(gslab_out, gslab_in.at[slab], 1, at(slab=lax.rem(slab + r, slabs)))

    def pair_half(part):
        term = None
        for w in range(walkers):
            dq = dqt_ref[part, w * lanes : (w + 1) * lanes, :].T
            cols = slice(part * lanes, (part + 1) * lanes)
            own_ref[w, :, cols] = dq[RIM : RIM + rows]
            dqb = dq.astype(BF16)
            rim_out[0, w, :, cols] = dqb[:RIM]
            rim_out[1, w, :, cols] = dqb[RIM + rows : 2 * RIM + rows]
            more = dot(ext_ref[w].T, dqb, NN)
            term = more if w == 0 else term + more
        pair_ref[part] = term.reshape(pair_ref.shape[1:])
        return send(pair_ref.at[part, :, 1 - core], core_in_p.at[part], 3 + part, at(geom=pair + 1 - core))

    owner = lax.rem(z + core, 2) == 0
    zz = z // 2

    def ring_half(part, cross):
        cross.wait()
        ring_out_p[part] = (pair_ref[part, :, core] + core_in_p[part]).astype(BF16)

        @pl.when(owner)
        def _():
            ring_in_p[part, z] = ring_out_p[part, zz]

        @pl.when(jnp.logical_not(owner))
        def _():
            send(ring_out_p.at[part, zz], ring_in_p.at[part, z], 11 + part, at(walker=2 * zz + core))

        for r in range(1, walks // 2):
            to = lax.rem(zz + r, walks // 2)
            send(ring_out_p.at[part, to], ring_in_p.at[part, z], 11 + part, at(walker=2 * to + core))

    backward_pass(0, 0, groups // 2, d_ref, t_ref, slide_ref, v_ref, dqt_ref)

    cross.wait()
    half_us[...] = grads_ref[pl.ds(0, 2), :, mine] + core_in_us[...]
    for c in range(chips):
        for n in range(2):
            plane_out[c, n] = half_us[n, pl.ds(c, walks, stride=chips), :].astype(BF16)
    plane_in[chip] = plane_out[chip]
    for r in range(1, chips):
        to = lax.rem(chip + r, chips)
        send(plane_out.at[to], plane_in.at[chip], 2, chip_at(to, core))

    backward_pass(0, groups // 2, groups // 2, d_ref, t_ref, slide_ref, v_ref, dqt_ref)
    cross_p = pair_half(0)
    backward_pass(1, 0, 2, d_ref, t_ref, slide_ref, v_ref, dqt_ref)
    ring_half(0, cross_p)
    settle(gslab_in.at[pl.ds(0, slabs - 1)], 1)
    gsum = gslab_in[0]
    for s in range(1, slabs):
        gsum = gsum + gslab_in[s]
    gring_out[...] = gsum
    gring_in[z] = gsum
    for r in range(1, walks):
        send(gring_out, gring_in.at[z], 7, at(walker=lax.rem(z + r, walks)))

    backward_pass(1, 2, groups - 2, d_ref, t_ref, slide_ref, v_ref, dqt_ref)
    cross_p = pair_half(1)
    down = send(rim_out.at[0], rim_in.at[0], 5, at(slab=prv))
    up = send(rim_out.at[1], rim_in.at[1], 6, at(slab=nxt))
    ring_half(1, cross_p)

    for w in range(walkers):
        newf_ref[w] = (feats_ref[w].astype(F32) + upd_ref[w]).astype(BF16)
        df_ref[w] = cot_ref[w].astype(F32) + dot(dp_ref[w], ws_ref[...], NT)

    settle(plane_in.at[pl.ds(0, chips - 1)], 2)
    part = plane_in[0].astype(F32)
    for c in range(1, chips):
        part = part + plane_in[c].astype(F32)
    for v in range(walks):
        for n in range(2):
            ring_out_us[v, pl.ds(n, 1), :] = part[n, v : v + 1, :]
    ring_in_us[z] = ring_out_us[z]
    for r in range(1, walks):
        to = lax.rem(z + r, walks)
        send(ring_out_us.at[to], ring_in_us.at[z], 8, at(walker=to))

    down.wait()
    up.wait()
    for w in range(walkers):
        dq = jnp.concatenate(
            (
                own_ref[w, pl.ds(0, RIM), :] + rim_in[1, w].astype(F32),
                own_ref[w, pl.ds(RIM, rows - 2 * RIM), :],
                own_ref[w, pl.ds(rows - RIM, RIM), :] + rim_in[0, w].astype(F32),
            ),
            axis=0,
        ).astype(BF16)
        df_ref[w] = df_ref[w] + dot(dq, wp_ref[...], NT)

    slot = core * chips + chip

    for part in range(2):

        @pl.when(jnp.logical_not(owner))
        def _():
            settle_send(ring_out_p.at[part], 11 + part)

        @pl.when(owner)
        def _():
            settle_send(ring_out_p.at[part, pl.ds(0, walks // 2 - 1)], 11 + part)
            settle_recv(ring_in_p.at[part, pl.ds(0, walks - 1)], 11 + part)
            total = ring_in_p[part, 0].astype(F32)
            for v in range(1, walks):
                total = total + ring_in_p[part, v].astype(F32)
            row_p[part] = total.astype(BF16)
            gather_p[part * chips + chip] = row_p[part]
            for k in range(2):
                kk = core if k == 0 else 1 - core
                for r in range(k ^ 1, chips):
                    send(row_p.at[part], gather_p.at[part * chips + chip], 13 + part, chip_at(lax.rem(chip + r, chips), kk))

    settle(ring_in_us.at[pl.ds(0, walks - 1)], 8)
    row = ring_in_us[0]
    for v in range(1, walks):
        row = row + ring_in_us[v]
    row_us[...] = row
    gather_us[slot] = row
    for k in range(2):
        kk = core if k == 0 else 1 - core
        for r in range(k ^ 1, chips):
            send(row_us, gather_us.at[slot], 10, chip_at(lax.rem(chip + r, chips), kk))

    settle(gring_in.at[pl.ds(0, walks - 1)], 7)
    gsum = gring_in[0]
    for v in range(1, walks):
        gsum = gsum + gring_in[v]
    geo_out_ref[...] = gsum

    for part in range(2):

        @pl.when(owner)
        def _():
            settle_recv(gather_p.at[pl.ds(0, chips - 1)], 13 + part)
            settle_send(gather_p.at[pl.ds(0, 2 * chips - 1)], 13 + part)

        @pl.when(jnp.logical_not(owner))
        def _():
            settle_recv(gather_p.at[pl.ds(0, chips)], 13 + part)

        total = gather_p[part * chips].astype(F32)
        for c in range(1, chips):
            total = total + gather_p[part * chips + c].astype(F32)
        share_ref[1, :, part * lanes : (part + 1) * lanes] = total
    settle(gather_us.at[pl.ds(0, 2 * chips - 1)], 10)
    for n in range(2):
        for k in range(2):
            for c in range(chips):
                share_ref[2 * n, pl.ds(c, 1), pl.ds(k * lanes, lanes)] = gather_us[k * chips + c, pl.ds(n, 1), :]


def last_kernel(newf, df, share, geo, newf_out, df_out, gs_out, gp_out, gu_out, geo_out, sem):
    copies = [
        pltpu.make_async_copy(src, dst, sem.at[n])
        for n, (src, dst) in enumerate((
            (df, df_out), (newf, newf_out), (share.at[0], gs_out), (share.at[1], gp_out), (share.at[2], gu_out), (geo, geo_out),
        ))
    ]
    for c in copies:
        c.start()
    for c in copies:
        c.wait()


def vmem(n):
    return [pl.BlockSpec(memory_space=pltpu.VMEM)] * n


def hbm(n):
    return [pl.BlockSpec(memory_space=pltpu.HBM)] * n


def far(*arrays):
    return [pltpu.with_memory_space_constraint(x, pltpu.HBM) for x in arrays]


def body(sizes, features, w_self, w_pair, w_update, geo_embed, lattice, neighbours, counts, envelope, cotangent):
    slabs, walks, geoms = sizes
    feats, cot = features[0], cotangent[0]
    walkers, rows, width = feats.shape
    slots = neighbours.shape[3]
    lats = geo_embed.shape[1]
    wide = 2 * rows
    nbr = jnp.swapaxes(neighbours[0], 1, 2)
    env = jnp.swapaxes(envelope[0], 1, 2)
    sds = jax.ShapeDtypeStruct
    scr = pltpu.VMEM
    dma = pltpu.SemaphoreType.DMA
    ext, weights, p, slide, feats_v, feats_t, inv, member, wp_v = pl.pallas_call(
        functools.partial(first_kernel, slabs),
        out_shape=(
            sds((walkers, wide, width), BF16),
            sds((walkers, slots, rows), F32),
            sds((walkers * width, rows), F32),
            sds((wide, SLOTS * rows), BF16),
            sds((walkers, rows, width), BF16),
            sds((walkers, width, rows), BF16),
            sds((walkers, rows), F32),
            sds((walkers, lats, width), F32),
            sds((width, width), BF16),
        ),
        in_specs=hbm(8),
        out_specs=vmem(9),
        scratch_shapes=[
            pltpu.SMEM((1, walkers), jnp.int32),
            scr((walkers, slots, rows), jnp.int32),
            scr((walkers, slots, rows), BF16),
            scr((walkers, rows), jnp.int32),
            scr((width, width), BF16),
            scr((lats, width), F32),
            scr((slots, rows), jnp.int32),
            scr((slots, rows), F32),
            dma((8,)),
            dma((2,)),
            dma((2,)),
        ],
        compiler_params=pltpu.CompilerParams(collective_id=0, has_side_effects=True, vmem_limit_bytes=12 * MIB),
        name="first",
    )(*far(lattice, feats, nbr, env, counts[0], w_self, geo_embed[0], w_pair))

    chips = slabs * geoms // 2
    lanes = width // 2
    share_rows = width // walks
    newf, df, share, geo = pl.pallas_call(
        functools.partial(main_kernel, slabs, walks, geoms),
        out_shape=(
            sds((walkers, rows, width), BF16),
            sds((walkers, rows, width), F32),
            sds((3, share_rows, width), F32),
            sds((lats, width), F32),
        ),
        in_specs=vmem(9) + hbm(3),
        out_specs=vmem(4),
        scratch_shapes=[
            scr((width, width), BF16),
            scr((width, width), BF16),
            scr((walkers, rows, width), BF16),
            scr((walkers * width, wide), BF16),
            scr((2, walkers * width, FGROUP * rows), F32),
            scr((slots, walkers * width, rows), F32),
            scr((walkers * width, rows), F32),
            scr((walkers * width, rows), F32),
            scr((walkers * width, rows), F32),
            scr((2, width, BGROUP * rows), BF16),
            scr((2, width, wide), F32),
            scr((walkers, rows, width), F32),
            scr((walkers, rows, width), BF16),
            scr((walkers, rows, width), F32),
            scr((2, walkers, RIM, width), BF16),
            scr((2, walkers, RIM, width), BF16),
            scr((2, width, width), F32),
            scr((2, width, lanes), F32),
            scr((2, walks // 2, 2, share_rows, lanes), F32),
            scr((2, width, lanes), F32),
            scr((2, walks // 2, share_rows, lanes), F32),
            scr((chips, 2, walks, lanes), BF16),
            scr((chips, 2, walks, lanes), BF16),
            scr((walks, 2, lanes), F32),
            scr((walks, 2, lanes), F32),
            scr((2, walks // 2, share_rows, lanes), BF16),
            scr((2, walks, share_rows, lanes), BF16),
            scr((2, lanes), F32),
            scr((2 * chips, 2, lanes), F32),
            scr((2, share_rows, lanes), BF16),
            scr((2 * chips, share_rows, lanes), BF16),
            scr((lats, width), F32),
            scr((slabs, lats, width), F32),
            scr((lats, width), F32),
            scr((walks, lats, width), F32),
            dma((3,)),
            dma((15,)),
            dma((15,)),
        ],
        compiler_params=pltpu.CompilerParams(collective_id=1, has_side_effects=True, vmem_limit_bytes=44 * MIB),
        name="main",
    )(ext, weights, p, slide, feats_v, feats_t, inv, member, wp_v, *far(w_self, w_update, cot))

    block = sds((share_rows, width), F32)
    newf, df, gs, gp, gu, geo = pl.pallas_call(
        last_kernel,
        out_shape=(
            sds((walkers, rows, width), BF16),
            sds((walkers, rows, width), F32),
            block,
            block,
            block,
            sds((lats, width), F32),
        ),
        in_specs=vmem(4),
        out_specs=hbm(6),
        scratch_shapes=[dma((6,))],
        compiler_params=pltpu.CompilerParams(vmem_limit_bytes=4 * MIB),
        name="last",
    )(newf, df, share, geo)
    return newf[None], df[None], gs, gp, gu, geo[None]


def solution(mesh):
    sizes = (mesh.shape["slab"], mesh.shape["walker"], mesh.shape["geom"])
    return jax.shard_map(
        functools.partial(body, sizes),
        mesh=mesh,
        in_specs=(
            P("geom", "walker", "slab", None),
            P(),
            P(),
            P(),
            P("geom", None, None),
            P("geom", "walker"),
            P("geom", "walker", "slab", None),
            P("geom", "walker", "slab"),
            P("geom", "walker", "slab", None),
            P("geom", "walker", "slab", None),
        ),
        out_specs=(
            P("geom", "walker", "slab", None),
            P("geom", "walker", "slab", None),
            P("walker", None),
            P("walker", None),
            P("walker", None),
            P("geom", None, None),
        ),
        check_vma=False,
    )
```

```python
import functools

import jax
import jax.numpy as jnp
from jax import lax
from jax.experimental import pallas as pl
from jax.experimental.pallas import tpu as pltpu
from jax.sharding import PartitionSpec as P

RIM = 32
F32 = jnp.float32
BF16 = jnp.bfloat16
MESH = pl.DeviceIdType.MESH
SLOTS = 2 * RIM
FGROUP = 4
BGROUP = 8
TILE = 32
MIB = 1024 * 1024
NN = ((1,), (0,))
NT = ((1,), (1,))


def dot(a, b, dims):
    return lax.dot_general(a, b, (dims, ((), ())), preferred_element_type=F32)


def at(**coords):
    return dict(device_id=coords, device_id_type=MESH)


def iota(shape, dim):
    return lax.broadcasted_iota(jnp.int32, shape, dim)


def window_matrix(slide_ref):
    wide, rows = slide_ref.shape[0], slide_ref.shape[1] // SLOTS
    gap = iota((wide, rows), 0) - iota((wide, rows), 1)

    def block(m, carry):
        off = m + jnp.where(m >= RIM, 1, 0)
        slide_ref[:, pl.ds(pl.multiple_of(m * rows, rows), rows)] = jnp.where(gap == off, 1.0, 0.0).astype(BF16)
        return carry

    lax.fori_loop(0, SLOTS, block, 0)


def slot_weights(nbr, env, count, off_ref, wt_ref):
    slots, rows = nbr.shape
    rel = nbr - iota((slots, rows), 1)
    off_ref[...] = rel - (rel > RIM).astype(jnp.int32)
    slot = iota((slots, rows), 0)
    wt_ref[...] = jnp.where(slot < count, env.astype(F32), 0.0)

    def place(step, acc):
        for u in range(8):
            k = step * 8 + u
            acc = acc + jnp.where(off_ref[pl.ds(k, 1), :] == slot, wt_ref[pl.ds(k, 1), :], 0.0)
        return acc

    return lax.fori_loop(0, slots // 8, place, jnp.zeros((slots, rows), F32))


def forward_pass(q_ref, p_ref, w_ref, slide_ref, h_ref, t_ref, agg_ref, tot_ref):
    total, rows = p_ref.shape
    width = total // w_ref.shape[0]
    groups = SLOTS // FGROUP
    agg_ref[...] = jnp.zeros(agg_ref.shape, F32)
    tot_ref[...] = jnp.zeros(tot_ref.shape, F32)

    def windows(g, at_slot):
        cols = pl.ds(pl.multiple_of(g * FGROUP * rows, FGROUP * rows), FGROUP * rows)
        h_ref[at_slot] = dot(q_ref[...], slide_ref[:, cols], NN)

    def work(g, at_slot):
        for r in range(0, total, TILE):
            here = slice(r, r + TILE)
            p = p_ref[here, :]
            ga = sa = None
            for x in range(FGROUP):
                h = h_ref[at_slot, here, x * rows : (x + 1) * rows] + p
                u = 1.0 + jnp.tanh(h)
                wu = u * w_ref[r // width, pl.ds(g * FGROUP + x, 1), :]
                wg = h * wu
                t = wu + wg * (2.0 - u)
                t_ref[g * FGROUP + x, here, :] = t
                ga = wg if x == 0 else ga + wg
                sa = t if x == 0 else sa + t
            agg_ref[here, :] += ga
            tot_ref[here, :] += sa

    windows(0, 0)

    def step(i, carry):
        windows(2 * i + 1, 1)
        work(2 * i, 0)
        windows(jnp.minimum(2 * i + 2, groups - 1), 0)
        work(2 * i + 1, 1)
        return carry

    lax.fori_loop(0, groups // 2, step, 0)


def backward_pass(part, first, count, d_ref, t_ref, slide_ref, v_ref, dqt_ref):
    rows = d_ref.shape[1]
    lanes = dqt_ref.shape[1] // 2
    width = 2 * lanes

    def work(g, at_slot):
        for w in range(2):
            for r in range(0, lanes, TILE):
                here = slice(w * width + part * lanes + r, w * width + part * lanes + r + TILE)
                there = slice(w * lanes + r, w * lanes + r + TILE)
                d = d_ref[here, :]
                for x in range(BGROUP):
                    v_ref[at_slot, there, x * rows : (x + 1) * rows] = (t_ref[g * BGROUP + x, here, :] * d).astype(BF16)

    def gather(g, at_slot):
        cols = pl.ds(pl.multiple_of(g * BGROUP * rows, BGROUP * rows), BGROUP * rows)
        dqt_ref[part] += dot(v_ref[at_slot], slide_ref[:, cols], NT)

    work(first, 0)

    def step(i, carry):
        g = first + 2 * i
        work(g + 1, 1)
        gather(g, 0)
        work(jnp.minimum(g + 2, first + count - 1), 0)
        gather(g + 1, 1)
        return carry

    lax.fori_loop(0, count // 2, step, 0)


def first_kernel(
    slabs, lat_hbm, feats_hbm, nbr_hbm, env_hbm, cnt_hbm, ws_hbm, geo_hbm, wp_hbm,
    ext_ref, w_ref, p_ref, slide_ref, feats_ref, feats_t_ref, inv_ref, member_ref, wp_ref,
    lat_ref, nbr_ref, env_ref, cnt_ref, ws_ref, geo_ref, off_ref, wt_ref, load_sem, send_sem, recv_sem,
):
    me = lax.axis_index("slab")
    nxt, prv = lax.rem(me + 1, slabs), lax.rem(me + slabs - 1, slabs)
    barrier = pltpu.get_barrier_semaphore()
    pl.semaphore_signal(barrier, inc=1, **at(slab=nxt))
    pl.semaphore_signal(barrier, inc=1, **at(slab=prv))
    loads = []
    for n, (src, dst) in enumerate((
        (feats_hbm, feats_ref), (nbr_hbm, nbr_ref), (env_hbm, env_ref), (cnt_hbm, cnt_ref), (ws_hbm, ws_ref), (geo_hbm, geo_ref), (lat_hbm, lat_ref), (wp_hbm, wp_ref),
    )):
        loads.append(pltpu.make_async_copy(src, dst, load_sem.at[n]))
        loads[-1].start()
    walkers, rows, width = feats_ref.shape
    for c in loads:
        c.wait()
    pl.semaphore_wait(barrier, 2)
    up = pltpu.make_async_remote_copy(
        feats_ref.at[:, pl.ds(rows - RIM, RIM)], ext_ref.at[:, pl.ds(0, RIM)], send_sem.at[0], recv_sem.at[0], **at(slab=nxt)
    )
    down = pltpu.make_async_remote_copy(
        feats_ref.at[:, pl.ds(0, RIM)], ext_ref.at[:, pl.ds(rows + RIM, RIM)], send_sem.at[1], recv_sem.at[1], **at(slab=prv)
    )
    up.start()
    down.start()
    window_matrix(slide_ref)
    geo = geo_ref[...]
    inv_ref[...] = 1.0 / cnt_ref[...].astype(F32)
    for w in range(walkers):
        w_ref[w] = slot_weights(nbr_ref[w], env_ref[w], cnt_ref[pl.ds(w, 1), :], off_ref, wt_ref)
        lats = geo.shape[0]
        member = (iota((lats, width), 0) == lat_ref[0, w]).astype(F32)
        member_ref[w] = member
        row = jnp.sum(jnp.where(member > 0.0, geo, 0.0), axis=0, keepdims=True)
        p = 0.5 * (dot(feats_ref[w], ws_ref[...], NN) + row)
        p_ref[w * width : (w + 1) * width, :] = p.T
        feats_t_ref[w] = feats_ref[w].T
        ext_ref[w, pl.ds(RIM, rows), :] = feats_ref[w]
        pad = ext_ref.shape[1] - rows - 2 * RIM
        ext_ref[w, pl.ds(rows + 2 * RIM, pad), :] = jnp.zeros((pad, width), BF16)
    up.wait()
    down.wait()


def main_kernel(
    slabs, walks, geoms,
    ext_ref, w_ref, p_ref, slide_ref, feats_ref, feats_t_ref, inv_ref, member_ref, wp_ref, ws_hbm, wu_hbm, cot_hbm,
    newf_ref, df_ref, share_ref, geo_out_ref,
    ws_ref, wu_ref, cot_ref, q_ref, h_ref, t_ref, agg_ref, tot_ref, d_ref, v_ref, dqt_ref, upd_ref, dp_ref, own_ref,
    rim_out, rim_in, grads_ref, half_us, pair_ref,
    core_out_us, core_in_us, core_in_p, plane_out, plane_in, ring_out_us, ring_in_us, ring_out_p, ring_in_p,
    row_us, gather_us, row_p, gather_p, gslab_out, gslab_in, gring_out, gring_in,
    load_sem, send_sem, recv_sem,
):
    slab, z, geom = lax.axis_index("slab"), lax.axis_index("walker"), lax.axis_index("geom")
    core = lax.rem(geom, 2)
    pair = geom - core
    half_geoms = geoms // 2
    chips = slabs * half_geoms
    chip = slab * half_geoms + pair // 2
    nxt, prv = lax.rem(slab + 1, slabs), lax.rem(slab + slabs - 1, slabs)
    walkers, rows, width = feats_ref.shape
    lanes = width // 2
    lats = gslab_out.shape[0]
    groups = SLOTS // BGROUP

    def chip_at(c, k):
        return at(slab=c // half_geoms, geom=lax.rem(c, half_geoms) * 2 + k)

    barrier = pltpu.get_barrier_semaphore()
    for k in range(2):
        kk = core if k == 0 else 1 - core
        for r in range(k ^ 1, chips):
            pl.semaphore_signal(barrier, inc=1, **chip_at(lax.rem(chip + r, chips), kk))
    for r in range(1, walks):
        pl.semaphore_signal(barrier, inc=1, **at(walker=lax.rem(z + r, walks)))

    def send(src, dst, n, where):
        c = pltpu.make_async_remote_copy(src, dst, send_sem.at[n], recv_sem.at[n], **where)
        c.start()
        return c

    def settle_send(ref, n):
        pltpu.make_async_remote_copy(ref, ref, send_sem.at[n], recv_sem.at[n], **at(slab=nxt)).wait_send()

    def settle_recv(ref, n):
        pltpu.make_async_remote_copy(ref, ref, send_sem.at[n], recv_sem.at[n], **at(slab=nxt)).wait_recv()

    def settle(ref, n):
        settle_send(ref, n)
        settle_recv(ref, n)

    loads = []
    for n, (src, dst) in enumerate(((wu_hbm, wu_ref), (cot_hbm, cot_ref), (ws_hbm, ws_ref))):
        loads.append(pltpu.make_async_copy(src, dst, load_sem.at[n]))
        loads[-1].start()

    for w in range(walkers):
        q = (0.5 * dot(ext_ref[w], wp_ref[...], NN)).astype(BF16)
        q_ref[w * width : (w + 1) * width, :] = q.T

    forward_pass(q_ref, p_ref, w_ref, slide_ref, h_ref, t_ref, agg_ref, tot_ref)

    for c in loads:
        c.wait()
    dgeo = jnp.zeros((lats, width), F32)
    for w in range(walkers):
        part = slice(w * width, (w + 1) * width)
        inv = inv_ref[pl.ds(w, 1), :]
        agg_t = (agg_ref[part, :] * inv).astype(BF16)
        upd = dot(agg_t.T, wu_ref[...], NN)
        sig = 0.5 + 0.5 * jnp.tanh(0.5 * upd)
        upd_ref[w] = upd * sig
        du = (cot_ref[w].astype(F32) * (sig * (1.0 + upd * (1.0 - sig)))).astype(BF16)
        dd = 0.5 * dot(wu_ref[...], du, NT) * inv
        d_ref[part, :] = dd
        dp = (dd * tot_ref[part, :]).T
        dgeo = dgeo + jnp.where(member_ref[w] > 0.0, jnp.sum(dp, axis=0, keepdims=True), 0.0)
        dp = dp.astype(BF16)
        dp_ref[w] = dp
        for n, term in enumerate((dot(feats_t_ref[w], dp, NN), dot(agg_t, du, NN))):
            grads_ref[n] = term if w == 0 else grads_ref[n] + term
    gslab_out[...] = dgeo
    dqt_ref[...] = jnp.zeros(dqt_ref.shape, F32)

    mine = pl.ds(pl.multiple_of(core * lanes, lanes), lanes)
    theirs = pl.ds(pl.multiple_of((1 - core) * lanes, lanes), lanes)
    pl.semaphore_wait(barrier, 2 * chips - 1 + walks - 1)
    core_out_us[...] = grads_ref[:, :, theirs].astype(BF16)
    cross = send(core_out_us, core_in_us, 0, at(geom=pair + 1 - core))
    gslab_in[slab] = gslab_out[...]
    for r in range(1, slabs):
        send(gslab_out, gslab_in.at[slab], 1, at(slab=lax.rem(slab + r, slabs)))

    def pair_half(part):
        term = None
        for w in range(walkers):
            dq = dqt_ref[part, w * lanes : (w + 1) * lanes, :].T
            cols = slice(part * lanes, (part + 1) * lanes)
            own_ref[w, :, cols] = dq[RIM : RIM + rows]
            dqb = dq.astype(BF16)
            rim_out[0, w, :, cols] = dqb[:RIM]
            rim_out[1, w, :, cols] = dqb[RIM + rows : 2 * RIM + rows]
            more = dot(ext_ref[w].T, dqb, NN)
            term = more if w == 0 else term + more
        pair_ref[part] = term.reshape(pair_ref.shape[1:])
        return send(pair_ref.at[part, :, 1 - core], core_in_p.at[part], 3 + part, at(geom=pair + 1 - core))

    owner = lax.rem(z + core, 2) == 0
    zz = z // 2

    def ring_half(part, cross):
        cross.wait()
        ring_out_p[part] = (pair_ref[part, :, core] + core_in_p[part]).astype(BF16)

        @pl.when(owner)
        def _():
            ring_in_p[part, z] = ring_out_p[part, zz]

        @pl.when(jnp.logical_not(owner))
        def _():
            send(ring_out_p.at[part, zz], ring_in_p.at[part, z], 11 + part, at(walker=2 * zz + core))

        for r in range(1, walks // 2):
            to = lax.rem(zz + r, walks // 2)
            send(ring_out_p.at[part, to], ring_in_p.at[part, z], 11 + part, at(walker=2 * to + core))

    backward_pass(0, 0, groups // 2, d_ref, t_ref, slide_ref, v_ref, dqt_ref)

    cross.wait()
    half_us[...] = grads_ref[:, :, mine] + core_in_us[...].astype(F32)
    for c in range(chips):
        for n in range(2):
            plane_out[c, n] = half_us[n, pl.ds(c, walks, stride=chips), :].astype(BF16)
    plane_in[chip] = plane_out[chip]
    for r in range(1, chips):
        to = lax.rem(chip + r, chips)
        send(plane_out.at[to], plane_in.at[chip], 2, chip_at(to, core))

    backward_pass(0, groups // 2, groups // 2, d_ref, t_ref, slide_ref, v_ref, dqt_ref)
    cross_p = pair_half(0)
    backward_pass(1, 0, groups // 2, d_ref, t_ref, slide_ref, v_ref, dqt_ref)
    ring_half(0, cross_p)
    backward_pass(1, groups // 2, groups // 2, d_ref, t_ref, slide_ref, v_ref, dqt_ref)
    settle(gslab_in.at[pl.ds(0, slabs - 1)], 1)
    gsum = gslab_in[0]
    for s in range(1, slabs):
        gsum = gsum + gslab_in[s]
    gring_out[...] = gsum
    gring_in[z] = gsum
    for r in range(1, walks):
        send(gring_out, gring_in.at[z], 7, at(walker=lax.rem(z + r, walks)))
    cross_p = pair_half(1)
    down = send(rim_out.at[0], rim_in.at[0], 5, at(slab=prv))
    up = send(rim_out.at[1], rim_in.at[1], 6, at(slab=nxt))
    ring_half(1, cross_p)

    for w in range(walkers):
        newf_ref[w] = (feats_ref[w].astype(F32) + upd_ref[w]).astype(BF16)
        df_ref[w] = cot_ref[w].astype(F32) + dot(dp_ref[w], ws_ref[...], NT)

    settle(plane_in.at[pl.ds(0, chips - 1)], 2)
    part = plane_in[0].astype(F32)
    for c in range(1, chips):
        part = part + plane_in[c].astype(F32)
    for v in range(walks):
        for n in range(2):
            ring_out_us[v, pl.ds(n, 1), :] = part[n, v : v + 1, :]
    ring_in_us[z] = ring_out_us[z]
    for r in range(1, walks):
        to = lax.rem(z + r, walks)
        send(ring_out_us.at[to], ring_in_us.at[z], 8, at(walker=to))

    down.wait()
    up.wait()
    for w in range(walkers):
        dq = jnp.concatenate(
            (
                own_ref[w, pl.ds(0, RIM), :] + rim_in[1, w].astype(F32),
                own_ref[w, pl.ds(RIM, rows - 2 * RIM), :],
                own_ref[w, pl.ds(rows - RIM, RIM), :] + rim_in[0, w].astype(F32),
            ),
            axis=0,
        ).astype(BF16)
        df_ref[w] = df_ref[w] + dot(dq, wp_ref[...], NT)

    slot = core * chips + chip

    for part in range(2):

        @pl.when(jnp.logical_not(owner))
        def _():
            settle_send(ring_out_p.at[part], 11 + part)

        @pl.when(owner)
        def _():
            settle_send(ring_out_p.at[part, pl.ds(0, walks // 2 - 1)], 11 + part)
            settle_recv(ring_in_p.at[part, pl.ds(0, walks - 1)], 11 + part)
            total = ring_in_p[part, 0].astype(F32)
            for v in range(1, walks):
                total = total + ring_in_p[part, v].astype(F32)
            row_p[part] = total.astype(BF16)
            gather_p[part * chips + chip] = row_p[part]
            for k in range(2):
                kk = core if k == 0 else 1 - core
                for r in range(k ^ 1, chips):
                    send(row_p.at[part], gather_p.at[part * chips + chip], 13 + part, chip_at(lax.rem(chip + r, chips), kk))

    settle(ring_in_us.at[pl.ds(0, walks - 1)], 8)
    row = ring_in_us[0]
    for v in range(1, walks):
        row = row + ring_in_us[v]
    row_us[...] = row
    gather_us[slot] = row
    for k in range(2):
        kk = core if k == 0 else 1 - core
        for r in range(k ^ 1, chips):
            send(row_us, gather_us.at[slot], 10, chip_at(lax.rem(chip + r, chips), kk))

    settle(gring_in.at[pl.ds(0, walks - 1)], 7)
    gsum = gring_in[0]
    for v in range(1, walks):
        gsum = gsum + gring_in[v]
    geo_out_ref[...] = gsum

    for part in range(2):

        @pl.when(owner)
        def _():
            settle_recv(gather_p.at[pl.ds(0, chips - 1)], 13 + part)
            settle_send(gather_p.at[pl.ds(0, 2 * chips - 1)], 13 + part)

        @pl.when(jnp.logical_not(owner))
        def _():
            settle_recv(gather_p.at[pl.ds(0, chips)], 13 + part)

        total = gather_p[part * chips].astype(F32)
        for c in range(1, chips):
            total = total + gather_p[part * chips + c].astype(F32)
        share_ref[1, :, part * lanes : (part + 1) * lanes] = total
    settle(gather_us.at[pl.ds(0, 2 * chips - 1)], 10)
    for n in range(2):
        for k in range(2):
            for c in range(chips):
                share_ref[2 * n, pl.ds(c, 1), pl.ds(k * lanes, lanes)] = gather_us[k * chips + c, pl.ds(n, 1), :]


def last_kernel(newf, df, share, geo, newf_out, df_out, gs_out, gp_out, gu_out, geo_out, sem):
    copies = [
        pltpu.make_async_copy(src, dst, sem.at[n])
        for n, (src, dst) in enumerate((
            (df, df_out), (newf, newf_out), (share.at[0], gs_out), (share.at[1], gp_out), (share.at[2], gu_out), (geo, geo_out),
        ))
    ]
    for c in copies:
        c.start()
    for c in copies:
        c.wait()


def vmem(n):
    return [pl.BlockSpec(memory_space=pltpu.VMEM)] * n


def hbm(n):
    return [pl.BlockSpec(memory_space=pltpu.HBM)] * n


def far(*arrays):
    return [pltpu.with_memory_space_constraint(x, pltpu.HBM) for x in arrays]


def body(sizes, features, w_self, w_pair, w_update, geo_embed, lattice, neighbours, counts, envelope, cotangent):
    slabs, walks, geoms = sizes
    feats, cot = features[0], cotangent[0]
    walkers, rows, width = feats.shape
    slots = neighbours.shape[3]
    lats = geo_embed.shape[1]
    wide = 2 * rows
    nbr = jnp.swapaxes(neighbours[0], 1, 2)
    env = jnp.swapaxes(envelope[0], 1, 2)
    sds = jax.ShapeDtypeStruct
    scr = pltpu.VMEM
    dma = pltpu.SemaphoreType.DMA
    ext, weights, p, slide, feats_v, feats_t, inv, member, wp_v = pl.pallas_call(
        functools.partial(first_kernel, slabs),
        out_shape=(
            sds((walkers, wide, width), BF16),
            sds((walkers, slots, rows), F32),
            sds((walkers * width, rows), F32),
            sds((wide, SLOTS * rows), BF16),
            sds((walkers, rows, width), BF16),
            sds((walkers, width, rows), BF16),
            sds((walkers, rows), F32),
            sds((walkers, lats, width), F32),
            sds((width, width), BF16),
        ),
        in_specs=hbm(8),
        out_specs=vmem(9),
        scratch_shapes=[
            pltpu.SMEM((1, walkers), jnp.int32),
            scr((walkers, slots, rows), jnp.int32),
            scr((walkers, slots, rows), BF16),
            scr((walkers, rows), jnp.int32),
            scr((width, width), BF16),
            scr((lats, width), F32),
            scr((slots, rows), jnp.int32),
            scr((slots, rows), F32),
            dma((8,)),
            dma((2,)),
            dma((2,)),
        ],
        compiler_params=pltpu.CompilerParams(collective_id=0, has_side_effects=True, vmem_limit_bytes=12 * MIB),
        name="first",
    )(*far(lattice, feats, nbr, env, counts[0], w_self, geo_embed[0], w_pair))

    chips = slabs * geoms // 2
    lanes = width // 2
    share_rows = width // walks
    newf, df, share, geo = pl.pallas_call(
        functools.partial(main_kernel, slabs, walks, geoms),
        out_shape=(
            sds((walkers, rows, width), BF16),
            sds((walkers, rows, width), F32),
            sds((3, share_rows, width), F32),
            sds((lats, width), F32),
        ),
        in_specs=vmem(9) + hbm(3),
        out_specs=vmem(4),
        scratch_shapes=[
            scr((width, width), BF16),
            scr((width, width), BF16),
            scr((walkers, rows, width), BF16),
            scr((walkers * width, wide), BF16),
            scr((2, walkers * width, FGROUP * rows), F32),
            scr((slots, walkers * width, rows), F32),
            scr((walkers * width, rows), F32),
            scr((walkers * width, rows), F32),
            scr((walkers * width, rows), F32),
            scr((2, width, BGROUP * rows), BF16),
            scr((2, width, wide), F32),
            scr((walkers, rows, width), F32),
            scr((walkers, rows, width), BF16),
            scr((walkers, rows, width), F32),
            scr((2, walkers, RIM, width), BF16),
            scr((2, walkers, RIM, width), BF16),
            scr((2, width, width), F32),
            scr((2, width, lanes), F32),
            scr((2, walks // 2, 2, share_rows, lanes), F32),
            scr((2, width, lanes), BF16),
            scr((2, width, lanes), BF16),
            scr((2, walks // 2, share_rows, lanes), F32),
            scr((chips, 2, walks, lanes), BF16),
            scr((chips, 2, walks, lanes), BF16),
            scr((walks, 2, lanes), F32),
            scr((walks, 2, lanes), F32),
            scr((2, walks // 2, share_rows, lanes), BF16),
            scr((2, walks, share_rows, lanes), BF16),
            scr((2, lanes), F32),
            scr((2 * chips, 2, lanes), F32),
            scr((2, share_rows, lanes), BF16),
            scr((2 * chips, share_rows, lanes), BF16),
            scr((lats, width), F32),
            scr((slabs, lats, width), F32),
            scr((lats, width), F32),
            scr((walks, lats, width), F32),
            dma((3,)),
            dma((15,)),
            dma((15,)),
        ],
        compiler_params=pltpu.CompilerParams(collective_id=1, has_side_effects=True, vmem_limit_bytes=44 * MIB),
        name="main",
    )(ext, weights, p, slide, feats_v, feats_t, inv, member, wp_v, *far(w_self, w_update, cot))

    block = sds((share_rows, width), F32)
    newf, df, gs, gp, gu, geo = pl.pallas_call(
        last_kernel,
        out_shape=(
            sds((walkers, rows, width), BF16),
            sds((walkers, rows, width), F32),
            block,
            block,
            block,
            sds((lats, width), F32),
        ),
        in_specs=vmem(4),
        out_specs=hbm(6),
        scratch_shapes=[dma((6,))],
        compiler_params=pltpu.CompilerParams(vmem_limit_bytes=4 * MIB),
        name="last",
    )(newf, df, share, geo)
    return newf[None], df[None], gs, gp, gu, geo[None]


def solution(mesh):
    sizes = (mesh.shape["slab"], mesh.shape["walker"], mesh.shape["geom"])
    return jax.shard_map(
        functools.partial(body, sizes),
        mesh=mesh,
        in_specs=(
            P("geom", "walker", "slab", None),
            P(),
            P(),
            P(),
            P("geom", None, None),
            P("geom", "walker"),
            P("geom", "walker", "slab", None),
            P("geom", "walker", "slab"),
            P("geom", "walker", "slab", None),
            P("geom", "walker", "slab", None),
        ),
        out_specs=(
            P("geom", "walker", "slab", None),
            P("geom", "walker", "slab", None),
            P("walker", None),
            P("walker", None),
            P("walker", None),
            P("geom", None, None),
        ),
        check_vma=False,
    )
```

```python
import functools

import jax
import jax.numpy as jnp
from jax import lax
from jax.experimental import pallas as pl
from jax.experimental.pallas import tpu as pltpu
from jax.sharding import PartitionSpec as P

RIM = 32
F32 = jnp.float32
BF16 = jnp.bfloat16
MESH = pl.DeviceIdType.MESH
SLOTS = 2 * RIM
FGROUP = 4
BGROUP = 8
TILE = 32
MIB = 1024 * 1024
NN = ((1,), (0,))
NT = ((1,), (1,))


def dot(a, b, dims):
    return lax.dot_general(a, b, (dims, ((), ())), preferred_element_type=F32)


def at(**coords):
    return dict(device_id=coords, device_id_type=MESH)


def iota(shape, dim):
    return lax.broadcasted_iota(jnp.int32, shape, dim)


def window_matrix(slide_ref):
    wide, rows = slide_ref.shape[0], slide_ref.shape[1] // SLOTS
    gap = iota((wide, rows), 0) - iota((wide, rows), 1)

    def block(m, carry):
        off = m + jnp.where(m >= RIM, 1, 0)
        slide_ref[:, pl.ds(pl.multiple_of(m * rows, rows), rows)] = jnp.where(gap == off, 1.0, 0.0).astype(BF16)
        return carry

    lax.fori_loop(0, SLOTS, block, 0)


def slot_weights(nbr, env, count, off_ref, wt_ref):
    slots, rows = nbr.shape
    rel = nbr - iota((slots, rows), 1)
    off_ref[...] = rel - (rel > RIM).astype(jnp.int32)
    slot = iota((slots, rows), 0)
    wt_ref[...] = jnp.where(slot < count, env.astype(F32), 0.0)

    def place(step, acc):
        for u in range(8):
            k = step * 8 + u
            acc = acc + jnp.where(off_ref[pl.ds(k, 1), :] == slot, wt_ref[pl.ds(k, 1), :], 0.0)
        return acc

    return lax.fori_loop(0, slots // 8, place, jnp.zeros((slots, rows), F32))


def forward_pass(q_ref, p_ref, w_ref, slide_ref, h_ref, t_ref, agg_ref, tot_ref):
    total, rows = p_ref.shape
    width = total // w_ref.shape[0]
    groups = SLOTS // FGROUP
    agg_ref[...] = jnp.zeros(agg_ref.shape, F32)
    tot_ref[...] = jnp.zeros(tot_ref.shape, F32)

    def windows(g, at_slot):
        cols = pl.ds(pl.multiple_of(g * FGROUP * rows, FGROUP * rows), FGROUP * rows)
        h_ref[at_slot] = dot(q_ref[...], slide_ref[:, cols], NN)

    def work(g, at_slot):
        for r in range(0, total, TILE):
            here = slice(r, r + TILE)
            p = p_ref[here, :]
            ga = sa = None
            for x in range(FGROUP):
                h = h_ref[at_slot, here, x * rows : (x + 1) * rows] + p
                u = 1.0 + jnp.tanh(h)
                wu = u * w_ref[r // width, pl.ds(g * FGROUP + x, 1), :]
                wg = h * wu
                t = wu + wg * (2.0 - u)
                t_ref[g * FGROUP + x, here, :] = t
                ga = wg if x == 0 else ga + wg
                sa = t if x == 0 else sa + t
            agg_ref[here, :] += ga
            tot_ref[here, :] += sa

    windows(0, 0)

    def step(i, carry):
        windows(2 * i + 1, 1)
        work(2 * i, 0)
        windows(jnp.minimum(2 * i + 2, groups - 1), 0)
        work(2 * i + 1, 1)
        return carry

    lax.fori_loop(0, groups // 2, step, 0)


def backward_pass(part, first, count, d_ref, t_ref, slide_ref, v_ref, dqt_ref):
    rows = d_ref.shape[1]
    lanes = dqt_ref.shape[1] // 2
    width = 2 * lanes

    def work(g, at_slot):
        for w in range(2):
            for r in range(0, lanes, TILE):
                here = slice(w * width + part * lanes + r, w * width + part * lanes + r + TILE)
                there = slice(w * lanes + r, w * lanes + r + TILE)
                d = d_ref[here, :]
                for x in range(BGROUP):
                    v_ref[at_slot, there, x * rows : (x + 1) * rows] = (t_ref[g * BGROUP + x, here, :] * d).astype(BF16)

    def gather(g, at_slot):
        cols = pl.ds(pl.multiple_of(g * BGROUP * rows, BGROUP * rows), BGROUP * rows)
        dqt_ref[part] += dot(v_ref[at_slot], slide_ref[:, cols], NT)

    work(first, 0)

    def step(i, carry):
        g = first + 2 * i
        work(g + 1, 1)
        gather(g, 0)
        work(jnp.minimum(g + 2, first + count - 1), 0)
        gather(g + 1, 1)
        return carry

    lax.fori_loop(0, count // 2, step, 0)


def first_kernel(
    slabs, lat_hbm, feats_hbm, nbr_hbm, env_hbm, cnt_hbm, ws_hbm, geo_hbm, wp_hbm,
    ext_ref, w_ref, p_ref, slide_ref, feats_ref, feats_t_ref, inv_ref, member_ref, wp_ref,
    lat_ref, nbr_ref, env_ref, cnt_ref, ws_ref, geo_ref, off_ref, wt_ref, load_sem, send_sem, recv_sem,
):
    me = lax.axis_index("slab")
    nxt, prv = lax.rem(me + 1, slabs), lax.rem(me + slabs - 1, slabs)
    barrier = pltpu.get_barrier_semaphore()
    pl.semaphore_signal(barrier, inc=1, **at(slab=nxt))
    pl.semaphore_signal(barrier, inc=1, **at(slab=prv))
    loads = []
    for n, (src, dst) in enumerate((
        (feats_hbm, feats_ref), (nbr_hbm, nbr_ref), (env_hbm, env_ref), (cnt_hbm, cnt_ref), (ws_hbm, ws_ref), (geo_hbm, geo_ref), (lat_hbm, lat_ref), (wp_hbm, wp_ref),
    )):
        loads.append(pltpu.make_async_copy(src, dst, load_sem.at[n]))
        loads[-1].start()
    walkers, rows, width = feats_ref.shape
    for c in loads:
        c.wait()
    pl.semaphore_wait(barrier, 2)
    up = pltpu.make_async_remote_copy(
        feats_ref.at[:, pl.ds(rows - RIM, RIM)], ext_ref.at[:, pl.ds(0, RIM)], send_sem.at[0], recv_sem.at[0], **at(slab=nxt)
    )
    down = pltpu.make_async_remote_copy(
        feats_ref.at[:, pl.ds(0, RIM)], ext_ref.at[:, pl.ds(rows + RIM, RIM)], send_sem.at[1], recv_sem.at[1], **at(slab=prv)
    )
    up.start()
    down.start()
    window_matrix(slide_ref)
    geo = geo_ref[...]
    inv_ref[...] = 1.0 / cnt_ref[...].astype(F32)
    for w in range(walkers):
        w_ref[w] = slot_weights(nbr_ref[w], env_ref[w], cnt_ref[pl.ds(w, 1), :], off_ref, wt_ref)
        lats = geo.shape[0]
        member = (iota((lats, width), 0) == lat_ref[0, w]).astype(F32)
        member_ref[w] = member
        row = jnp.sum(jnp.where(member > 0.0, geo, 0.0), axis=0, keepdims=True)
        p = 0.5 * (dot(feats_ref[w], ws_ref[...], NN) + row)
        p_ref[w * width : (w + 1) * width, :] = p.T
        feats_t_ref[w] = feats_ref[w].T
        ext_ref[w, pl.ds(RIM, rows), :] = feats_ref[w]
        pad = ext_ref.shape[1] - rows - 2 * RIM
        ext_ref[w, pl.ds(rows + 2 * RIM, pad), :] = jnp.zeros((pad, width), BF16)
    up.wait()
    down.wait()


def main_kernel(
    slabs, walks, geoms,
    ext_ref, w_ref, p_ref, slide_ref, feats_ref, feats_t_ref, inv_ref, member_ref, wp_ref, ws_hbm, wu_hbm, cot_hbm,
    newf_ref, df_ref, share_ref, geo_out_ref,
    ws_ref, wu_ref, cot_ref, q_ref, h_ref, t_ref, agg_ref, tot_ref, d_ref, v_ref, dqt_ref, upd_ref, dp_ref, own_ref,
    rim_out, rim_in, grads_ref, half_us, pair_ref,
    core_out_us, core_in_us, core_in_p, plane_out, plane_in, ring_out_us, ring_in_us, ring_out_p, ring_in_p,
    row_us, gather_us, row_p, gather_p, gslab_out, gslab_in, gring_out, gring_in,
    load_sem, send_sem, recv_sem,
):
    slab, z, geom = lax.axis_index("slab"), lax.axis_index("walker"), lax.axis_index("geom")
    core = lax.rem(geom, 2)
    pair = geom - core
    half_geoms = geoms // 2
    chips = slabs * half_geoms
    chip = slab * half_geoms + pair // 2
    nxt, prv = lax.rem(slab + 1, slabs), lax.rem(slab + slabs - 1, slabs)
    walkers, rows, width = feats_ref.shape
    lanes = width // 2
    lats = gslab_out.shape[0]
    groups = SLOTS // BGROUP

    nx, ny = slabs // 2, 2 * half_geoms
    px, py = lax.rem(slab, nx), slab // nx * half_geoms + pair // 2
    offsets = [(dx, dy) for dx in range(nx) for dy in range(ny) if dx or dy]
    offsets.sort(key=lambda o: -min(o[0], nx - o[0]) - min(o[1], ny - o[1]))
    others = []
    for dx, dy in offsets:
        tx, ty = lax.rem(px + dx, nx), lax.rem(py + dy, ny)
        others.append((ty // half_geoms * nx + tx, lax.rem(ty, half_geoms)))

    def ring_order(n):
        return sorted(range(1, n), key=lambda r: -min(r, n - r))

    barrier = pltpu.get_barrier_semaphore()
    for to_slab, to_pair in others:
        for k in range(2):
            pl.semaphore_signal(barrier, inc=1, **at(slab=to_slab, geom=to_pair * 2 + k))
    pl.semaphore_signal(barrier, inc=1, **at(geom=pair + 1 - core))
    for r in ring_order(walks):
        pl.semaphore_signal(barrier, inc=1, **at(walker=lax.rem(z + r, walks)))

    def send(src, dst, n, where):
        c = pltpu.make_async_remote_copy(src, dst, send_sem.at[n], recv_sem.at[n], **where)
        c.start()
        return c

    def spread(src, dst, n):
        for to_slab, to_pair in others:
            for k in range(2):
                send(src, dst, n, at(slab=to_slab, geom=to_pair * 2 + k))
        send(src, dst, n, at(geom=pair + 1 - core))

    def settle_send(ref, n):
        pltpu.make_async_remote_copy(ref, ref, send_sem.at[n], recv_sem.at[n], **at(slab=nxt)).wait_send()

    def settle_recv(ref, n):
        pltpu.make_async_remote_copy(ref, ref, send_sem.at[n], recv_sem.at[n], **at(slab=nxt)).wait_recv()

    def settle(ref, n):
        settle_send(ref, n)
        settle_recv(ref, n)

    loads = []
    for n, (src, dst) in enumerate(((wu_hbm, wu_ref), (cot_hbm, cot_ref), (ws_hbm, ws_ref))):
        loads.append(pltpu.make_async_copy(src, dst, load_sem.at[n]))
        loads[-1].start()

    for w in range(walkers):
        q = (0.5 * dot(ext_ref[w], wp_ref[...], NN)).astype(BF16)
        q_ref[w * width : (w + 1) * width, :] = q.T

    forward_pass(q_ref, p_ref, w_ref, slide_ref, h_ref, t_ref, agg_ref, tot_ref)

    for c in loads:
        c.wait()
    dgeo = jnp.zeros((lats, width), F32)
    for w in range(walkers):
        part = slice(w * width, (w + 1) * width)
        inv = inv_ref[pl.ds(w, 1), :]
        agg_t = (agg_ref[part, :] * inv).astype(BF16)
        upd = dot(agg_t.T, wu_ref[...], NN)
        sig = 0.5 + 0.5 * jnp.tanh(0.5 * upd)
        upd_ref[w] = upd * sig
        du = (cot_ref[w].astype(F32) * (sig * (1.0 + upd * (1.0 - sig)))).astype(BF16)
        dd = 0.5 * dot(wu_ref[...], du, NT) * inv
        d_ref[part, :] = dd
        dp = (dd * tot_ref[part, :]).T
        dgeo = dgeo + jnp.where(member_ref[w] > 0.0, jnp.sum(dp, axis=0, keepdims=True), 0.0)
        dp = dp.astype(BF16)
        dp_ref[w] = dp
        for n, term in enumerate((dot(feats_t_ref[w], dp, NN), dot(agg_t, du, NN))):
            grads_ref[n] = term if w == 0 else grads_ref[n] + term
    gslab_out[...] = dgeo
    dqt_ref[...] = jnp.zeros(dqt_ref.shape, F32)

    mine = pl.ds(pl.multiple_of(core * lanes, lanes), lanes)
    theirs = pl.ds(pl.multiple_of((1 - core) * lanes, lanes), lanes)
    pl.semaphore_wait(barrier, 2 * chips - 1 + walks - 1)
    core_out_us[...] = grads_ref[:, :, theirs].astype(BF16)
    cross = send(core_out_us, core_in_us, 0, at(geom=pair + 1 - core))
    gslab_in[slab] = gslab_out[...]
    for r in range(1, slabs):
        send(gslab_out, gslab_in.at[slab], 1, at(slab=lax.rem(slab + r, slabs)))

    def pair_half(part):
        term = None
        for w in range(walkers):
            dq = dqt_ref[part, w * lanes : (w + 1) * lanes, :].T
            cols = slice(part * lanes, (part + 1) * lanes)
            own_ref[w, :, cols] = dq[RIM : RIM + rows]
            dqb = dq.astype(BF16)
            rim_out[0, w, :, cols] = dqb[:RIM]
            rim_out[1, w, :, cols] = dqb[RIM + rows : 2 * RIM + rows]
            more = dot(ext_ref[w].T, dqb, NN)
            term = more if w == 0 else term + more
        pair_ref[part] = term.reshape(pair_ref.shape[1:])
        return send(pair_ref.at[part, :, 1 - core], core_in_p.at[part], 3 + part, at(geom=pair + 1 - core))

    owner = lax.rem(z + core, 2) == 0
    zz = z // 2

    def ring_half(part, cross):
        cross.wait()
        ring_out_p[part] = (pair_ref[part, :, core] + core_in_p[part]).astype(BF16)

        @pl.when(owner)
        def _():
            ring_in_p[part, z] = ring_out_p[part, zz]

        for r in ring_order(walks // 2):
            to = lax.rem(zz + r, walks // 2)
            send(ring_out_p.at[part, to], ring_in_p.at[part, z], 11 + part, at(walker=2 * to + core))

        @pl.when(jnp.logical_not(owner))
        def _():
            send(ring_out_p.at[part, zz], ring_in_p.at[part, z], 11 + part, at(walker=2 * zz + core))

    backward_pass(0, 0, groups // 2, d_ref, t_ref, slide_ref, v_ref, dqt_ref)

    cross.wait()
    half_us[...] = grads_ref[:, :, mine] + core_in_us[...].astype(F32)
    for c in range(chips):
        for n in range(2):
            plane_out[c, n] = half_us[n, pl.ds(c, walks, stride=chips), :].astype(BF16)
    plane_in[chip] = plane_out[chip]
    for to_slab, to_pair in others:
        send(plane_out.at[to_slab * half_geoms + to_pair], plane_in.at[chip], 2, at(slab=to_slab, geom=to_pair * 2 + core))

    backward_pass(0, groups // 2, groups // 2, d_ref, t_ref, slide_ref, v_ref, dqt_ref)
    cross_p = pair_half(0)
    backward_pass(1, 0, groups // 2, d_ref, t_ref, slide_ref, v_ref, dqt_ref)
    ring_half(0, cross_p)
    backward_pass(1, groups // 2, groups // 2, d_ref, t_ref, slide_ref, v_ref, dqt_ref)
    settle(gslab_in.at[pl.ds(0, slabs - 1)], 1)
    gsum = gslab_in[0]
    for s in range(1, slabs):
        gsum = gsum + gslab_in[s]
    gring_out[...] = gsum
    gring_in[z] = gsum
    for r in ring_order(walks):
        send(gring_out, gring_in.at[z], 7, at(walker=lax.rem(z + r, walks)))
    cross_p = pair_half(1)
    down = send(rim_out.at[0], rim_in.at[0], 5, at(slab=prv))
    up = send(rim_out.at[1], rim_in.at[1], 6, at(slab=nxt))
    ring_half(1, cross_p)

    for w in range(walkers):
        newf_ref[w] = (feats_ref[w].astype(F32) + upd_ref[w]).astype(BF16)
        df_ref[w] = cot_ref[w].astype(F32) + dot(dp_ref[w], ws_ref[...], NT)

    settle(plane_in.at[pl.ds(0, chips - 1)], 2)
    part = plane_in[0].astype(F32)
    for c in range(1, chips):
        part = part + plane_in[c].astype(F32)
    for v in range(walks):
        for n in range(2):
            ring_out_us[v, pl.ds(n, 1), :] = part[n, v : v + 1, :]
    ring_in_us[z] = ring_out_us[z]
    for r in ring_order(walks):
        to = lax.rem(z + r, walks)
        send(ring_out_us.at[to], ring_in_us.at[z], 8, at(walker=to))

    down.wait()
    up.wait()
    for w in range(walkers):
        dq = jnp.concatenate(
            (
                own_ref[w, pl.ds(0, RIM), :] + rim_in[1, w].astype(F32),
                own_ref[w, pl.ds(RIM, rows - 2 * RIM), :],
                own_ref[w, pl.ds(rows - RIM, RIM), :] + rim_in[0, w].astype(F32),
            ),
            axis=0,
        ).astype(BF16)
        df_ref[w] = df_ref[w] + dot(dq, wp_ref[...], NT)

    slot = core * chips + chip

    for part in range(2):

        @pl.when(jnp.logical_not(owner))
        def _():
            settle_send(ring_out_p.at[part], 11 + part)

        @pl.when(owner)
        def _():
            settle_send(ring_out_p.at[part, pl.ds(0, walks // 2 - 1)], 11 + part)
            settle_recv(ring_in_p.at[part, pl.ds(0, walks - 1)], 11 + part)
            total = ring_in_p[part, 0].astype(F32)
            for v in range(1, walks):
                total = total + ring_in_p[part, v].astype(F32)
            row_p[part] = total.astype(BF16)
            gather_p[part * chips + chip] = row_p[part]
            spread(row_p.at[part], gather_p.at[part * chips + chip], 13 + part)

    settle(ring_in_us.at[pl.ds(0, walks - 1)], 8)
    row = ring_in_us[0]
    for v in range(1, walks):
        row = row + ring_in_us[v]
    row_us[...] = row
    gather_us[slot] = row
    spread(row_us, gather_us.at[slot], 10)

    settle(gring_in.at[pl.ds(0, walks - 1)], 7)
    gsum = gring_in[0]
    for v in range(1, walks):
        gsum = gsum + gring_in[v]
    geo_out_ref[...] = gsum

    for part in range(2):

        @pl.when(owner)
        def _():
            settle_recv(gather_p.at[pl.ds(0, chips - 1)], 13 + part)
            settle_send(gather_p.at[pl.ds(0, 2 * chips - 1)], 13 + part)

        @pl.when(jnp.logical_not(owner))
        def _():
            settle_recv(gather_p.at[pl.ds(0, chips)], 13 + part)

        total = gather_p[part * chips].astype(F32)
        for c in range(1, chips):
            total = total + gather_p[part * chips + c].astype(F32)
        share_ref[1, :, part * lanes : (part + 1) * lanes] = total
    settle(gather_us.at[pl.ds(0, 2 * chips - 1)], 10)
    for n in range(2):
        for k in range(2):
            for c in range(chips):
                share_ref[2 * n, pl.ds(c, 1), pl.ds(k * lanes, lanes)] = gather_us[k * chips + c, pl.ds(n, 1), :]


def last_kernel(newf, df, share, geo, newf_out, df_out, gs_out, gp_out, gu_out, geo_out, sem):
    copies = [
        pltpu.make_async_copy(src, dst, sem.at[n])
        for n, (src, dst) in enumerate((
            (df, df_out), (newf, newf_out), (share.at[0], gs_out), (share.at[1], gp_out), (share.at[2], gu_out), (geo, geo_out),
        ))
    ]
    for c in copies:
        c.start()
    for c in copies:
        c.wait()


def vmem(n):
    return [pl.BlockSpec(memory_space=pltpu.VMEM)] * n


def hbm(n):
    return [pl.BlockSpec(memory_space=pltpu.HBM)] * n


def far(*arrays):
    return [pltpu.with_memory_space_constraint(x, pltpu.HBM) for x in arrays]


def body(sizes, features, w_self, w_pair, w_update, geo_embed, lattice, neighbours, counts, envelope, cotangent):
    slabs, walks, geoms = sizes
    feats, cot = features[0], cotangent[0]
    walkers, rows, width = feats.shape
    slots = neighbours.shape[3]
    lats = geo_embed.shape[1]
    wide = 2 * rows
    nbr = jnp.swapaxes(neighbours[0], 1, 2)
    env = jnp.swapaxes(envelope[0], 1, 2)
    sds = jax.ShapeDtypeStruct
    scr = pltpu.VMEM
    dma = pltpu.SemaphoreType.DMA
    ext, weights, p, slide, feats_v, feats_t, inv, member, wp_v = pl.pallas_call(
        functools.partial(first_kernel, slabs),
        out_shape=(
            sds((walkers, wide, width), BF16),
            sds((walkers, slots, rows), F32),
            sds((walkers * width, rows), F32),
            sds((wide, SLOTS * rows), BF16),
            sds((walkers, rows, width), BF16),
            sds((walkers, width, rows), BF16),
            sds((walkers, rows), F32),
            sds((walkers, lats, width), F32),
            sds((width, width), BF16),
        ),
        in_specs=hbm(8),
        out_specs=vmem(9),
        scratch_shapes=[
            pltpu.SMEM((1, walkers), jnp.int32),
            scr((walkers, slots, rows), jnp.int32),
            scr((walkers, slots, rows), BF16),
            scr((walkers, rows), jnp.int32),
            scr((width, width), BF16),
            scr((lats, width), F32),
            scr((slots, rows), jnp.int32),
            scr((slots, rows), F32),
            dma((8,)),
            dma((2,)),
            dma((2,)),
        ],
        compiler_params=pltpu.CompilerParams(collective_id=0, has_side_effects=True, vmem_limit_bytes=12 * MIB),
        name="first",
    )(*far(lattice, feats, nbr, env, counts[0], w_self, geo_embed[0], w_pair))

    chips = slabs * geoms // 2
    lanes = width // 2
    share_rows = width // walks
    newf, df, share, geo = pl.pallas_call(
        functools.partial(main_kernel, slabs, walks, geoms),
        out_shape=(
            sds((walkers, rows, width), BF16),
            sds((walkers, rows, width), F32),
            sds((3, share_rows, width), F32),
            sds((lats, width), F32),
        ),
        in_specs=vmem(9) + hbm(3),
        out_specs=vmem(4),
        scratch_shapes=[
            scr((width, width), BF16),
            scr((width, width), BF16),
            scr((walkers, rows, width), BF16),
            scr((walkers * width, wide), BF16),
            scr((2, walkers * width, FGROUP * rows), F32),
            scr((slots, walkers * width, rows), F32),
            scr((walkers * width, rows), F32),
            scr((walkers * width, rows), F32),
            scr((walkers * width, rows), F32),
            scr((2, width, BGROUP * rows), BF16),
            scr((2, width, wide), F32),
            scr((walkers, rows, width), F32),
            scr((walkers, rows, width), BF16),
            scr((walkers, rows, width), F32),
            scr((2, walkers, RIM, width), BF16),
            scr((2, walkers, RIM, width), BF16),
            scr((2, width, width), F32),
            scr((2, width, lanes), F32),
            scr((2, walks // 2, 2, share_rows, lanes), F32),
            scr((2, width, lanes), BF16),
            scr((2, width, lanes), BF16),
            scr((2, walks // 2, share_rows, lanes), F32),
            scr((chips, 2, walks, lanes), BF16),
            scr((chips, 2, walks, lanes), BF16),
            scr((walks, 2, lanes), F32),
            scr((walks, 2, lanes), F32),
            scr((2, walks // 2, share_rows, lanes), BF16),
            scr((2, walks, share_rows, lanes), BF16),
            scr((2, lanes), F32),
            scr((2 * chips, 2, lanes), F32),
            scr((2, share_rows, lanes), BF16),
            scr((2 * chips, share_rows, lanes), BF16),
            scr((lats, width), F32),
            scr((slabs, lats, width), F32),
            scr((lats, width), F32),
            scr((walks, lats, width), F32),
            dma((3,)),
            dma((15,)),
            dma((15,)),
        ],
        compiler_params=pltpu.CompilerParams(collective_id=1, has_side_effects=True, vmem_limit_bytes=44 * MIB),
        name="main",
    )(ext, weights, p, slide, feats_v, feats_t, inv, member, wp_v, *far(w_self, w_update, cot))

    block = sds((share_rows, width), F32)
    newf, df, gs, gp, gu, geo = pl.pallas_call(
        last_kernel,
        out_shape=(
            sds((walkers, rows, width), BF16),
            sds((walkers, rows, width), F32),
            block,
            block,
            block,
            sds((lats, width), F32),
        ),
        in_specs=vmem(4),
        out_specs=hbm(6),
        scratch_shapes=[dma((6,))],
        compiler_params=pltpu.CompilerParams(vmem_limit_bytes=4 * MIB),
        name="last",
    )(newf, df, share, geo)
    return newf[None], df[None], gs, gp, gu, geo[None]


def solution(mesh):
    sizes = (mesh.shape["slab"], mesh.shape["walker"], mesh.shape["geom"])
    return jax.shard_map(
        functools.partial(body, sizes),
        mesh=mesh,
        in_specs=(
            P("geom", "walker", "slab", None),
            P(),
            P(),
            P(),
            P("geom", None, None),
            P("geom", "walker"),
            P("geom", "walker", "slab", None),
            P("geom", "walker", "slab"),
            P("geom", "walker", "slab", None),
            P("geom", "walker", "slab", None),
        ),
        out_specs=(
            P("geom", "walker", "slab", None),
            P("geom", "walker", "slab", None),
            P("walker", None),
            P("walker", None),
            P("walker", None),
            P("geom", None, None),
        ),
        check_vma=False,
    )
```

```python
import functools

import jax
import jax.numpy as jnp
from jax import lax
from jax.experimental import pallas as pl
from jax.experimental.pallas import tpu as pltpu
from jax.sharding import PartitionSpec as P

RIM = 32
F32 = jnp.float32
BF16 = jnp.bfloat16
MESH = pl.DeviceIdType.MESH
SLOTS = 2 * RIM
FGROUP = 4
BGROUP = 8
TILE = 32
MIB = 1024 * 1024
NN = ((1,), (0,))
NT = ((1,), (1,))


def dot(a, b, dims):
    return lax.dot_general(a, b, (dims, ((), ())), preferred_element_type=F32)


def at(**coords):
    return dict(device_id=coords, device_id_type=MESH)


def iota(shape, dim):
    return lax.broadcasted_iota(jnp.int32, shape, dim)


def window_matrix(slide_ref):
    wide, rows = slide_ref.shape[0], slide_ref.shape[1] // SLOTS
    gap = iota((wide, rows), 0) - iota((wide, rows), 1)

    def block(m, carry):
        off = m + jnp.where(m >= RIM, 1, 0)
        slide_ref[:, pl.ds(pl.multiple_of(m * rows, rows), rows)] = jnp.where(gap == off, 1.0, 0.0).astype(BF16)
        return carry

    lax.fori_loop(0, SLOTS, block, 0)


def slot_weights(nbr, env, count, off_ref, wt_ref):
    slots, rows = nbr.shape
    rel = nbr - iota((slots, rows), 1)
    off_ref[...] = rel - (rel > RIM).astype(jnp.int32)
    slot = iota((slots, rows), 0)
    wt_ref[...] = jnp.where(slot < count, env.astype(F32), 0.0)

    def place(step, acc):
        for u in range(8):
            k = step * 8 + u
            acc = acc + jnp.where(off_ref[pl.ds(k, 1), :] == slot, wt_ref[pl.ds(k, 1), :], 0.0)
        return acc

    return lax.fori_loop(0, slots // 8, place, jnp.zeros((slots, rows), F32))


def forward_pass(q_ref, p_ref, w_ref, slide_ref, h_ref, t_ref, agg_ref, tot_ref):
    total, rows = p_ref.shape
    width = total // w_ref.shape[0]
    groups = SLOTS // FGROUP
    agg_ref[...] = jnp.zeros(agg_ref.shape, F32)
    tot_ref[...] = jnp.zeros(tot_ref.shape, F32)

    def windows(g, at_slot):
        cols = pl.ds(pl.multiple_of(g * FGROUP * rows, FGROUP * rows), FGROUP * rows)
        h_ref[at_slot] = dot(q_ref[...], slide_ref[:, cols], NN)

    def work(g, at_slot):
        for r in range(0, total, TILE):
            here = slice(r, r + TILE)
            p = p_ref[here, :]
            ga = sa = None
            for x in range(FGROUP):
                h = h_ref[at_slot, here, x * rows : (x + 1) * rows] + p
                u = 1.0 + jnp.tanh(h)
                wu = u * w_ref[r // width, pl.ds(g * FGROUP + x, 1), :]
                wg = h * wu
                t = wu + wg * (2.0 - u)
                t_ref[g * FGROUP + x, here, :] = t
                ga = wg if x == 0 else ga + wg
                sa = t if x == 0 else sa + t
            agg_ref[here, :] += ga
            tot_ref[here, :] += sa

    windows(0, 0)

    def step(i, carry):
        windows(2 * i + 1, 1)
        work(2 * i, 0)
        windows(jnp.minimum(2 * i + 2, groups - 1), 0)
        work(2 * i + 1, 1)
        return carry

    lax.fori_loop(0, groups // 2, step, 0)


def backward_pass(part, first, count, d_ref, t_ref, slide_ref, v_ref, dqt_ref):
    rows = d_ref.shape[1]
    lanes = dqt_ref.shape[1] // 2
    width = 2 * lanes

    def work(g, at_slot):
        for w in range(2):
            for r in range(0, lanes, TILE):
                here = slice(w * width + part * lanes + r, w * width + part * lanes + r + TILE)
                there = slice(w * lanes + r, w * lanes + r + TILE)
                d = d_ref[here, :]
                for x in range(BGROUP):
                    v_ref[at_slot, there, x * rows : (x + 1) * rows] = (t_ref[g * BGROUP + x, here, :] * d).astype(BF16)

    def gather(g, at_slot):
        cols = pl.ds(pl.multiple_of(g * BGROUP * rows, BGROUP * rows), BGROUP * rows)
        dqt_ref[part] += dot(v_ref[at_slot], slide_ref[:, cols], NT)

    work(first, 0)

    def step(i, carry):
        g = first + 2 * i
        work(g + 1, 1)
        gather(g, 0)
        work(jnp.minimum(g + 2, first + count - 1), 0)
        gather(g + 1, 1)
        return carry

    lax.fori_loop(0, count // 2, step, 0)


def first_kernel(
    slabs, lat_hbm, feats_hbm, nbr_hbm, env_hbm, cnt_hbm, ws_hbm, geo_hbm, wp_hbm,
    ext_ref, w_ref, p_ref, slide_ref, feats_ref, feats_t_ref, inv_ref, member_ref, wp_ref,
    lat_ref, nbr_ref, env_ref, cnt_ref, ws_ref, geo_ref, off_ref, wt_ref, load_sem, send_sem, recv_sem,
):
    me = lax.axis_index("slab")
    nxt, prv = lax.rem(me + 1, slabs), lax.rem(me + slabs - 1, slabs)
    barrier = pltpu.get_barrier_semaphore()
    pl.semaphore_signal(barrier, inc=1, **at(slab=nxt))
    pl.semaphore_signal(barrier, inc=1, **at(slab=prv))
    loads = []
    for n, (src, dst) in enumerate((
        (feats_hbm, feats_ref), (nbr_hbm, nbr_ref), (env_hbm, env_ref), (cnt_hbm, cnt_ref), (ws_hbm, ws_ref), (geo_hbm, geo_ref), (lat_hbm, lat_ref), (wp_hbm, wp_ref),
    )):
        loads.append(pltpu.make_async_copy(src, dst, load_sem.at[n]))
        loads[-1].start()
    walkers, rows, width = feats_ref.shape
    window_matrix(slide_ref)
    for c in loads:
        c.wait()
    pl.semaphore_wait(barrier, 2)
    up = pltpu.make_async_remote_copy(
        feats_ref.at[:, pl.ds(rows - RIM, RIM)], ext_ref.at[:, pl.ds(0, RIM)], send_sem.at[0], recv_sem.at[0], **at(slab=nxt)
    )
    down = pltpu.make_async_remote_copy(
        feats_ref.at[:, pl.ds(0, RIM)], ext_ref.at[:, pl.ds(rows + RIM, RIM)], send_sem.at[1], recv_sem.at[1], **at(slab=prv)
    )
    up.start()
    down.start()
    geo = geo_ref[...]
    inv_ref[...] = 1.0 / cnt_ref[...].astype(F32)
    for w in range(walkers):
        w_ref[w] = slot_weights(nbr_ref[w], env_ref[w], cnt_ref[pl.ds(w, 1), :], off_ref, wt_ref)
        lats = geo.shape[0]
        member = (iota((lats, width), 0) == lat_ref[0, w]).astype(F32)
        member_ref[w] = member
        row = jnp.sum(jnp.where(member > 0.0, geo, 0.0), axis=0, keepdims=True)
        p = 0.5 * (dot(feats_ref[w], ws_ref[...], NN) + row)
        p_ref[w * width : (w + 1) * width, :] = p.T
        feats_t_ref[w] = feats_ref[w].T
        ext_ref[w, pl.ds(RIM, rows), :] = feats_ref[w]
        pad = ext_ref.shape[1] - rows - 2 * RIM
        ext_ref[w, pl.ds(rows + 2 * RIM, pad), :] = jnp.zeros((pad, width), BF16)
    up.wait()
    down.wait()


def main_kernel(
    slabs, walks, geoms,
    ext_ref, w_ref, p_ref, slide_ref, feats_ref, feats_t_ref, inv_ref, member_ref, wp_ref, ws_hbm, wu_hbm, cot_hbm,
    newf_ref, df_ref, share_ref, geo_out_ref,
    ws_ref, wu_ref, cot_ref, q_ref, h_ref, t_ref, agg_ref, tot_ref, d_ref, v_ref, dqt_ref, upd_ref, dp_ref, own_ref,
    rim_out, rim_in, grads_ref, half_us, pair_ref,
    core_out_us, core_in_us, core_in_p, plane_out, plane_in, ring_out_us, ring_in_us, ring_out_p, ring_in_p,
    row_us, gather_us, row_p, gather_p, gslab_out, gslab_in, gring_out, gring_in,
    load_sem, send_sem, recv_sem,
):
    slab, z, geom = lax.axis_index("slab"), lax.axis_index("walker"), lax.axis_index("geom")
    core = lax.rem(geom, 2)
    pair = geom - core
    half_geoms = geoms // 2
    chips = slabs * half_geoms
    chip = slab * half_geoms + pair // 2
    nxt, prv = lax.rem(slab + 1, slabs), lax.rem(slab + slabs - 1, slabs)
    walkers, rows, width = feats_ref.shape
    lanes = width // 2
    lats = gslab_out.shape[0]
    groups = SLOTS // BGROUP

    nx, ny = slabs // 2, 2 * half_geoms
    px, py = lax.rem(slab, nx), slab // nx * half_geoms + pair // 2
    offsets = [(dx, dy) for dx in range(nx) for dy in range(ny) if dx or dy]
    offsets.sort(key=lambda o: -min(o[0], nx - o[0]) - min(o[1], ny - o[1]))
    others = []
    for dx, dy in offsets:
        tx, ty = lax.rem(px + dx, nx), lax.rem(py + dy, ny)
        others.append((ty // half_geoms * nx + tx, lax.rem(ty, half_geoms)))

    def ring_order(n):
        return sorted(range(1, n), key=lambda r: -min(r, n - r))

    barrier = pltpu.get_barrier_semaphore()
    for to_slab, to_pair in others:
        for k in range(2):
            pl.semaphore_signal(barrier, inc=1, **at(slab=to_slab, geom=to_pair * 2 + k))
    pl.semaphore_signal(barrier, inc=1, **at(geom=pair + 1 - core))
    for r in ring_order(walks):
        pl.semaphore_signal(barrier, inc=1, **at(walker=lax.rem(z + r, walks)))

    def send(src, dst, n, where):
        c = pltpu.make_async_remote_copy(src, dst, send_sem.at[n], recv_sem.at[n], **where)
        c.start()
        return c

    def spread(src, dst, n):
        for to_slab, to_pair in others:
            for k in range(2):
                send(src, dst, n, at(slab=to_slab, geom=to_pair * 2 + k))
        send(src, dst, n, at(geom=pair + 1 - core))

    def settle_send(ref, n):
        pltpu.make_async_remote_copy(ref, ref, send_sem.at[n], recv_sem.at[n], **at(slab=nxt)).wait_send()

    def settle_recv(ref, n):
        pltpu.make_async_remote_copy(ref, ref, send_sem.at[n], recv_sem.at[n], **at(slab=nxt)).wait_recv()

    def settle(ref, n):
        settle_send(ref, n)
        settle_recv(ref, n)

    loads = []
    for n, (src, dst) in enumerate(((wu_hbm, wu_ref), (cot_hbm, cot_ref), (ws_hbm, ws_ref))):
        loads.append(pltpu.make_async_copy(src, dst, load_sem.at[n]))
        loads[-1].start()

    for w in range(walkers):
        q = (0.5 * dot(ext_ref[w], wp_ref[...], NN)).astype(BF16)
        q_ref[w * width : (w + 1) * width, :] = q.T

    forward_pass(q_ref, p_ref, w_ref, slide_ref, h_ref, t_ref, agg_ref, tot_ref)

    for c in loads:
        c.wait()
    dgeo = jnp.zeros((lats, width), F32)
    for w in range(walkers):
        part = slice(w * width, (w + 1) * width)
        inv = inv_ref[pl.ds(w, 1), :]
        agg_t = (agg_ref[part, :] * inv).astype(BF16)
        upd = dot(agg_t.T, wu_ref[...], NN)
        sig = 0.5 + 0.5 * jnp.tanh(0.5 * upd)
        upd_ref[w] = upd * sig
        du = (cot_ref[w].astype(F32) * (sig * (1.0 + upd * (1.0 - sig)))).astype(BF16)
        dd = 0.5 * dot(wu_ref[...], du, NT) * inv
        d_ref[part, :] = dd
        dp = (dd * tot_ref[part, :]).T
        dgeo = dgeo + jnp.where(member_ref[w] > 0.0, jnp.sum(dp, axis=0, keepdims=True), 0.0)
        dp = dp.astype(BF16)
        dp_ref[w] = dp
        for n, term in enumerate((dot(feats_t_ref[w], dp, NN), dot(agg_t, du, NN))):
            grads_ref[n] = term if w == 0 else grads_ref[n] + term
    gslab_out[...] = dgeo
    dqt_ref[...] = jnp.zeros(dqt_ref.shape, F32)

    mine = pl.ds(pl.multiple_of(core * lanes, lanes), lanes)
    theirs = pl.ds(pl.multiple_of((1 - core) * lanes, lanes), lanes)
    pl.semaphore_wait(barrier, 2 * chips - 1 + walks - 1)
    core_out_us[...] = grads_ref[:, :, theirs].astype(BF16)
    cross = send(core_out_us, core_in_us, 0, at(geom=pair + 1 - core))
    gslab_in[slab] = gslab_out[...]
    for r in range(1, slabs):
        send(gslab_out, gslab_in.at[slab], 1, at(slab=lax.rem(slab + r, slabs)))

    def pair_half(part):
        term = None
        for w in range(walkers):
            dq = dqt_ref[part, w * lanes : (w + 1) * lanes, :].T
            cols = slice(part * lanes, (part + 1) * lanes)
            own_ref[w, :, cols] = dq[RIM : RIM + rows]
            dqb = dq.astype(BF16)
            rim_out[0, w, :, cols] = dqb[:RIM]
            rim_out[1, w, :, cols] = dqb[RIM + rows : 2 * RIM + rows]
            more = dot(ext_ref[w].T, dqb, NN)
            term = more if w == 0 else term + more
        pair_ref[part] = term.reshape(pair_ref.shape[1:])
        return send(pair_ref.at[part, :, 1 - core], core_in_p.at[part], 3 + part, at(geom=pair + 1 - core))

    owner = lax.rem(z + core, 2) == 0
    zz = z // 2

    def ring_half(part, cross):
        cross.wait()
        ring_out_p[part] = (pair_ref[part, :, core] + core_in_p[part]).astype(BF16)

        @pl.when(owner)
        def _():
            ring_in_p[part, z] = ring_out_p[part, zz]

        for r in ring_order(walks // 2):
            to = lax.rem(zz + r, walks // 2)
            send(ring_out_p.at[part, to], ring_in_p.at[part, z], 11 + part, at(walker=2 * to + core))

        @pl.when(jnp.logical_not(owner))
        def _():
            send(ring_out_p.at[part, zz], ring_in_p.at[part, z], 11 + part, at(walker=2 * zz + core))

    backward_pass(0, 0, groups // 2, d_ref, t_ref, slide_ref, v_ref, dqt_ref)

    cross.wait()
    half_us[...] = grads_ref[:, :, mine] + core_in_us[...].astype(F32)
    for c in range(chips):
        for n in range(2):
            plane_out[c, n] = half_us[n, pl.ds(c, walks, stride=chips), :].astype(BF16)
    plane_in[chip] = plane_out[chip]
    for to_slab, to_pair in others:
        send(plane_out.at[to_slab * half_geoms + to_pair], plane_in.at[chip], 2, at(slab=to_slab, geom=to_pair * 2 + core))

    backward_pass(0, groups // 2, groups // 2, d_ref, t_ref, slide_ref, v_ref, dqt_ref)
    cross_p = pair_half(0)
    backward_pass(1, 0, groups // 2, d_ref, t_ref, slide_ref, v_ref, dqt_ref)
    ring_half(0, cross_p)
    backward_pass(1, groups // 2, groups // 2, d_ref, t_ref, slide_ref, v_ref, dqt_ref)
    settle(gslab_in.at[pl.ds(0, slabs - 1)], 1)
    gsum = gslab_in[0]
    for s in range(1, slabs):
        gsum = gsum + gslab_in[s]
    gring_out[...] = gsum
    gring_in[z] = gsum
    for r in ring_order(walks):
        send(gring_out, gring_in.at[z], 7, at(walker=lax.rem(z + r, walks)))
    cross_p = pair_half(1)
    down = send(rim_out.at[0], rim_in.at[0], 5, at(slab=prv))
    up = send(rim_out.at[1], rim_in.at[1], 6, at(slab=nxt))
    ring_half(1, cross_p)

    for w in range(walkers):
        newf_ref[w] = (feats_ref[w].astype(F32) + upd_ref[w]).astype(BF16)
        df_ref[w] = cot_ref[w].astype(F32) + dot(dp_ref[w], ws_ref[...], NT)

    settle(plane_in.at[pl.ds(0, chips - 1)], 2)
    part = plane_in[0].astype(F32)
    for c in range(1, chips):
        part = part + plane_in[c].astype(F32)
    for v in range(walks):
        for n in range(2):
            ring_out_us[v, pl.ds(n, 1), :] = part[n, v : v + 1, :]
    ring_in_us[z] = ring_out_us[z]
    for r in ring_order(walks):
        to = lax.rem(z + r, walks)
        send(ring_out_us.at[to], ring_in_us.at[z], 8, at(walker=to))

    down.wait()
    up.wait()
    for w in range(walkers):
        dq = jnp.concatenate(
            (
                own_ref[w, pl.ds(0, RIM), :] + rim_in[1, w].astype(F32),
                own_ref[w, pl.ds(RIM, rows - 2 * RIM), :],
                own_ref[w, pl.ds(rows - RIM, RIM), :] + rim_in[0, w].astype(F32),
            ),
            axis=0,
        ).astype(BF16)
        df_ref[w] = df_ref[w] + dot(dq, wp_ref[...], NT)

    slot = core * chips + chip

    for part in range(2):

        @pl.when(jnp.logical_not(owner))
        def _():
            settle_send(ring_out_p.at[part], 11 + part)

        @pl.when(owner)
        def _():
            settle_send(ring_out_p.at[part, pl.ds(0, walks // 2 - 1)], 11 + part)
            settle_recv(ring_in_p.at[part, pl.ds(0, walks - 1)], 11 + part)
            total = ring_in_p[part, 0].astype(F32)
            for v in range(1, walks):
                total = total + ring_in_p[part, v].astype(F32)
            row_p[part] = total.astype(BF16)
            gather_p[part * chips + chip] = row_p[part]
            spread(row_p.at[part], gather_p.at[part * chips + chip], 13 + part)

    settle(ring_in_us.at[pl.ds(0, walks - 1)], 8)
    row = ring_in_us[0]
    for v in range(1, walks):
        row = row + ring_in_us[v]
    row_us[...] = row
    gather_us[slot] = row
    spread(row_us, gather_us.at[slot], 10)

    settle(gring_in.at[pl.ds(0, walks - 1)], 7)
    gsum = gring_in[0]
    for v in range(1, walks):
        gsum = gsum + gring_in[v]
    geo_out_ref[...] = gsum

    for part in range(2):

        @pl.when(owner)
        def _():
            settle_recv(gather_p.at[pl.ds(0, chips - 1)], 13 + part)
            settle_send(gather_p.at[pl.ds(0, 2 * chips - 1)], 13 + part)

        @pl.when(jnp.logical_not(owner))
        def _():
            settle_recv(gather_p.at[pl.ds(0, chips)], 13 + part)

        total = gather_p[part * chips].astype(F32)
        for c in range(1, chips):
            total = total + gather_p[part * chips + c].astype(F32)
        share_ref[1, :, part * lanes : (part + 1) * lanes] = total
    settle(gather_us.at[pl.ds(0, 2 * chips - 1)], 10)
    for n in range(2):
        for k in range(2):
            for c in range(chips):
                share_ref[2 * n, pl.ds(c, 1), pl.ds(k * lanes, lanes)] = gather_us[k * chips + c, pl.ds(n, 1), :]


def last_kernel(newf, df, share, geo, newf_out, df_out, gs_out, gp_out, gu_out, geo_out, sem):
    copies = [
        pltpu.make_async_copy(src, dst, sem.at[n])
        for n, (src, dst) in enumerate((
            (df, df_out), (newf, newf_out), (share.at[0], gs_out), (share.at[1], gp_out), (share.at[2], gu_out), (geo, geo_out),
        ))
    ]
    for c in copies:
        c.start()
    for c in copies:
        c.wait()


def vmem(n):
    return [pl.BlockSpec(memory_space=pltpu.VMEM)] * n


def hbm(n):
    return [pl.BlockSpec(memory_space=pltpu.HBM)] * n


def far(*arrays):
    return [pltpu.with_memory_space_constraint(x, pltpu.HBM) for x in arrays]


def body(sizes, features, w_self, w_pair, w_update, geo_embed, lattice, neighbours, counts, envelope, cotangent):
    slabs, walks, geoms = sizes
    feats, cot = features[0], cotangent[0]
    walkers, rows, width = feats.shape
    slots = neighbours.shape[3]
    lats = geo_embed.shape[1]
    wide = 2 * rows
    nbr = jnp.swapaxes(neighbours[0], 1, 2)
    env = jnp.swapaxes(envelope[0], 1, 2)
    sds = jax.ShapeDtypeStruct
    scr = pltpu.VMEM
    dma = pltpu.SemaphoreType.DMA
    ext, weights, p, slide, feats_v, feats_t, inv, member, wp_v = pl.pallas_call(
        functools.partial(first_kernel, slabs),
        out_shape=(
            sds((walkers, wide, width), BF16),
            sds((walkers, slots, rows), F32),
            sds((walkers * width, rows), F32),
            sds((wide, SLOTS * rows), BF16),
            sds((walkers, rows, width), BF16),
            sds((walkers, width, rows), BF16),
            sds((walkers, rows), F32),
            sds((walkers, lats, width), F32),
            sds((width, width), BF16),
        ),
        in_specs=hbm(8),
        out_specs=vmem(9),
        scratch_shapes=[
            pltpu.SMEM((1, walkers), jnp.int32),
            scr((walkers, slots, rows), jnp.int32),
            scr((walkers, slots, rows), BF16),
            scr((walkers, rows), jnp.int32),
            scr((width, width), BF16),
            scr((lats, width), F32),
            scr((slots, rows), jnp.int32),
            scr((slots, rows), F32),
            dma((8,)),
            dma((2,)),
            dma((2,)),
        ],
        compiler_params=pltpu.CompilerParams(collective_id=0, has_side_effects=True, vmem_limit_bytes=12 * MIB),
        name="first",
    )(*far(lattice, feats, nbr, env, counts[0], w_self, geo_embed[0], w_pair))

    chips = slabs * geoms // 2
    lanes = width // 2
    share_rows = width // walks
    newf, df, share, geo = pl.pallas_call(
        functools.partial(main_kernel, slabs, walks, geoms),
        out_shape=(
            sds((walkers, rows, width), BF16),
            sds((walkers, rows, width), F32),
            sds((3, share_rows, width), F32),
            sds((lats, width), F32),
        ),
        in_specs=vmem(9) + hbm(3),
        out_specs=vmem(4),
        scratch_shapes=[
            scr((width, width), BF16),
            scr((width, width), BF16),
            scr((walkers, rows, width), BF16),
            scr((walkers * width, wide), BF16),
            scr((2, walkers * width, FGROUP * rows), F32),
            scr((slots, walkers * width, rows), F32),
            scr((walkers * width, rows), F32),
            scr((walkers * width, rows), F32),
            scr((walkers * width, rows), F32),
            scr((2, width, BGROUP * rows), BF16),
            scr((2, width, wide), F32),
            scr((walkers, rows, width), F32),
            scr((walkers, rows, width), BF16),
            scr((walkers, rows, width), F32),
            scr((2, walkers, RIM, width), BF16),
            scr((2, walkers, RIM, width), BF16),
            scr((2, width, width), F32),
            scr((2, width, lanes), F32),
            scr((2, walks // 2, 2, share_rows, lanes), F32),
            scr((2, width, lanes), BF16),
            scr((2, width, lanes), BF16),
            scr((2, walks // 2, share_rows, lanes), F32),
            scr((chips, 2, walks, lanes), BF16),
            scr((chips, 2, walks, lanes), BF16),
            scr((walks, 2, lanes), F32),
            scr((walks, 2, lanes), F32),
            scr((2, walks // 2, share_rows, lanes), BF16),
            scr((2, walks, share_rows, lanes), BF16),
            scr((2, lanes), F32),
            scr((2 * chips, 2, lanes), F32),
            scr((2, share_rows, lanes), BF16),
            scr((2 * chips, share_rows, lanes), BF16),
            scr((lats, width), F32),
            scr((slabs, lats, width), F32),
            scr((lats, width), F32),
            scr((walks, lats, width), F32),
            dma((3,)),
            dma((15,)),
            dma((15,)),
        ],
        compiler_params=pltpu.CompilerParams(collective_id=1, has_side_effects=True, vmem_limit_bytes=44 * MIB),
        name="main",
    )(ext, weights, p, slide, feats_v, feats_t, inv, member, wp_v, *far(w_self, w_update, cot))

    block = sds((share_rows, width), F32)
    newf, df, gs, gp, gu, geo = pl.pallas_call(
        last_kernel,
        out_shape=(
            sds((walkers, rows, width), BF16),
            sds((walkers, rows, width), F32),
            block,
            block,
            block,
            sds((lats, width), F32),
        ),
        in_specs=vmem(4),
        out_specs=hbm(6),
        scratch_shapes=[dma((6,))],
        compiler_params=pltpu.CompilerParams(vmem_limit_bytes=4 * MIB),
        name="last",
    )(newf, df, share, geo)
    return newf[None], df[None], gs, gp, gu, geo[None]


def solution(mesh):
    sizes = (mesh.shape["slab"], mesh.shape["walker"], mesh.shape["geom"])
    return jax.shard_map(
        functools.partial(body, sizes),
        mesh=mesh,
        in_specs=(
            P("geom", "walker", "slab", None),
            P(),
            P(),
            P(),
            P("geom", None, None),
            P("geom", "walker"),
            P("geom", "walker", "slab", None),
            P("geom", "walker", "slab"),
            P("geom", "walker", "slab", None),
            P("geom", "walker", "slab", None),
        ),
        out_specs=(
            P("geom", "walker", "slab", None),
            P("geom", "walker", "slab", None),
            P("walker", None),
            P("walker", None),
            P("walker", None),
            P("geom", None, None),
        ),
        check_vma=False,
    )
```

```python
import functools

import jax
import jax.numpy as jnp
from jax import lax
from jax.experimental import pallas as pl
from jax.experimental.pallas import tpu as pltpu
from jax.sharding import PartitionSpec as P

RIM = 32
F32 = jnp.float32
BF16 = jnp.bfloat16
MESH = pl.DeviceIdType.MESH
SLOTS = 2 * RIM
FGROUP = 4
BGROUP = 8
TILE = 32
MIB = 1024 * 1024
NN = ((1,), (0,))
NT = ((1,), (1,))


def dot(a, b, dims):
    return lax.dot_general(a, b, (dims, ((), ())), preferred_element_type=F32)


def at(**coords):
    return dict(device_id=coords, device_id_type=MESH)


def iota(shape, dim):
    return lax.broadcasted_iota(jnp.int32, shape, dim)


def window_matrix(slide_ref):
    wide, rows = slide_ref.shape[0], slide_ref.shape[1] // SLOTS
    gap = iota((wide, rows), 0) - iota((wide, rows), 1)

    def block(m, carry):
        off = m + jnp.where(m >= RIM, 1, 0)
        slide_ref[:, pl.ds(pl.multiple_of(m * rows, rows), rows)] = jnp.where(gap == off, 1.0, 0.0).astype(BF16)
        return carry

    lax.fori_loop(0, SLOTS, block, 0)


def slot_weights(nbr, env, count, off_ref, wt_ref):
    slots, rows = nbr.shape
    rel = nbr - iota((slots, rows), 1)
    off_ref[...] = rel - (rel > RIM).astype(jnp.int32)
    slot = iota((slots, rows), 0)
    wt_ref[...] = jnp.where(slot < count, env.astype(F32), 0.0)

    def place(step, acc):
        for u in range(8):
            k = step * 8 + u
            acc = acc + jnp.where(off_ref[pl.ds(k, 1), :] == slot, wt_ref[pl.ds(k, 1), :], 0.0)
        return acc

    return lax.fori_loop(0, slots // 8, place, jnp.zeros((slots, rows), F32))


def forward_pass(q_ref, p_ref, w_ref, slide_ref, h_ref, t_ref, agg_ref, tot_ref):
    total, rows = p_ref.shape
    width = total // w_ref.shape[0]
    groups = SLOTS // FGROUP
    agg_ref[...] = jnp.zeros(agg_ref.shape, F32)
    tot_ref[...] = jnp.zeros(tot_ref.shape, F32)

    def windows(g, at_slot):
        cols = pl.ds(pl.multiple_of(g * FGROUP * rows, FGROUP * rows), FGROUP * rows)
        h_ref[at_slot] = dot(q_ref[...], slide_ref[:, cols], NN)

    def work(g, at_slot):
        for r in range(0, total, TILE):
            here = slice(r, r + TILE)
            p = p_ref[here, :]
            ga = sa = None
            for x in range(FGROUP):
                h = h_ref[at_slot, here, x * rows : (x + 1) * rows] + p
                u = 1.0 + jnp.tanh(h)
                wu = u * w_ref[r // width, pl.ds(g * FGROUP + x, 1), :]
                wg = h * wu
                t = wu + wg * (2.0 - u)
                t_ref[g * FGROUP + x, here, :] = t
                ga = wg if x == 0 else ga + wg
                sa = t if x == 0 else sa + t
            agg_ref[here, :] += ga
            tot_ref[here, :] += sa

    windows(0, 0)

    def step(i, carry):
        windows(2 * i + 1, 1)
        work(2 * i, 0)
        windows(jnp.minimum(2 * i + 2, groups - 1), 0)
        work(2 * i + 1, 1)
        return carry

    lax.fori_loop(0, groups // 2, step, 0)


def backward_pass(part, first, count, d_ref, t_ref, slide_ref, v_ref, dqt_ref):
    rows = d_ref.shape[1]
    lanes = dqt_ref.shape[1] // 2
    width = 2 * lanes

    def work(g, at_slot):
        for w in range(2):
            for r in range(0, lanes, TILE):
                here = slice(w * width + part * lanes + r, w * width + part * lanes + r + TILE)
                there = slice(w * lanes + r, w * lanes + r + TILE)
                d = d_ref[here, :]
                for x in range(BGROUP):
                    v_ref[at_slot, there, x * rows : (x + 1) * rows] = (t_ref[g * BGROUP + x, here, :] * d).astype(BF16)

    def gather(g, at_slot):
        cols = pl.ds(pl.multiple_of(g * BGROUP * rows, BGROUP * rows), BGROUP * rows)
        dqt_ref[part] += dot(v_ref[at_slot], slide_ref[:, cols], NT)

    work(first, 0)

    def step(i, carry):
        g = first + 2 * i
        work(g + 1, 1)
        gather(g, 0)
        work(jnp.minimum(g + 2, first + count - 1), 0)
        gather(g + 1, 1)
        return carry

    lax.fori_loop(0, count // 2, step, 0)


def first_kernel(
    slabs, lat_hbm, feats_hbm, nbr_hbm, env_hbm, cnt_hbm, ws_hbm, geo_hbm, wp_hbm,
    ext_ref, w_ref, p_ref, slide_ref, feats_ref, feats_t_ref, inv_ref, member_ref, wp_ref,
    lat_ref, nbr_ref, env_ref, cnt_ref, ws_ref, geo_ref, off_ref, wt_ref, load_sem, send_sem, recv_sem,
):
    me = lax.axis_index("slab")
    nxt, prv = lax.rem(me + 1, slabs), lax.rem(me + slabs - 1, slabs)
    barrier = pltpu.get_barrier_semaphore()
    pl.semaphore_signal(barrier, inc=1, **at(slab=nxt))
    pl.semaphore_signal(barrier, inc=1, **at(slab=prv))
    loads = []
    for n, (src, dst) in enumerate((
        (feats_hbm, feats_ref), (nbr_hbm, nbr_ref), (env_hbm, env_ref), (cnt_hbm, cnt_ref), (ws_hbm, ws_ref), (geo_hbm, geo_ref), (lat_hbm, lat_ref), (wp_hbm, wp_ref),
    )):
        loads.append(pltpu.make_async_copy(src, dst, load_sem.at[n]))
        loads[-1].start()
    walkers, rows, width = feats_ref.shape
    window_matrix(slide_ref)
    for c in loads:
        c.wait()
    pl.semaphore_wait(barrier, 2)
    up = pltpu.make_async_remote_copy(
        feats_ref.at[:, pl.ds(rows - RIM, RIM)], ext_ref.at[:, pl.ds(0, RIM)], send_sem.at[0], recv_sem.at[0], **at(slab=nxt)
    )
    down = pltpu.make_async_remote_copy(
        feats_ref.at[:, pl.ds(0, RIM)], ext_ref.at[:, pl.ds(rows + RIM, RIM)], send_sem.at[1], recv_sem.at[1], **at(slab=prv)
    )
    up.start()
    down.start()
    geo = geo_ref[...]
    inv_ref[...] = 1.0 / cnt_ref[...].astype(F32)
    for w in range(walkers):
        w_ref[w] = slot_weights(nbr_ref[w], env_ref[w], cnt_ref[pl.ds(w, 1), :], off_ref, wt_ref)
        lats = geo.shape[0]
        member = (iota((lats, width), 0) == lat_ref[0, w]).astype(F32)
        member_ref[w] = member
        row = jnp.sum(jnp.where(member > 0.0, geo, 0.0), axis=0, keepdims=True)
        p = 0.5 * (dot(feats_ref[w], ws_ref[...], NN) + row)
        p_ref[w * width : (w + 1) * width, :] = p.T
        feats_t_ref[w] = feats_ref[w].T
        ext_ref[w, pl.ds(RIM, rows), :] = feats_ref[w]
        pad = ext_ref.shape[1] - rows - 2 * RIM
        ext_ref[w, pl.ds(rows + 2 * RIM, pad), :] = jnp.zeros((pad, width), BF16)
    up.wait()
    down.wait()


def main_kernel(
    slabs, walks, geoms,
    ext_ref, w_ref, p_ref, slide_ref, feats_ref, feats_t_ref, inv_ref, member_ref, wp_ref, ws_hbm, wu_hbm, cot_hbm,
    newf_ref, df_ref, share_ref, geo_out_ref,
    ws_ref, wu_ref, cot_ref, q_ref, h_ref, t_ref, agg_ref, tot_ref, d_ref, v_ref, dqt_ref, upd_ref, dp_ref, own_ref,
    rim_out, rim_in, grads_ref, half_us, pair_ref,
    core_out_us, core_in_us, core_in_p, plane_out, plane_in, ring_out_us, ring_in_us, ring_out_p, ring_in_p,
    row_us, gather_us, row_p, gather_p, gslab_out, gslab_in, gring_out, gring_in,
    load_sem, send_sem, recv_sem,
):
    slab, z, geom = lax.axis_index("slab"), lax.axis_index("walker"), lax.axis_index("geom")
    core = lax.rem(geom, 2)
    pair = geom - core
    half_geoms = geoms // 2
    chips = slabs * half_geoms
    chip = slab * half_geoms + pair // 2
    nxt, prv = lax.rem(slab + 1, slabs), lax.rem(slab + slabs - 1, slabs)
    walkers, rows, width = feats_ref.shape
    lanes = width // 2
    lats = gslab_out.shape[0]
    groups = SLOTS // BGROUP

    nx, ny = slabs // 2, 2 * half_geoms
    px, py = lax.rem(slab, nx), slab // nx * half_geoms + pair // 2
    offsets = [(dx, dy) for dx in range(nx) for dy in range(ny) if dx or dy]
    offsets.sort(key=lambda o: -min(o[0], nx - o[0]) - min(o[1], ny - o[1]))
    others = []
    for dx, dy in offsets:
        tx, ty = lax.rem(px + dx, nx), lax.rem(py + dy, ny)
        others.append((ty // half_geoms * nx + tx, lax.rem(ty, half_geoms)))

    def ring_order(n):
        return sorted(range(1, n), key=lambda r: -min(r, n - r))

    barrier = pltpu.get_barrier_semaphore()
    for to_slab, to_pair in others:
        for k in range(2):
            pl.semaphore_signal(barrier, inc=1, **at(slab=to_slab, geom=to_pair * 2 + k))
    pl.semaphore_signal(barrier, inc=1, **at(geom=pair + 1 - core))
    for r in ring_order(walks):
        pl.semaphore_signal(barrier, inc=1, **at(walker=lax.rem(z + r, walks)))

    def send(src, dst, n, where):
        c = pltpu.make_async_remote_copy(src, dst, send_sem.at[n], recv_sem.at[n], **where)
        c.start()
        return c

    def spread(src, dst, n):
        for to_slab, to_pair in others:
            for k in range(2):
                send(src, dst, n, at(slab=to_slab, geom=to_pair * 2 + k))
        send(src, dst, n, at(geom=pair + 1 - core))

    def settle_send(ref, n):
        pltpu.make_async_remote_copy(ref, ref, send_sem.at[n], recv_sem.at[n], **at(slab=nxt)).wait_send()

    def settle_recv(ref, n):
        pltpu.make_async_remote_copy(ref, ref, send_sem.at[n], recv_sem.at[n], **at(slab=nxt)).wait_recv()

    def settle(ref, n):
        settle_send(ref, n)
        settle_recv(ref, n)

    loads = []
    for n, (src, dst) in enumerate(((wu_hbm, wu_ref), (cot_hbm, cot_ref), (ws_hbm, ws_ref))):
        loads.append(pltpu.make_async_copy(src, dst, load_sem.at[n]))
        loads[-1].start()

    for w in range(walkers):
        q = (0.5 * dot(ext_ref[w], wp_ref[...], NN)).astype(BF16)
        q_ref[w * width : (w + 1) * width, :] = q.T

    forward_pass(q_ref, p_ref, w_ref, slide_ref, h_ref, t_ref, agg_ref, tot_ref)

    for c in loads:
        c.wait()
    dgeo = jnp.zeros((lats, width), F32)
    for w in range(walkers):
        part = slice(w * width, (w + 1) * width)
        inv = inv_ref[pl.ds(w, 1), :]
        agg_t = (agg_ref[part, :] * inv).astype(BF16)
        upd = dot(agg_t.T, wu_ref[...], NN)
        sig = 0.5 + 0.5 * jnp.tanh(0.5 * upd)
        upd_ref[w] = upd * sig
        du = (cot_ref[w].astype(F32) * (sig * (1.0 + upd * (1.0 - sig)))).astype(BF16)
        dd = 0.5 * dot(wu_ref[...], du, NT) * inv
        d_ref[part, :] = dd
        dp = (dd * tot_ref[part, :]).T
        dgeo = dgeo + jnp.where(member_ref[w] > 0.0, jnp.sum(dp, axis=0, keepdims=True), 0.0)
        dp = dp.astype(BF16)
        dp_ref[w] = dp
        for n, term in enumerate((dot(feats_t_ref[w], dp, NN), dot(agg_t, du, NN))):
            grads_ref[n] = term if w == 0 else grads_ref[n] + term
    gslab_out[...] = dgeo
    dqt_ref[...] = jnp.zeros(dqt_ref.shape, F32)

    mine = pl.ds(pl.multiple_of(core * lanes, lanes), lanes)
    theirs = pl.ds(pl.multiple_of((1 - core) * lanes, lanes), lanes)
    pl.semaphore_wait(barrier, 2 * chips - 1 + walks - 1)
    core_out_us[...] = grads_ref[:, :, theirs].astype(BF16)
    cross = send(core_out_us, core_in_us, 0, at(geom=pair + 1 - core))
    gslab_in[slab] = gslab_out[...]
    for r in range(1, slabs):
        send(gslab_out, gslab_in.at[slab], 1, at(slab=lax.rem(slab + r, slabs)))

    def pair_half(part):
        term = None
        for w in range(walkers):
            dq = dqt_ref[part, w * lanes : (w + 1) * lanes, :].T
            cols = slice(part * lanes, (part + 1) * lanes)
            own_ref[w, :, cols] = dq[RIM : RIM + rows]
            dqb = dq.astype(BF16)
            rim_out[0, w, :, cols] = dqb[:RIM]
            rim_out[1, w, :, cols] = dqb[RIM + rows : 2 * RIM + rows]
            more = dot(ext_ref[w].T, dqb, NN)
            term = more if w == 0 else term + more
        pair_ref[part] = term.reshape(pair_ref.shape[1:])
        return send(pair_ref.at[part, :, 1 - core], core_in_p.at[part], 3 + part, at(geom=pair + 1 - core))

    owner = lax.rem(z + core, 2) == 0
    zz = z // 2

    def ring_half(part, cross):
        cross.wait()
        ring_out_p[part] = (pair_ref[part, :, core] + core_in_p[part]).astype(BF16)

        @pl.when(owner)
        def _():
            ring_in_p[part, z] = ring_out_p[part, zz]

        for r in ring_order(walks // 2):
            to = lax.rem(zz + r, walks // 2)
            send(ring_out_p.at[part, to], ring_in_p.at[part, z], 11 + part, at(walker=2 * to + core))

        @pl.when(jnp.logical_not(owner))
        def _():
            send(ring_out_p.at[part, zz], ring_in_p.at[part, z], 11 + part, at(walker=2 * zz + core))

    backward_pass(0, 0, groups // 2, d_ref, t_ref, slide_ref, v_ref, dqt_ref)

    cross.wait()
    half_us[...] = grads_ref[:, :, mine] + core_in_us[...].astype(F32)
    for c in range(chips):
        for n in range(2):
            plane_out[c, n] = half_us[n, pl.ds(c, walks, stride=chips), :].astype(BF16)
    plane_in[chip] = plane_out[chip]
    for to_slab, to_pair in others:
        send(plane_out.at[to_slab * half_geoms + to_pair], plane_in.at[chip], 2, at(slab=to_slab, geom=to_pair * 2 + core))

    backward_pass(0, groups // 2, groups // 2, d_ref, t_ref, slide_ref, v_ref, dqt_ref)
    cross_p = pair_half(0)
    backward_pass(1, 0, groups // 2, d_ref, t_ref, slide_ref, v_ref, dqt_ref)
    ring_half(0, cross_p)
    backward_pass(1, groups // 2, groups // 2, d_ref, t_ref, slide_ref, v_ref, dqt_ref)
    cross_p = pair_half(1)
    down = send(rim_out.at[0], rim_in.at[0], 5, at(slab=prv))
    up = send(rim_out.at[1], rim_in.at[1], 6, at(slab=nxt))
    ring_half(1, cross_p)

    for w in range(walkers):
        newf_ref[w] = (feats_ref[w].astype(F32) + upd_ref[w]).astype(BF16)
        df_ref[w] = cot_ref[w].astype(F32) + dot(dp_ref[w], ws_ref[...], NT)

    settle(plane_in.at[pl.ds(0, chips - 1)], 2)
    part = plane_in[0].astype(F32)
    for c in range(1, chips):
        part = part + plane_in[c].astype(F32)
    for v in range(walks):
        for n in range(2):
            ring_out_us[v, pl.ds(n, 1), :] = part[n, v : v + 1, :]
    ring_in_us[z] = ring_out_us[z]
    for r in ring_order(walks):
        to = lax.rem(z + r, walks)
        send(ring_out_us.at[to], ring_in_us.at[z], 8, at(walker=to))

    settle(gslab_in.at[pl.ds(0, slabs - 1)], 1)
    gsum = gslab_in[0]
    for s in range(1, slabs):
        gsum = gsum + gslab_in[s]
    gring_out[...] = gsum
    gring_in[z] = gsum
    for r in ring_order(walks):
        send(gring_out, gring_in.at[z], 7, at(walker=lax.rem(z + r, walks)))

    down.wait()
    up.wait()
    for w in range(walkers):
        dq = jnp.concatenate(
            (
                own_ref[w, pl.ds(0, RIM), :] + rim_in[1, w].astype(F32),
                own_ref[w, pl.ds(RIM, rows - 2 * RIM), :],
                own_ref[w, pl.ds(rows - RIM, RIM), :] + rim_in[0, w].astype(F32),
            ),
            axis=0,
        ).astype(BF16)
        df_ref[w] = df_ref[w] + dot(dq, wp_ref[...], NT)

    slot = core * chips + chip

    for part in range(2):

        @pl.when(jnp.logical_not(owner))
        def _():
            settle_send(ring_out_p.at[part], 11 + part)

        @pl.when(owner)
        def _():
            settle_send(ring_out_p.at[part, pl.ds(0, walks // 2 - 1)], 11 + part)
            settle_recv(ring_in_p.at[part, pl.ds(0, walks - 1)], 11 + part)
            total = ring_in_p[part, 0].astype(F32)
            for v in range(1, walks):
                total = total + ring_in_p[part, v].astype(F32)
            row_p[part] = total.astype(BF16)
            gather_p[part * chips + chip] = row_p[part]
            spread(row_p.at[part], gather_p.at[part * chips + chip], 13 + part)

    settle(ring_in_us.at[pl.ds(0, walks - 1)], 8)
    row = ring_in_us[0]
    for v in range(1, walks):
        row = row + ring_in_us[v]
    row_us[...] = row
    gather_us[slot] = row
    spread(row_us, gather_us.at[slot], 10)

    settle(gring_in.at[pl.ds(0, walks - 1)], 7)
    gsum = gring_in[0]
    for v in range(1, walks):
        gsum = gsum + gring_in[v]
    geo_out_ref[...] = gsum

    for part in range(2):

        @pl.when(owner)
        def _():
            settle_recv(gather_p.at[pl.ds(0, chips - 1)], 13 + part)
            settle_send(gather_p.at[pl.ds(0, 2 * chips - 1)], 13 + part)

        @pl.when(jnp.logical_not(owner))
        def _():
            settle_recv(gather_p.at[pl.ds(0, chips)], 13 + part)

        total = gather_p[part * chips].astype(F32)
        for c in range(1, chips):
            total = total + gather_p[part * chips + c].astype(F32)
        share_ref[1, :, part * lanes : (part + 1) * lanes] = total
    settle(gather_us.at[pl.ds(0, 2 * chips - 1)], 10)
    for n in range(2):
        for k in range(2):
            for c in range(chips):
                share_ref[2 * n, pl.ds(c, 1), pl.ds(k * lanes, lanes)] = gather_us[k * chips + c, pl.ds(n, 1), :]


def last_kernel(newf, df, share, geo, newf_out, df_out, gs_out, gp_out, gu_out, geo_out, sem):
    copies = [
        pltpu.make_async_copy(src, dst, sem.at[n])
        for n, (src, dst) in enumerate((
            (df, df_out), (newf, newf_out), (share.at[0], gs_out), (share.at[1], gp_out), (share.at[2], gu_out), (geo, geo_out),
        ))
    ]
    for c in copies:
        c.start()
    for c in copies:
        c.wait()


def vmem(n):
    return [pl.BlockSpec(memory_space=pltpu.VMEM)] * n


def hbm(n):
    return [pl.BlockSpec(memory_space=pltpu.HBM)] * n


def far(*arrays):
    return [pltpu.with_memory_space_constraint(x, pltpu.HBM) for x in arrays]


def body(sizes, features, w_self, w_pair, w_update, geo_embed, lattice, neighbours, counts, envelope, cotangent):
    slabs, walks, geoms = sizes
    feats, cot = features[0], cotangent[0]
    walkers, rows, width = feats.shape
    slots = neighbours.shape[3]
    lats = geo_embed.shape[1]
    wide = 2 * rows
    nbr = jnp.swapaxes(neighbours[0], 1, 2)
    env = jnp.swapaxes(envelope[0], 1, 2)
    sds = jax.ShapeDtypeStruct
    scr = pltpu.VMEM
    dma = pltpu.SemaphoreType.DMA
    ext, weights, p, slide, feats_v, feats_t, inv, member, wp_v = pl.pallas_call(
        functools.partial(first_kernel, slabs),
        out_shape=(
            sds((walkers, wide, width), BF16),
            sds((walkers, slots, rows), F32),
            sds((walkers * width, rows), F32),
            sds((wide, SLOTS * rows), BF16),
            sds((walkers, rows, width), BF16),
            sds((walkers, width, rows), BF16),
            sds((walkers, rows), F32),
            sds((walkers, lats, width), F32),
            sds((width, width), BF16),
        ),
        in_specs=hbm(8),
        out_specs=vmem(9),
        scratch_shapes=[
            pltpu.SMEM((1, walkers), jnp.int32),
            scr((walkers, slots, rows), jnp.int32),
            scr((walkers, slots, rows), BF16),
            scr((walkers, rows), jnp.int32),
            scr((width, width), BF16),
            scr((lats, width), F32),
            scr((slots, rows), jnp.int32),
            scr((slots, rows), F32),
            dma((8,)),
            dma((2,)),
            dma((2,)),
        ],
        compiler_params=pltpu.CompilerParams(collective_id=0, has_side_effects=True, vmem_limit_bytes=12 * MIB),
        name="first",
    )(*far(lattice, feats, nbr, env, counts[0], w_self, geo_embed[0], w_pair))

    chips = slabs * geoms // 2
    lanes = width // 2
    share_rows = width // walks
    newf, df, share, geo = pl.pallas_call(
        functools.partial(main_kernel, slabs, walks, geoms),
        out_shape=(
            sds((walkers, rows, width), BF16),
            sds((walkers, rows, width), F32),
            sds((3, share_rows, width), F32),
            sds((lats, width), F32),
        ),
        in_specs=vmem(9) + hbm(3),
        out_specs=vmem(4),
        scratch_shapes=[
            scr((width, width), BF16),
            scr((width, width), BF16),
            scr((walkers, rows, width), BF16),
            scr((walkers * width, wide), BF16),
            scr((2, walkers * width, FGROUP * rows), F32),
            scr((slots, walkers * width, rows), F32),
            scr((walkers * width, rows), F32),
            scr((walkers * width, rows), F32),
            scr((walkers * width, rows), F32),
            scr((2, width, BGROUP * rows), BF16),
            scr((2, width, wide), F32),
            scr((walkers, rows, width), F32),
            scr((walkers, rows, width), BF16),
            scr((walkers, rows, width), F32),
            scr((2, walkers, RIM, width), BF16),
            scr((2, walkers, RIM, width), BF16),
            scr((2, width, width), F32),
            scr((2, width, lanes), F32),
            scr((2, walks // 2, 2, share_rows, lanes), F32),
            scr((2, width, lanes), BF16),
            scr((2, width, lanes), BF16),
            scr((2, walks // 2, share_rows, lanes), F32),
            scr((chips, 2, walks, lanes), BF16),
            scr((chips, 2, walks, lanes), BF16),
            scr((walks, 2, lanes), F32),
            scr((walks, 2, lanes), F32),
            scr((2, walks // 2, share_rows, lanes), BF16),
            scr((2, walks, share_rows, lanes), BF16),
            scr((2, lanes), F32),
            scr((2 * chips, 2, lanes), F32),
            scr((2, share_rows, lanes), BF16),
            scr((2 * chips, share_rows, lanes), BF16),
            scr((lats, width), F32),
            scr((slabs, lats, width), F32),
            scr((lats, width), F32),
            scr((walks, lats, width), F32),
            dma((3,)),
            dma((15,)),
            dma((15,)),
        ],
        compiler_params=pltpu.CompilerParams(collective_id=1, has_side_effects=True, vmem_limit_bytes=44 * MIB),
        name="main",
    )(ext, weights, p, slide, feats_v, feats_t, inv, member, wp_v, *far(w_self, w_update, cot))

    block = sds((share_rows, width), F32)
    newf, df, gs, gp, gu, geo = pl.pallas_call(
        last_kernel,
        out_shape=(
            sds((walkers, rows, width), BF16),
            sds((walkers, rows, width), F32),
            block,
            block,
            block,
            sds((lats, width), F32),
        ),
        in_specs=vmem(4),
        out_specs=hbm(6),
        scratch_shapes=[dma((6,))],
        compiler_params=pltpu.CompilerParams(vmem_limit_bytes=4 * MIB),
        name="last",
    )(newf, df, share, geo)
    return newf[None], df[None], gs, gp, gu, geo[None]


def solution(mesh):
    sizes = (mesh.shape["slab"], mesh.shape["walker"], mesh.shape["geom"])
    return jax.shard_map(
        functools.partial(body, sizes),
        mesh=mesh,
        in_specs=(
            P("geom", "walker", "slab", None),
            P(),
            P(),
            P(),
            P("geom", None, None),
            P("geom", "walker"),
            P("geom", "walker", "slab", None),
            P("geom", "walker", "slab"),
            P("geom", "walker", "slab", None),
            P("geom", "walker", "slab", None),
        ),
        out_specs=(
            P("geom", "walker", "slab", None),
            P("geom", "walker", "slab", None),
            P("walker", None),
            P("walker", None),
            P("walker", None),
            P("geom", None, None),
        ),
        check_vma=False,
    )
```
